32 devices in a mesh: dp: 4 (over z), expert: 8 (over y, x, core).
Axes of the slice: x: 2, y: 2, z: 4, core: 2. Of those that a mesh axis runs over, the one named last changes fastest.
Arguments:
- block_input_vectors: bfloat16 [8, 1024, 1280], P('expert', 'dp'), may hold values from -6 to 6
- output_sensitivity: bfloat16 [8, 1024, 1280], P('expert', 'dp'), may hold values from -6 to 6
- rotary_offsets: int32 [8, 1024], P('expert'), may hold values from 0 to 895, as said below
- dispatched_specialist_ids: int32 [8, 1024, 7], P('expert', 'dp'), may hold values from 0 to 15, all different within a row; in each aligned block of 256 rows (0 to 255, 256 to 511, ..., all dimensions but the last counted through in order) at most 224 rows name the same one
- specialist_quotas: int32 [16], replicated, may hold values from 112 to 224
- storage_holder: int32 [16], replicated, may hold values from 0 to 15, each once
- mixer_projection_matrices: float32 [4, 1280, 1280], P(None, ('dp', 'expert'))
- mixer_mean_estimate: float32 [4, 1280, 1280], P(None, ('dp', 'expert'))
- mixer_variance_estimate: float32 [4, 1280, 1280], P(None, ('dp', 'expert'))
- common_projection_matrices: float32 [3, 1280, 896], P(None, ('dp', 'expert'))
- common_mean_estimate: float32 [3, 1280, 896], P(None, ('dp', 'expert'))
- common_variance_estimate: float32 [3, 1280, 896], P(None, ('dp', 'expert'))
- gating_projection_matrix: float32 [1280, 16], P(('dp', 'expert')), may hold values from -0.078125 to 0.078125
- gating_mean_estimate: float32 [1280, 16], P(('dp', 'expert'))
- gating_variance_estimate: float32 [1280, 16], P(('dp', 'expert'))
- scaling_factors: float32 [2, 1280], P(None, ('dp', 'expert'))
- scaling_mean_estimate: float32 [2, 1280], P(None, ('dp', 'expert'))
- scaling_variance_estimate: float32 [2, 1280], P(None, ('dp', 'expert'))
- dispatched_projection_matrices: float32 [16, 3, 1280, 896], P('expert', None, 'dp')
- dispatched_mean_estimate: float32 [16, 3, 1280, 896], P('expert', None, 'dp')
- dispatched_variance_estimate: float32 [16, 3, 1280, 896], P('expert', None, 'dp')
Outputs:
- block_out: bfloat16 [8, 1024, 1280], P('expert', 'dp')
- input_grad: float32 [8, 1024, 1280], P('expert', 'dp')
- grad_norm: float32 [], replicated
- attn_new: float32 [4, 1280, 1280], P(None, ('dp', 'expert'))
- attn_moment: float32 [4, 1280, 1280], P(None, ('dp', 'expert'))
- attn_square: float32 [4, 1280, 1280], P(None, ('dp', 'expert'))
- attn_copy: bfloat16 [4, 1280, 1280], P(None, ('dp', 'expert'))
- shared_new: float32 [3, 1280, 896], P(None, ('dp', 'expert'))
- shared_moment: float32 [3, 1280, 896], P(None, ('dp', 'expert'))
- shared_square: float32 [3, 1280, 896], P(None, ('dp', 'expert'))
- shared_copy: bfloat16 [3, 1280, 896], P(None, ('dp', 'expert'))
- router_new: float32 [1280, 16], P(('dp', 'expert'))
- router_moment: float32 [1280, 16], P(('dp', 'expert'))
- router_square: float32 [1280, 16], P(('dp', 'expert'))
- router_copy: bfloat16 [1280, 16], P(('dp', 'expert'))
- gain_new: float32 [2, 1280], P(None, ('dp', 'expert'))
- gain_moment: float32 [2, 1280], P(None, ('dp', 'expert'))
- gain_square: float32 [2, 1280], P(None, ('dp', 'expert'))
- expert_new: float32 [16, 3, 1280, 896], P('expert', None, 'dp')
- expert_moment: float32 [16, 3, 1280, 896], P('expert', None, 'dp')
- expert_square: float32 [16, 3, 1280, 896], P('expert', None, 'dp')
- expert_copy: bfloat16 [16, 3, 1280, 896], P('expert', None, 'dp')
The draws below stay inside these ranges and needn't reach their ends.
Inputs may be any that keep to these rules, and one draw needn't show every extreme that they name: `rotary_offsets`: each sequence holds three documents; positions count from 0 at each document's start; the middle document holds exactly 896 tokens, begins within the first 128 tokens and ends within the last 128. `dispatched_specialist_ids`: within the rows of one device no expert is named more than 224 times. `storage_holder`: A permutation; storage row r lies on index r // 2 of the expert axis.
All inputs are finite; a program needn't handle non-finite values.
Results may differ from the reference program's by a relative error of at most 0.02.
The reference program's roundings to bfloat16 on the way count: a program that leaves them out, or rounds other values in their place, can miss the bound.
Values may be sent and summed in bfloat16 or wider, within the bound.
No kernel may reach another device: no remote copies, remote signals or barrier semaphores. Data moves between devices by JAX's collectives and lax.ppermute only.
A program may use at most 384 MiB of HBM per device.

```python
import math
from functools import partial
import jax
import jax.numpy as jnp
import numpy as np
from jax import lax

D = 1280
HEADS = 10
HEAD_DIM = 128
FF = 896
TOPK = 7
TOK_DEV = 256
STEP = 10
EXPERTS = 16
LEN = 1024
SEQS = 8
SPECIALIST_QUOTA = 224
N_DP = 4
N_EXPERT = 8


CLIP_VALUE = 1.0


def gradient_size(factor):
    count = 4 * D * D + 3 * D * FF + D * EXPERTS + 2 * D + EXPERTS * 3 * D * FF
    return factor * CLIP_VALUE / math.sqrt(count)


def first_moment(key, array_shape, factor):
    return 0.11 * gradient_size(factor) * jax.random.normal(key, array_shape, jnp.float32)


def second_moment(key, array_shape, factor):
    size = gradient_size(factor)
    spread = jnp.exp(jax.random.uniform(key, array_shape, jnp.float32, math.log(0.5), math.log(8.0)))
    return 0.001 * size * size * spread


def draw_rotary_offsets(key, part):
    key = jax.random.fold_in(key, 5)
    half = max(TOK_DEV // 2, 2)
    first = jax.random.randint(key, (SEQS, 1), 1, half)
    last = first + LEN - half
    index = jnp.arange(LEN, dtype=jnp.int32)[None, :]
    starts = jnp.where(index < first, 0, jnp.where(index < last, first, last))
    return (index - starts).astype(jnp.int32)


def draw_specialist_quotas(key, part):
    key = jax.random.fold_in(key, 7)
    value_key, pick_key = jax.random.split(key)
    values = jax.random.randint(value_key, (EXPERTS,), max(SPECIALIST_QUOTA // 2, 1), SPECIALIST_QUOTA + 1)
    chosen = jax.random.randint(pick_key, (), 0, EXPERTS)
    return jnp.where(jnp.arange(EXPERTS) == chosen, SPECIALIST_QUOTA, values).astype(jnp.int32)


def draw_mixer_projection_matrices(key, part):
    key = jax.random.fold_in(key, 11)
    base = jax.random.normal(key, (4, D, D), jnp.float32)
    boost = jnp.array([1.0, 1.0, 1.0, LEN ** 0.25], jnp.float32)[:, None, None]
    return base * boost / math.sqrt(D)


def draw_mixer_mean_estimate(key, part):
    key = jax.random.fold_in(key, 12)
    return first_moment(key, (4, D, D), 1.0)


def draw_mixer_variance_estimate(key, part):
    key = jax.random.fold_in(key, 13)
    return second_moment(key, (4, D, D), 1.0)


def draw_common_projection_matrices(key, part):
    key = jax.random.fold_in(key, 14)
    base = jax.random.normal(key, (3, D, FF), jnp.float32)
    factor = jnp.array([D ** (-0.5), D ** (-0.5), FF ** (-0.5)], jnp.float32)[:, None, None]
    return base * factor


def draw_common_mean_estimate(key, part):
    key = jax.random.fold_in(key, 15)
    return first_moment(key, (3, D, FF), 1.0)


def draw_common_variance_estimate(key, part):
    key = jax.random.fold_in(key, 16)
    return second_moment(key, (3, D, FF), 1.0)


def draw_gating_mean_estimate(key, part):
    key = jax.random.fold_in(key, 17)
    return first_moment(key, (D, EXPERTS), 1.0)


def draw_gating_variance_estimate(key, part):
    key = jax.random.fold_in(key, 18)
    return second_moment(key, (D, EXPERTS), 1.0)


def draw_scaling_factors(key, part):
    key = jax.random.fold_in(key, 19)
    groups = N_DP * N_EXPERT
    index = jnp.arange(D) // (D // groups)
    outer = (index // N_EXPERT).astype(jnp.float32) / max(N_DP - 1, 1)
    inner = (index % N_EXPERT).astype(jnp.float32) / max(N_EXPERT - 1, 1)
    rise = 3.0
    ramp = rise ** (0.5 * outer) * rise ** (0.5 * inner)
    noise = jax.random.uniform(key, (2, D), jnp.float32, 0.9, 1.1)
    return 0.6 * ramp[None, :] * noise


def draw_scaling_mean_estimate(key, part):
    key = jax.random.fold_in(key, 20)
    return first_moment(key, (2, D), 4.0)


def draw_scaling_variance_estimate(key, part):
    key = jax.random.fold_in(key, 21)
    return second_moment(key, (2, D), 4.0)


def draw_dispatched_projection_matrices(key, part):
    key = jax.random.fold_in(key, 22)
    base = jax.random.normal(key, (EXPERTS, 3, D, FF), jnp.float32)
    factor = jnp.array([D ** (-0.5), D ** (-0.5), EXPERTS / math.sqrt(TOPK) / math.sqrt(FF)], jnp.float32)[None, :, None, None]
    return base * factor


def draw_dispatched_mean_estimate(key, part):
    key = jax.random.fold_in(key, 23)
    return first_moment(key, (EXPERTS, 3, D, FF), 1.0)


def draw_dispatched_variance_estimate(key, part):
    key = jax.random.fold_in(key, 24)
    return second_moment(key, (EXPERTS, 3, D, FF), 1.0)


def steps_of(key, shape, pieces, least, largest):
    level = 1.0
    for axis_at, parts in pieces:
        heights = jax.random.uniform(jax.random.fold_in(jax.random.fold_in(key, 6), axis_at), (parts,), jnp.float32, least / len(pieces), largest / len(pieces))
        level = level * jnp.repeat(jnp.exp(heights), shape[axis_at] // parts).reshape((-1,) + (1,) * (len(shape) - 1 - axis_at))
    return level


def deal_out(own_key, own, number, rows, count, top, bound, skew):
    sequence = jax.random.permutation(own_key, count)
    crowded, usual = portions_of(count, rows * top, bound, skew, True), portions_of(count, rows * top, bound, skew, False)
    places = jnp.arange(count)

    def named(tallies, rotation):
        used = int((tallies > 0).sum())
        fixed = max(1, used // 4)
        passed = fixed + (places - fixed + rotation * (used - fixed)) % max(1, count - fixed)
        return jnp.zeros((count,), jnp.int32).at[sequence[jnp.where(places < fixed, places, passed)]].set(jnp.asarray(tallies, jnp.int32))

    tallies = jnp.where(number % 4 == 0, named(crowded, number // 4), named(usual, number - number // 4 - 1))
    mixed = jax.random.permutation(jax.random.fold_in(own, 3), count)
    donor, taker = mixed[0:count // 2 * 2:2], mixed[1:count // 2 * 2:2]
    margin = jnp.minimum(tallies[donor] - 1, bound - tallies[taker]) // 2
    margin = jnp.where((donor == sequence[0]) | (taker == sequence[0]) | (tallies[taker] == 0), 0, jnp.maximum(margin, 0))
    passed = jax.random.randint(jax.random.fold_in(own, 4), (count // 2,), 0, 1 << 20) % (margin + 1)
    tallies = tallies.at[donor].add(-passed).at[taker].add(passed)
    items = jnp.searchsorted(jnp.cumsum(tallies), jnp.arange(rows * top), side="right").astype(jnp.int32)
    table = items.reshape(top, rows).T
    table = table[jax.random.permutation(jax.random.fold_in(own, 1), rows)]
    rotation = jax.random.randint(jax.random.fold_in(own, 2), (rows, 1), 0, top)
    return jnp.take_along_axis(table, (jnp.arange(top)[None, :] + rotation) % top, axis=1)


def portions_of(count, total, reach, slope, full):
    weights = [(1 << 20) // math.isqrt(grade ** slope) + 1 for grade in range(1, count + 1)]
    largest = reach if full else min(reach, max(-(-total // count), total * weights[0] // sum(weights)))
    least = 1 if total - largest >= count - 1 else 0
    counts, surplus = [largest] + [least] * (count - 1), total - largest - least * (count - 1)
    while surplus > 0:
        free = [i for i in range(1, count) if counts[i] < largest] or [i for i in range(1, count) if counts[i] < reach]
        pool, remaining = sum([weights[i] for i in free]), surplus
        for i in free:
            addition = min(reach - counts[i], max(1, remaining * weights[i] // pool), surplus)
            counts[i] = counts[i] + addition
            surplus = surplus - addition
    return np.array(counts)


def gaussian(rng, shape, width, limit, cuts=(), held_as=jnp.bfloat16):
    values = width * jax.random.normal(rng, shape, jnp.float32)
    if cuts:
        values = values * steps_of(rng, shape, cuts, -0.22, 0.18)
    return jnp.clip(values, -limit, limit).astype(held_as)


def setup_inputs(seed: int = 0) -> dict:
    splits = jax.random.split(jax.random.key(seed), 22)
    block_input_vectors = gaussian(splits[0], (SEQS, LEN, D), 1.0, 6.0, ((0, 8), (1, 4)))
    output_sensitivity = gaussian(splits[1], (SEQS, LEN, D), 1.0, 6.0, ((0, 8), (1, 4)))
    rotary_offsets = draw_rotary_offsets(jax.random.fold_in(splits[21], 71), 0)
    dispatched_specialist_ids_keys = jax.random.split(jax.random.fold_in(splits[3], 1), SEQS * LEN // TOK_DEV)
    dispatched_specialist_ids_turns = jax.random.permutation(jax.random.fold_in(splits[3], 3), SEQS * LEN // TOK_DEV)
    dispatched_specialist_ids = jax.vmap(lambda own, number: deal_out(jax.random.fold_in(splits[3], 2), own, number, TOK_DEV, EXPERTS, TOPK, SPECIALIST_QUOTA, 2))(dispatched_specialist_ids_keys, dispatched_specialist_ids_turns).reshape((SEQS, LEN, TOPK))
    specialist_quotas = draw_specialist_quotas(jax.random.fold_in(splits[21], 71), 0)
    storage_holder = jax.random.permutation(splits[5], EXPERTS).astype(jnp.int32)
    mixer_projection_matrices = draw_mixer_projection_matrices(jax.random.fold_in(splits[21], 71), 0)
    mixer_mean_estimate = draw_mixer_mean_estimate(jax.random.fold_in(splits[21], 71), 0)
    mixer_variance_estimate = draw_mixer_variance_estimate(jax.random.fold_in(splits[21], 71), 0)
    common_projection_matrices = draw_common_projection_matrices(jax.random.fold_in(splits[21], 71), 0)
    common_mean_estimate = draw_common_mean_estimate(jax.random.fold_in(splits[21], 71), 0)
    common_variance_estimate = draw_common_variance_estimate(jax.random.fold_in(splits[21], 71), 0)
    gating_projection_matrix = gaussian(splits[12], (D, EXPERTS), (4 * D) ** -0.5, 0.078125, ((0, 32),), jnp.float32)
    gating_mean_estimate = draw_gating_mean_estimate(jax.random.fold_in(splits[21], 71), 0)
    gating_variance_estimate = draw_gating_variance_estimate(jax.random.fold_in(splits[21], 71), 0)
    scaling_factors = draw_scaling_factors(jax.random.fold_in(splits[21], 71), 0)
    scaling_mean_estimate = draw_scaling_mean_estimate(jax.random.fold_in(splits[21], 71), 0)
    scaling_variance_estimate = draw_scaling_variance_estimate(jax.random.fold_in(splits[21], 71), 0)
    dispatched_projection_matrices = draw_dispatched_projection_matrices(jax.random.fold_in(splits[21], 71), 0)
    dispatched_mean_estimate = draw_dispatched_mean_estimate(jax.random.fold_in(splits[21], 71), 0)
    dispatched_variance_estimate = draw_dispatched_variance_estimate(jax.random.fold_in(splits[21], 71), 0)
    return dict(block_input_vectors=block_input_vectors, output_sensitivity=output_sensitivity, rotary_offsets=rotary_offsets, dispatched_specialist_ids=dispatched_specialist_ids, specialist_quotas=specialist_quotas, storage_holder=storage_holder, mixer_projection_matrices=mixer_projection_matrices, mixer_mean_estimate=mixer_mean_estimate, mixer_variance_estimate=mixer_variance_estimate, common_projection_matrices=common_projection_matrices, common_mean_estimate=common_mean_estimate, common_variance_estimate=common_variance_estimate, gating_projection_matrix=gating_projection_matrix, gating_mean_estimate=gating_mean_estimate, gating_variance_estimate=gating_variance_estimate, scaling_factors=scaling_factors, scaling_mean_estimate=scaling_mean_estimate, scaling_variance_estimate=scaling_variance_estimate, dispatched_projection_matrices=dispatched_projection_matrices, dispatched_mean_estimate=dispatched_mean_estimate, dispatched_variance_estimate=dispatched_variance_estimate)


@jax.custom_vjp
def low(v):
    return lax.optimization_barrier(v.astype(jnp.bfloat16)).astype(jnp.float32)

@jax.custom_vjp
def low_back(v):
    return v

def low_keep(v):
    return (low(v), None)

def low_pass(kept, grad):
    return (grad,)

def back_keep(v):
    return (v, None)

def back_low(kept, grad):
    return (low(grad),)
low.defvjp(low_keep, low_pass)
low_back.defvjp(back_keep, back_low)
NORM_EPS = 1e-06
THETA = 10000.0
CLIP_VALUE = 1.0
BETA_ONE = 0.9
BETA_TWO = 0.999
ADAM_EPS = 1e-08
DECAY = 0.1
RATE_MATRIX = 0.02
RATE_EXPERT = 0.1
RATE_GAIN = 0.3
MASKED = -1e+30

def product(left, right):
    return jnp.dot(left, right, precision=lax.Precision.HIGHEST, preferred_element_type=jnp.float32)

def rms_norm(values, gain):
    inverse = lax.rsqrt(lax.optimization_barrier(jnp.mean(values * values, axis=-1, keepdims=True)) + NORM_EPS)
    return values * inverse * gain

def rotary(values, places):
    half = HEAD_DIM // 2
    freq = THETA ** (-2.0 * jnp.arange(half, dtype=jnp.float32) / HEAD_DIM)
    angle = places.astype(jnp.float32)[..., None] * freq
    cosine = jnp.concatenate([jnp.cos(angle), jnp.cos(angle)], -1)[..., None, :]
    sine = jnp.concatenate([jnp.sin(angle), jnp.sin(angle)], -1)[..., None, :]
    turned = jnp.concatenate([-values[..., half:], values[..., :half]], -1)
    return values * cosine + turned * sine

def attend_item(item):
    queries, keys, values, places = item
    index = jnp.arange(LEN, dtype=jnp.int32)
    starts = index - places
    allowed = (starts[:, None] == starts[None, :]) & (index[None, :] <= index[:, None])
    raw = jnp.einsum('qhd,khd->hqk', queries, keys, precision=lax.Precision.HIGHEST) * HEAD_DIM ** (-0.5)
    scores = jnp.where(allowed[None], low_back(raw), MASKED)
    weights = low(jax.nn.softmax(scores, axis=-1))
    return jnp.einsum('hqk,khd->qhd', weights, values, precision=lax.Precision.HIGHEST)

def assignment_place_number(linear_specialist_position, specialist_quotas, storage_holder, block_ordinal):
    specialist_total = specialist_quotas.shape[0]
    specialist_indicator = (linear_specialist_position[:, None] == jnp.arange(specialist_total, dtype=jnp.int32)[None, :]).astype(jnp.int32)
    earlier = jnp.cumsum(specialist_indicator, axis=0) - specialist_indicator
    rank = lax.optimization_barrier(jnp.sum(earlier * specialist_indicator, axis=1))
    quota_ceiling = lax.optimization_barrier(jnp.sum(specialist_indicator * specialist_quotas[None, :], axis=1))
    storage = lax.optimization_barrier(jnp.sum(specialist_indicator * storage_holder[None, :], axis=1))
    retained_indicator = rank < quota_ceiling
    place_number = jnp.where(retained_indicator, storage * block_ordinal + rank, specialist_total * block_ordinal)
    return (place_number.astype(jnp.int32), retained_indicator, specialist_indicator)

def slot_owners(place_number, specialist_total, block_ordinal):
    count = place_number.shape[0]
    table = jnp.full((specialist_total * block_ordinal + 1,), count, jnp.int32)
    table = table.at[place_number].set(jnp.arange(count, dtype=jnp.int32))
    return table[:specialist_total * block_ordinal]

def adam(master, first, second, grad, scale, rate):
    clipped = grad * scale
    first_new = BETA_ONE * first + (1.0 - BETA_ONE) * clipped
    second_new = BETA_TWO * second + (1.0 - BETA_TWO) * clipped * clipped
    first_hat = first_new / (1.0 - BETA_ONE ** STEP)
    second_hat = second_new / (1.0 - BETA_TWO ** STEP)
    master_new = master - rate * (first_hat / (jnp.sqrt(second_hat) + ADAM_EPS) + DECAY * master)
    return (master_new, first_new, second_new)

def reference(block_input_vectors, output_sensitivity, rotary_offsets, dispatched_specialist_ids, specialist_quotas, storage_holder, mixer_projection_matrices, mixer_mean_estimate, mixer_variance_estimate, common_projection_matrices, common_mean_estimate, common_variance_estimate, gating_projection_matrix, gating_mean_estimate, gating_variance_estimate, scaling_factors, scaling_mean_estimate, scaling_variance_estimate, dispatched_projection_matrices, dispatched_mean_estimate, dispatched_variance_estimate):
    total_rows = SEQS * LEN
    blocks = total_rows // TOK_DEV
    pairs = TOK_DEV * TOPK
    linear_specialist_position = dispatched_specialist_ids.reshape(blocks, pairs).astype(jnp.int32)
    place_number, retained_indicator, specialist_indicator = jax.vmap(partial(assignment_place_number, specialist_quotas=specialist_quotas, storage_holder=storage_holder, block_ordinal=SPECIALIST_QUOTA))(linear_specialist_position)
    owners_of_slots = jax.vmap(partial(slot_owners, specialist_total=EXPERTS, block_ordinal=SPECIALIST_QUOTA))(place_number)
    base = (jnp.arange(blocks, dtype=jnp.int32) * TOK_DEV)[:, None]
    token_of_slot = jnp.where(owners_of_slots < pairs, base + owners_of_slots // TOPK, total_rows).astype(jnp.int32)
    token_of_slot = token_of_slot.reshape(blocks, EXPERTS, SPECIALIST_QUOTA).transpose(1, 0, 2).reshape(EXPERTS, blocks * SPECIALIST_QUOTA)
    logical = jnp.zeros((EXPERTS,), jnp.int32).at[storage_holder].set(jnp.arange(EXPERTS, dtype=jnp.int32))

    def forward(inputs, attn, shared, router, gains, specialist_total):
        attn_low = low(attn)
        shared_low = low(shared)
        router_low = low(router)
        gains_low = low(gains)
        expert_low = low(specialist_total)
        flat = inputs.reshape(total_rows, D)
        normed = low(rms_norm(flat, gains_low[0]))
        query = low_back(product(normed, attn_low[0])).reshape(SEQS, LEN, HEADS, HEAD_DIM)
        key_part = low_back(product(normed, attn_low[1])).reshape(SEQS, LEN, HEADS, HEAD_DIM)
        value_part = low(low_back(product(normed, attn_low[2]))).reshape(SEQS, LEN, HEADS, HEAD_DIM)
        query = low(rotary(query, rotary_offsets))
        key_part = low(rotary(key_part, rotary_offsets))
        mixed = lax.map(jax.checkpoint(attend_item), (query, key_part, value_part, rotary_offsets))
        mixed = low(low_back(mixed.reshape(total_rows, D)))
        middle = flat + low_back(product(mixed, attn_low[3]))
        second = low(rms_norm(middle, gains_low[1]))
        probs = jax.nn.softmax(low_back(product(second, router_low)), axis=-1)
        gate_shared = low_back(product(second, shared_low[0]))
        up_shared = low_back(product(second, shared_low[1]))
        hidden_shared = low(jax.nn.silu(gate_shared) * up_shared)
        shared_out = product(hidden_shared, shared_low[2].T)
        padded = jnp.concatenate([second, jnp.zeros((1, D), jnp.float32)], 0)
        prob_pad = jnp.concatenate([probs, jnp.zeros((1, EXPERTS), jnp.float32)], 0)

        def expert_step(running, item):
            weights, chosen, which = item
            entry = low_back(padded[chosen])
            gate_part = low_back(product(entry, weights[0]))
            up_part = low_back(product(entry, weights[1]))
            hidden = low(jax.nn.silu(gate_part) * up_part)
            result = low(low_back(product(hidden, weights[2].T)))
            gate = prob_pad[chosen, which]
            return (running.at[chosen].add(gate[:, None] * result), None)
        routed = lax.scan(jax.checkpoint(expert_step), jnp.zeros((total_rows + 1, D), jnp.float32), (expert_low, token_of_slot, logical))[0]
        return (middle + shared_out + routed[:total_rows]).reshape(SEQS, LEN, D)
    inputs = block_input_vectors.astype(jnp.float32)
    output, pullback = jax.vjp(forward, inputs, mixer_projection_matrices, common_projection_matrices, gating_projection_matrix, scaling_factors, dispatched_projection_matrices)
    grads = pullback(output_sensitivity.astype(jnp.float32))
    input_grad, attn_grad, shared_grad, router_grad, gain_grad, expert_grad = grads
    squares = jnp.sum(attn_grad * attn_grad) + jnp.sum(shared_grad * shared_grad) + jnp.sum(router_grad * router_grad) + jnp.sum(gain_grad * gain_grad) + jnp.sum(expert_grad * expert_grad)
    grad_norm = jnp.sqrt(squares)
    scale = jnp.minimum(1.0, CLIP_VALUE / (grad_norm + 1e-06))
    attn_new, attn_moment, attn_square = adam(mixer_projection_matrices, mixer_mean_estimate, mixer_variance_estimate, attn_grad, scale, RATE_MATRIX)
    shared_new, shared_moment, shared_square = adam(common_projection_matrices, common_mean_estimate, common_variance_estimate, shared_grad, scale, RATE_MATRIX)
    router_new, router_moment, router_square = adam(gating_projection_matrix, gating_mean_estimate, gating_variance_estimate, router_grad, scale, RATE_MATRIX)
    gain_new, gain_moment, gain_square = adam(scaling_factors, scaling_mean_estimate, scaling_variance_estimate, gain_grad, scale, RATE_GAIN)
    expert_new, expert_moment, expert_square = adam(dispatched_projection_matrices, dispatched_mean_estimate, dispatched_variance_estimate, expert_grad, scale, RATE_EXPERT)
    return (output.astype(jnp.bfloat16), input_grad, grad_norm, attn_new, attn_moment, attn_square, attn_new.astype(jnp.bfloat16), shared_new, shared_moment, shared_square, shared_new.astype(jnp.bfloat16), router_new, router_moment, router_square, router_new.astype(jnp.bfloat16), gain_new, gain_moment, gain_square, expert_new, expert_moment, expert_square, expert_new.astype(jnp.bfloat16))
```

```python
import jax
import jax.numpy as jnp
from jax import lax
from jax.sharding import PartitionSpec as P

HEAD_DIM = 128
STEP = 10


NORM_EPS = 1e-06
THETA = 10000.0
CLIP_VALUE = 1.0
BETA_ONE = 0.9
BETA_TWO = 0.999
ADAM_EPS = 1e-08
DECAY = 0.1
RATE_MATRIX = 0.02
RATE_EXPERT = 0.1
RATE_GAIN = 0.3
MASKED = -1e30

F32 = jnp.float32
BF16 = jnp.bfloat16


def contract(left, right, left_dim, right_dim):
    return lax.dot_general(
        left, right, (((left_dim,), (right_dim,)), ((), ())), preferred_element_type=F32
    )


def rotary_tables(places, head_dim):
    half = head_dim // 2
    freq = THETA ** (-2.0 * jnp.arange(half, dtype=F32) / head_dim)
    angle = places.astype(F32)[:, None] * freq
    cosine = jnp.concatenate([jnp.cos(angle), jnp.cos(angle)], -1)[:, None, :]
    sine = jnp.concatenate([jnp.sin(angle), jnp.sin(angle)], -1)[:, None, :]
    return (cosine, sine)


def turn(values, cosine, sine):
    half = values.shape[-1] // 2
    turned = jnp.concatenate([-values[..., half:], values[..., :half]], -1)
    return values * cosine + turned * sine


def norm_forward(values, gain):
    inverse = lax.rsqrt(jnp.mean(values * values, axis=-1, keepdims=True) + NORM_EPS)
    scaled = values * inverse
    return ((scaled * gain).astype(BF16), scaled, inverse)


def norm_backward(grad, scaled, inverse, gain):
    local = grad * gain
    return inverse * (local - scaled * jnp.mean(local * scaled, axis=-1, keepdims=True))


def adam(master, first, second, grad, scale, rate):
    clipped = grad * scale
    first_new = BETA_ONE * first + (1.0 - BETA_ONE) * clipped
    second_new = BETA_TWO * second + (1.0 - BETA_TWO) * clipped * clipped
    first_hat = first_new / (1.0 - BETA_ONE**STEP)
    second_hat = second_new / (1.0 - BETA_TWO**STEP)
    master_new = master - rate * (first_hat / (jnp.sqrt(second_hat) + ADAM_EPS) + DECAY * master)
    return (master_new, first_new, second_new)


def after(value, *others):
    return lax.optimization_barrier((value,) + others)[0]


def swap(value, mask):
    size = lax.axis_size("expert")
    return lax.ppermute(value, "expert", [(i, i ^ mask) for i in range(size)])


def rotate(value, step):
    size = lax.axis_size("dp")
    return lax.ppermute(value, "dp", [(i, (i + step) % size) for i in range(size)])


def shift(value, step):
    size = lax.axis_size("dp")
    return lax.ppermute(
        value, "dp", [(i, i + step) for i in range(size) if 0 <= i + step < size]
    )


def put(buffer, block, index, axis):
    return lax.dynamic_update_slice_in_dim(buffer, jnp.expand_dims(block, axis), index, axis)


def pick(buffer, index, axis):
    return lax.dynamic_index_in_dim(buffer, index, axis, keepdims=False)


def gather_rotations(block):
    size, here = lax.axis_size("dp"), lax.axis_index("dp")
    received = [block] + [rotate(block, step) for step in range(1, size)]
    out = jnp.zeros((size,) + block.shape, block.dtype)
    for step, piece in enumerate(received):
        out = put(out, piece, (here - step) % size, 0)
    return out


def gather_swaps(block):
    size = lax.axis_size("expert")
    received = {0: block}
    for mask in range(2, size, 2):
        received[mask] = swap(block, mask)
    for mask in range(0, size, 2):
        received[mask + 1] = swap(received[mask], 1)
    return [received[mask] for mask in range(size)]


def gather_dense(block):
    size, here = lax.axis_size("expert"), lax.axis_index("expert")
    stacked = gather_rotations(block)
    received = gather_swaps(stacked)
    out = jnp.zeros((stacked.shape[0], size) + block.shape, block.dtype)
    for mask, piece in enumerate(received):
        out = put(out, piece, here ^ mask, 1)
    return out


def scatter_swaps(blocks):
    size = lax.axis_size("expert")
    other = swap(jnp.stack([blocks[m].astype(BF16) for m in range(1, size, 2)]), 1)
    summed = [blocks[m].astype(F32) + other[m // 2].astype(F32) for m in range(0, size, 2)]
    total = summed[0]
    for index in range(1, size // 2):
        total = total + swap(summed[index].astype(BF16), 2 * index).astype(F32)
    return total


def scatter_dense(grad):
    size, here = lax.axis_size("expert"), lax.axis_index("expert")
    deep, level = lax.axis_size("dp"), lax.axis_index("dp")
    core, chip = here % 2, here // 2
    low = grad.astype(BF16).reshape((deep, size // 2, 2) + grad.shape[2:])
    other = swap(pick(low, 1 - core, 2), 1)
    summed = (pick(low, core, 2).astype(F32) + other.astype(F32)).astype(BF16)
    total = pick(summed, chip, 1).astype(F32)
    for mask in range(1, size // 2):
        total = total + swap(pick(summed, chip ^ mask, 1), 2 * mask).astype(F32)
    column = total.astype(BF16)
    result = pick(total, level, 0)
    for step in range(1, deep):
        result = result + rotate(pick(column, (level + step) % deep, 0), step).astype(F32)
    return result


def roles(size, here):
    low = here < size // 2
    return (here, here ^ 1, jnp.where(low, 2, 1), jnp.where(low, 3, 0))


def send(value, pairs):
    return lax.ppermute(value, "dp", pairs)


ENDS_IN = [(1, 0), (2, 3)]
ENDS_OUT = [(0, 1), (3, 2)]
PAIRS = [(0, 1), (1, 0), (2, 3), (3, 2)]
MIDDLE = [(1, 2), (2, 1)]
LEAP = [(0, 2), (3, 1)]
LEAP_BACK = [(2, 0), (1, 3)]


def line_first(block):
    return (send(block, PAIRS), send(block, MIDDLE), send(block, LEAP))


def line_second(first):
    pair, near, far = first
    return (pair, near + send(near, ENDS_IN), far + send(far, ENDS_IN))


def line_join(block, pieces, axis):
    size, here = lax.axis_size("dp"), lax.axis_index("dp")
    shape = block.shape[:axis] + (size,) + block.shape[axis:]
    out = jnp.zeros(shape, block.dtype)
    for piece, index in zip((block,) + pieces, roles(size, here)):
        out = put(out, piece, index, axis)
    return out


def line_scatter(blocks):
    own, pair, near, far = blocks
    here = lax.axis_index("dp")
    inner = (here == 1) | (here == 2)
    from_pair = send(pair, PAIRS)
    near_in, far_in = send(near, ENDS_OUT), send(far, ENDS_OUT)
    near_sum = (near.astype(F32) + near_in.astype(F32)).astype(BF16)
    far_sum = (far.astype(F32) + far_in.astype(F32)).astype(BF16)
    near_out, far_out = send(near_sum, MIDDLE), send(far_sum, LEAP_BACK)
    return (
        own.astype(F32) + from_pair.astype(F32) + near_out.astype(F32) + far_out.astype(F32)
    )


def rotation_scatter(stacked):
    size, here = lax.axis_size("dp"), lax.axis_index("dp")
    total = pick(stacked, here, 0).astype(F32)
    for step in range(1, size):
        total = total + rotate(pick(stacked, (here + step) % size, 0), step).astype(F32)
    return total


def visible(starts, rows, place):
    index = jnp.arange(starts.shape[0], dtype=jnp.int32)
    own_start = lax.dynamic_slice_in_dim(starts, place, rows)
    own_index = place + jnp.arange(rows, dtype=jnp.int32)
    return (own_start[:, None] == starts[None, :]) & (index[None, :] <= own_index[:, None])


def expert_forward(tokens, weights):
    gate_part = contract(tokens, weights[0], 1, 0)
    up_part = contract(tokens, weights[1], 1, 0)
    hidden = (jax.nn.silu(gate_part) * up_part).astype(BF16)
    result = contract(hidden, weights[2], 1, 1).astype(BF16)
    return gate_part, up_part, hidden, result


def expert_backward(tokens, weights, gate_part, up_part, grad_pair):
    grad_hidden = contract(grad_pair, weights[2], 1, 0)
    sigma = jax.nn.sigmoid(gate_part)
    grad_gate = (grad_hidden * up_part * sigma * (1.0 + gate_part * (1.0 - sigma))).astype(BF16)
    grad_up = (grad_hidden * gate_part * sigma).astype(BF16)
    entry = (contract(grad_gate, weights[0], 1, 1) + contract(grad_up, weights[1], 1, 1)).astype(
        BF16
    )
    return grad_gate, grad_up, entry


def body(
    block_input_vectors,
    output_sensitivity,
    rotary_offsets,
    dispatched_specialist_ids,
    specialist_quotas,
    storage_holder,
    mixer_projection_matrices,
    mixer_mean_estimate,
    mixer_variance_estimate,
    common_projection_matrices,
    common_mean_estimate,
    common_variance_estimate,
    gating_projection_matrix,
    gating_mean_estimate,
    gating_variance_estimate,
    scaling_factors,
    scaling_mean_estimate,
    scaling_variance_estimate,
    dispatched_projection_matrices,
    dispatched_mean_estimate,
    dispatched_variance_estimate,
):
    token_rows = block_input_vectors.shape[1]
    width = block_input_vectors.shape[2]
    head_dim = HEAD_DIM
    heads = width // head_dim
    length = rotary_offsets.shape[1]
    specialist_total = specialist_quotas.shape[0]
    expert_local = dispatched_projection_matrices.shape[0]
    hidden_width = dispatched_projection_matrices.shape[3]
    part_rows = dispatched_projection_matrices.shape[2]
    dense_rows = mixer_projection_matrices.shape[1]
    groups = lax.axis_size("expert")
    deep = lax.axis_size("dp")
    here = lax.axis_index("expert")
    level = lax.axis_index("dp")
    scale_attn = head_dim ** (-0.5)
    straight = deep == 4

    attn_own = mixer_projection_matrices.astype(BF16)
    shared_own = common_projection_matrices.astype(BF16)
    router_own = gating_projection_matrix.astype(BF16)
    gain_own = scaling_factors.astype(BF16)
    expert_own = dispatched_projection_matrices.astype(BF16)

    small = jnp.concatenate([router_own.reshape(-1), gain_own.reshape(-1)])
    small_rows = -(-small.shape[0] // width)
    first_rows = 3 * dense_rows + small_rows
    fill = -first_rows % 8
    small = jnp.pad(small, (0, (small_rows + fill) * width - small.shape[0]))
    first_block = jnp.concatenate(
        [attn_own[:3].reshape(3 * dense_rows, width), small.reshape(small_rows + fill, width)], 0
    )
    first_all = gather_dense(first_block)
    projections = (
        first_all[:, :, : 3 * dense_rows]
        .reshape(deep, groups, 3, dense_rows, width)
        .transpose(2, 0, 1, 3, 4)
        .reshape(3, width, width)
    )
    small_all = first_all[:, :, 3 * dense_rows :].reshape(deep, groups, -1)
    router_low = small_all[:, :, : dense_rows * specialist_total].reshape(width, specialist_total)
    gain_low = (
        small_all[:, :, dense_rows * specialist_total : dense_rows * (specialist_total + 2)]
        .reshape(deep, groups, 2, dense_rows)
        .transpose(2, 0, 1, 3)
        .reshape(2, width)
    )
    gain_one = gain_low[0].astype(F32)
    gain_two = gain_low[1].astype(F32)

    inputs_low = block_input_vectors[0]
    sequence = jnp.zeros((deep, token_rows, width), BF16)
    sequence = put(sequence, inputs_low, level, 0)
    for step in range(1, deep):
        sequence = put(sequence, shift(inputs_low, step), (level - step) % deep, 0)
    sequence = sequence.reshape(length, width).astype(F32)

    out_all = gather_dense(attn_own[3])
    out_low = out_all.reshape(width, width)
    shared_all = gather_dense(shared_own.reshape(3 * dense_rows, hidden_width))
    shared_low = (
        shared_all.reshape(deep, groups, 3, dense_rows, hidden_width)
        .transpose(2, 0, 1, 3, 4)
        .reshape(3, width, hidden_width)
    )

    expert_low = []
    for number in range(expert_local):
        if straight:
            pieces = line_second(line_first(expert_own[number]))
            whole = line_join(expert_own[number], pieces, 1)
        else:
            whole = gather_rotations(expert_own[number]).transpose(1, 0, 2, 3)
        expert_low.append(whole.reshape(3, width, hidden_width))

    grad_low = output_sensitivity[0]
    grad_out = grad_low.astype(F32)
    grads_plane = jnp.concatenate(gather_swaps(grad_low), 0)

    normed_all, scaled_all, _ = norm_forward(sequence, gain_one)
    inputs = inputs_low.astype(F32)
    normed, scaled_one, inverse_one = norm_forward(inputs, gain_one)
    place = level * token_rows
    cosine_all, sine_all = rotary_tables(rotary_offsets[0], head_dim)
    cosine = lax.dynamic_slice_in_dim(cosine_all, place, token_rows)
    sine = lax.dynamic_slice_in_dim(sine_all, place, token_rows)
    query = turn(
        contract(normed, projections[0], 1, 0).reshape(token_rows, heads, head_dim), cosine, sine
    ).astype(BF16)
    keys = turn(
        contract(normed_all, projections[1], 1, 0).reshape(length, heads, head_dim),
        cosine_all,
        sine_all,
    ).astype(BF16)
    values = contract(normed_all, projections[2], 1, 0).astype(BF16)
    values = values.reshape(length, heads, head_dim)
    starts = jnp.arange(length, dtype=jnp.int32) - rotary_offsets[0]
    allowed = visible(starts, token_rows, place)[None]
    scores = jnp.einsum("qhd,khd->hqk", query, keys, preferred_element_type=F32) * scale_attn
    weights = jax.nn.softmax(jnp.where(allowed, scores, MASKED), axis=-1)
    weights_low = weights.astype(BF16)
    mixed = jnp.einsum("hqk,khd->qhd", weights_low, values, preferred_element_type=F32)
    mixed_low = mixed.reshape(token_rows, width).astype(BF16)
    middle = inputs + contract(mixed_low, out_low, 1, 0)
    second, scaled_two, inverse_two = norm_forward(middle, gain_two)

    probs = jax.nn.softmax(contract(second, router_low, 1, 0), axis=-1)
    experts = jnp.arange(specialist_total, dtype=jnp.int32)
    named = jnp.any(dispatched_specialist_ids[0][:, :, None] == experts, axis=1)
    order = jnp.arange(token_rows)
    earlier = contract(
        (order[:, None] > order[None, :]).astype(BF16), named.astype(BF16), 1, 0
    )
    kept = named & (earlier < specialist_quotas.astype(F32)[None, :])
    gate = jnp.where(kept, probs, 0.0)
    to_storage = (storage_holder[:, None] == experts[None, :]).astype(F32)
    gate_stored = jnp.sum(gate[:, :, None] * to_storage[None], axis=1)
    gates_sent = gate_stored.reshape(token_rows, groups, expert_local).transpose(1, 0, 2)
    gates_received = lax.all_to_all(gates_sent, "expert", 0, 0, tiled=True)
    relative = here ^ jnp.arange(groups)
    gates_plane = gates_received[relative].reshape(groups * token_rows, expert_local)

    tokens = jnp.concatenate(gather_swaps(second), 0)

    plane_rows = groups * token_rows
    routed_part = jnp.zeros((plane_rows, width), F32)
    entry_part = jnp.zeros((plane_rows, width), F32)
    grads_plane_wide = grads_plane.astype(F32)
    gate_grads = []
    expert_sums = []
    for number in range(expert_local):
        gate_column = gates_plane[:, number : number + 1]
        gate_part, up_part, hidden, result = expert_forward(tokens, expert_low[number])
        result_wide = result.astype(F32)
        routed_part = routed_part + gate_column * result_wide
        gate_grads.append(jnp.sum(grads_plane_wide * result_wide, axis=-1))
        grad_pair = (gate_column * grads_plane_wide).astype(BF16)
        grad_gate, grad_up, entry = expert_backward(
            tokens, expert_low[number], gate_part, up_part, grad_pair
        )
        entry_part = entry_part + entry.astype(F32)
        expert_grad = jnp.stack(
            [
                contract(tokens, grad_gate, 0, 0).astype(BF16),
                contract(tokens, grad_up, 0, 0).astype(BF16),
                contract(grad_pair, hidden, 0, 0).astype(BF16),
            ]
        ).reshape(3, deep, part_rows, hidden_width)
        if straight:
            expert_sums.append(
                line_scatter([pick(expert_grad, index, 1) for index in roles(deep, level)])
            )
        else:
            expert_sums.append(rotation_scatter(expert_grad.transpose(1, 0, 2, 3)))
    expert_sum = jnp.stack(expert_sums)

    entry_blocks = entry_part.reshape(groups, token_rows, width)
    grad_second = scatter_swaps([entry_blocks[m] for m in range(groups)])
    routed_blocks = routed_part.reshape(groups, token_rows, width)
    routed = scatter_swaps([routed_blocks[m] for m in range(groups)])
    gate_grad_sent = jnp.stack(gate_grads, -1).reshape(groups, token_rows, expert_local)[relative]
    gate_grad_back = lax.all_to_all(gate_grad_sent, "expert", 0, 0, tiled=True)
    gate_grad_stored = gate_grad_back.transpose(1, 0, 2).reshape(token_rows, specialist_total)
    grad_prob = jnp.sum(gate_grad_stored[:, None, :] * to_storage[None], axis=-1)
    grad_prob = jnp.where(kept, grad_prob, 0.0)

    gate_shared = contract(second, shared_low[0], 1, 0)
    up_shared = contract(second, shared_low[1], 1, 0)
    hidden_shared = (jax.nn.silu(gate_shared) * up_shared).astype(BF16)
    shared_out = contract(hidden_shared, shared_low[2], 1, 1)
    grad_gate_shared, grad_up_shared, _ = expert_backward(
        second, shared_low, gate_shared, up_shared, grad_low
    )
    shared_entry = contract(grad_gate_shared, shared_low[0], 1, 1) + contract(
        grad_up_shared, shared_low[1], 1, 1
    )
    block_out = (middle + shared_out + routed).astype(BF16)

    grad_logit = (probs * (grad_prob - jnp.sum(probs * grad_prob, axis=-1, keepdims=True))).astype(
        BF16
    )
    router_grad = contract(second, grad_logit, 0, 0)
    grad_second = grad_second + contract(grad_logit, router_low, 1, 1) + shared_entry
    shared_grad = jnp.stack(
        [
            contract(second, grad_gate_shared, 0, 0),
            contract(second, grad_up_shared, 0, 0),
            contract(grad_low, hidden_shared, 0, 0),
        ]
    )
    gain_two_grad = jnp.sum(grad_second * scaled_two, axis=0)
    grad_middle = norm_backward(grad_second, scaled_two, inverse_two, gain_two) + grad_out
    grad_attn_out = grad_middle.astype(BF16)
    out_grad = contract(mixed_low, grad_attn_out, 0, 0)
    grad_mixed = contract(grad_attn_out, out_low, 1, 1).astype(BF16)
    grad_mixed = grad_mixed.reshape(token_rows, heads, head_dim)
    correction = jnp.sum(grad_mixed.astype(F32) * mixed, axis=-1).T
    grad_weights = jnp.einsum("qhd,khd->hqk", grad_mixed, values, preferred_element_type=F32)
    grad_scores = jnp.where(
        allowed, weights * (grad_weights - correction[..., None]), 0.0
    ).astype(BF16)
    grad_query = (
        jnp.einsum("hqk,khd->qhd", grad_scores, keys, preferred_element_type=F32) * scale_attn
    )
    grad_keys = (
        jnp.einsum("hqk,qhd->khd", grad_scores, query, preferred_element_type=F32) * scale_attn
    )
    grad_values = jnp.einsum("hqk,qhd->khd", weights_low, grad_mixed, preferred_element_type=F32)
    grad_query_low = turn(grad_query, cosine, -sine).reshape(token_rows, width).astype(BF16)
    grad_key_low = turn(grad_keys, cosine_all, -sine_all).reshape(length, width).astype(BF16)
    grad_value_low = grad_values.reshape(length, width).astype(BF16)
    projection_grad = jnp.stack(
        [
            contract(normed, grad_query_low, 0, 0),
            contract(normed_all, grad_key_low, 0, 0),
            contract(normed_all, grad_value_low, 0, 0),
        ]
    )
    grad_normed_all = contract(grad_key_low, projections[1], 1, 1) + contract(
        grad_value_low, projections[2], 1, 1
    )
    grad_normed_own = contract(grad_query_low, projections[0], 1, 1)
    gain_one_grad = jnp.sum(grad_normed_all * scaled_all, axis=0) + jnp.sum(
        grad_normed_own * scaled_one, axis=0
    )
    normed_low = grad_normed_all.astype(BF16).reshape(deep, token_rows, width)
    grad_normed = grad_normed_own + pick(
        grad_normed_all.reshape(deep, token_rows, width), level, 0
    )
    for step in range(1, deep):
        grad_normed = grad_normed + shift(pick(normed_low, (level - step) % deep, 0), -step).astype(
            F32
        )
    grad_inputs = norm_backward(grad_normed, scaled_one, inverse_one, gain_one) + grad_middle

    def by_owner(grad):
        return grad.reshape(grad.shape[0], deep, groups, dense_rows, grad.shape[-1]).transpose(
            1, 2, 0, 3, 4
        )

    small_grad = jnp.concatenate(
        [
            router_grad.reshape(deep, groups, dense_rows * specialist_total),
            jnp.stack([gain_one_grad, gain_two_grad])
            .reshape(2, deep, groups, dense_rows)
            .transpose(1, 2, 0, 3)
            .reshape(deep, groups, 2 * dense_rows),
        ],
        -1,
    )
    small_grad = jnp.pad(
        small_grad, ((0, 0), (0, 0), (0, (small_rows + fill) * width - small_grad.shape[-1]))
    ).reshape(deep, groups, small_rows + fill, width)
    projection_sums = scatter_dense(
        jnp.concatenate(
            [
                by_owner(projection_grad).reshape(deep, groups, 3 * dense_rows, width),
                small_grad,
            ],
            2,
        )
    )
    out_sum = scatter_dense(out_grad.reshape(deep, groups, dense_rows, width))
    shared_sum = scatter_dense(
        by_owner(shared_grad).reshape(deep, groups, 3 * dense_rows, hidden_width)
    ).reshape(3, dense_rows, hidden_width)
    attn_sum = jnp.concatenate(
        [projection_sums[: 3 * dense_rows].reshape(3, dense_rows, width), out_sum[None]], 0
    )
    small_sum = projection_sums[3 * dense_rows :].reshape(-1)
    router_sum = small_sum[: dense_rows * specialist_total].reshape(dense_rows, specialist_total)
    gain_sum = small_sum[
        dense_rows * specialist_total : dense_rows * (specialist_total + 2)
    ].reshape(2, dense_rows)

    local_squares = (
        jnp.sum(attn_sum * attn_sum)
        + jnp.sum(shared_sum * shared_sum)
        + jnp.sum(router_sum * router_sum)
        + jnp.sum(gain_sum * gain_sum)
        + jnp.sum(expert_sum * expert_sum)
    )
    everyone = deep * groups
    spread = jnp.broadcast_to(local_squares, (everyone, 8, 128))
    squares = lax.all_to_all(spread, ("dp", "expert"), 0, 0, tiled=True)
    grad_norm = jnp.sqrt(jnp.sum(squares[:, 0, 0]))
    scale = jnp.minimum(1.0, CLIP_VALUE / (grad_norm + 1e-06))
    attn_new, attn_moment, attn_square = adam(
        mixer_projection_matrices,
        mixer_mean_estimate,
        mixer_variance_estimate,
        attn_sum,
        scale,
        RATE_MATRIX,
    )
    shared_new, shared_moment, shared_square = adam(
        common_projection_matrices,
        common_mean_estimate,
        common_variance_estimate,
        shared_sum,
        scale,
        RATE_MATRIX,
    )
    router_new, router_moment, router_square = adam(
        gating_projection_matrix,
        gating_mean_estimate,
        gating_variance_estimate,
        router_sum,
        scale,
        RATE_MATRIX,
    )
    gain_new, gain_moment, gain_square = adam(
        scaling_factors,
        scaling_mean_estimate,
        scaling_variance_estimate,
        gain_sum,
        scale,
        RATE_GAIN,
    )
    expert_new, expert_moment, expert_square = adam(
        dispatched_projection_matrices,
        dispatched_mean_estimate,
        dispatched_variance_estimate,
        expert_sum,
        scale,
        RATE_EXPERT,
    )
    return (
        block_out[None],
        grad_inputs[None],
        grad_norm,
        attn_new,
        attn_moment,
        attn_square,
        attn_new.astype(BF16),
        shared_new,
        shared_moment,
        shared_square,
        shared_new.astype(BF16),
        router_new,
        router_moment,
        router_square,
        router_new.astype(BF16),
        gain_new,
        gain_moment,
        gain_square,
        expert_new,
        expert_moment,
        expert_square,
        expert_new.astype(BF16),
    )


def solution(mesh):
    placed = (
        P("expert", "dp", None),
        P("expert", "dp", None),
        P("expert", None),
        P("expert", "dp", None),
        P(),
        P(),
        P(None, ("dp", "expert"), None),
        P(None, ("dp", "expert"), None),
        P(None, ("dp", "expert"), None),
        P(None, ("dp", "expert"), None),
        P(None, ("dp", "expert"), None),
        P(None, ("dp", "expert"), None),
        P(("dp", "expert"), None),
        P(("dp", "expert"), None),
        P(("dp", "expert"), None),
        P(None, ("dp", "expert")),
        P(None, ("dp", "expert")),
        P(None, ("dp", "expert")),
        P("expert", None, "dp", None),
        P("expert", None, "dp", None),
        P("expert", None, "dp", None),
    )
    return jax.shard_map(
        body,
        mesh=mesh,
        in_specs=placed,
        out_specs=(
            P("expert", "dp", None),
            P("expert", "dp", None),
            P(),
            P(None, ("dp", "expert"), None),
            P(None, ("dp", "expert"), None),
            P(None, ("dp", "expert"), None),
            P(None, ("dp", "expert"), None),
            P(None, ("dp", "expert"), None),
            P(None, ("dp", "expert"), None),
            P(None, ("dp", "expert"), None),
            P(None, ("dp", "expert"), None),
            P(("dp", "expert"), None),
            P(("dp", "expert"), None),
            P(("dp", "expert"), None),
            P(("dp", "expert"), None),
            P(None, ("dp", "expert")),
            P(None, ("dp", "expert")),
            P(None, ("dp", "expert")),
            P("expert", None, "dp", None),
            P("expert", None, "dp", None),
            P("expert", None, "dp", None),
            P("expert", None, "dp", None),
        ),
        check_vma=False,
    )
```

```python
import functools

import jax
import jax.numpy as jnp
from jax import lax
from jax.experimental import pallas as pl
from jax.experimental.pallas import tpu as pltpu
from jax.sharding import PartitionSpec as P

HEAD_DIM = 128
STEP = 10


NORM_EPS = 1e-06
THETA = 10000.0
CLIP_VALUE = 1.0
BETA_ONE = 0.9
BETA_TWO = 0.999
ADAM_EPS = 1e-08
DECAY = 0.1
RATE_MATRIX = 0.02
RATE_EXPERT = 0.1
RATE_GAIN = 0.3
MASKED = -1e30

F32 = jnp.float32
BF16 = jnp.bfloat16


def contract(left, right, left_dim, right_dim):
    return lax.dot_general(
        left, right, (((left_dim,), (right_dim,)), ((), ())), preferred_element_type=F32
    )


def rotary_tables(places, head_dim):
    half = head_dim // 2
    freq = THETA ** (-2.0 * jnp.arange(half, dtype=F32) / head_dim)
    angle = places.astype(F32)[:, None] * freq
    cosine, sine = jnp.cos(angle), jnp.sin(angle)
    return (jnp.concatenate([cosine, cosine], -1), jnp.concatenate([-sine, sine], -1))


def norm_forward(values, gain):
    inverse = lax.rsqrt(jnp.mean(values * values, axis=-1, keepdims=True) + NORM_EPS)
    scaled = values * inverse
    return ((scaled * gain).astype(BF16), scaled, inverse)


def norm_backward(grad, scaled, inverse, gain):
    local = grad * gain
    return inverse * (local - scaled * jnp.mean(local * scaled, axis=-1, keepdims=True))


def adam(master, first, second, grad, scale, rate):
    clipped = grad * scale
    first_new = BETA_ONE * first + (1.0 - BETA_ONE) * clipped
    second_new = BETA_TWO * second + (1.0 - BETA_TWO) * clipped * clipped
    first_hat = first_new / (1.0 - BETA_ONE**STEP)
    second_hat = second_new / (1.0 - BETA_TWO**STEP)
    master_new = master - rate * (first_hat / (jnp.sqrt(second_hat) + ADAM_EPS) + DECAY * master)
    return (master_new, first_new, second_new)


def after(value, *others):
    return lax.optimization_barrier((value,) + others)[0]


def swap(value, mask):
    size = lax.axis_size("expert")
    return lax.ppermute(value, "expert", [(i, i ^ mask) for i in range(size)])


def rotate(value, step):
    size = lax.axis_size("dp")
    return lax.ppermute(value, "dp", [(i, (i + step) % size) for i in range(size)])


def shift(value, step):
    size = lax.axis_size("dp")
    return lax.ppermute(
        value, "dp", [(i, i + step) for i in range(size) if 0 <= i + step < size]
    )


def put(buffer, block, index, axis):
    return lax.dynamic_update_slice_in_dim(buffer, jnp.expand_dims(block, axis), index, axis)


def pick(buffer, index, axis):
    return lax.dynamic_index_in_dim(buffer, index, axis, keepdims=False)


def fan(block, *others):
    size = lax.axis_size("expert")
    block = after(block, *others) if others else block
    return [block] + [swap(block, mask) for mask in range(2, size, 2)]


def gather_swaps(block, *others):
    even = jnp.stack(fan(block, *others))
    return even, swap(even, 1)


def join_cores(even, other):
    return [even[k].astype(F32) + other[k].astype(F32) for k in range(even.shape[0])]


def join_chips(summed):
    total = summed[0]
    for index in range(1, len(summed)):
        total = total + swap(summed[index].astype(BF16), 2 * index).astype(F32)
    return total


def scatter_dense(grad):
    size, here = lax.axis_size("expert"), lax.axis_index("expert")
    deep, level = lax.axis_size("dp"), lax.axis_index("dp")
    core, chip = here % 2, here // 2
    low = grad.astype(BF16).reshape((deep, size // 2, 2) + grad.shape[2:])
    other = swap(pick(low, 1 - core, 2), 1)
    summed = (pick(low, core, 2).astype(F32) + other.astype(F32)).astype(BF16)
    total = pick(summed, chip, 1).astype(F32)
    for mask in range(1, size // 2):
        total = total + swap(pick(summed, chip ^ mask, 1), 2 * mask).astype(F32)
    column = total.astype(BF16)
    result = pick(total, level, 0)
    for step in range(1, deep):
        result = result + rotate(pick(column, (level + step) % deep, 0), step).astype(F32)
    return result


VMEM_LIMIT = 60 * 1024 * 1024


def product(left, right, left_dim, right_dim):
    return lax.dot_general(
        left, right, (((left_dim,), (right_dim,)), ((), ())), preferred_element_type=F32
    )


def kernel_params(steps):
    return pltpu.CompilerParams(
        dimension_semantics=("arbitrary",) * steps, vmem_limit_bytes=VMEM_LIMIT
    )


def whole(array):
    shape = array.shape
    return pl.BlockSpec(shape, lambda *_: (0,) * len(shape), pipeline_mode=pl.Buffered(1))


def assemble_kernel(place_ref, even, odd, out):
    core = place_ref[0] % 2
    out[:, :, pl.ds(core, 1)] = jnp.swapaxes(even[0], 0, 1)[:, :, None]
    out[:, :, pl.ds(1 - core, 1)] = jnp.swapaxes(odd[0], 0, 1)[:, :, None]


def assemble(even, odd):
    chips, deep, parts, rows, width = even.shape
    here = lax.axis_index("expert")
    chip = pl.BlockSpec(
        (1, deep, parts, rows, width), lambda c, p: (c ^ (p[0] // 2), 0, 0, 0, 0)
    )
    joined = pl.pallas_call(
        assemble_kernel,
        grid_spec=pltpu.PrefetchScalarGridSpec(
            num_scalar_prefetch=1,
            grid=(chips,),
            in_specs=[chip, chip],
            out_specs=pl.BlockSpec(
                (parts, deep, 2, rows, width), lambda c, p: (0, 0, c, 0, 0)
            ),
        ),
        out_shape=jax.ShapeDtypeStruct((parts, deep, 2 * chips, rows, width), even.dtype),
        compiler_params=kernel_params(1),
        cost_estimate=pl.CostEstimate(
            flops=0, bytes_accessed=8 * even.size, transcendentals=0
        ),
        name="assemble",
    )(here[None], even, odd)
    return joined.reshape(parts, deep * 2 * chips * rows, width)


def turn_head(values, cosine, sine):
    return values * cosine + pltpu.roll(values, HEAD_DIM // 2, 1) * sine


def head_weights(query, keys, allowed):
    scores = product(query, keys, 1, 1) * HEAD_DIM ** (-0.5)
    scores = jnp.where(allowed, scores, MASKED)
    raised = jnp.exp(scores - jnp.max(scores, axis=-1, keepdims=True))
    return raised / jnp.sum(raised, axis=-1, keepdims=True)


def visible_keys(place, own_starts, starts):
    shape = (own_starts.shape[0], starts.shape[1])
    query_index = place + lax.broadcasted_iota(jnp.int32, shape, 0)
    key_index = lax.broadcasted_iota(jnp.int32, shape, 1)
    return (own_starts == starts) & (key_index <= query_index)


def attention_kernel(
    place_ref, normed, wq, wk, wv, cosine, sine, starts, own_starts, q_out, k_out, v_out, o_out, low_out
):
    rows = q_out.shape[0]
    place = pl.multiple_of(place_ref[0], rows)
    own = normed[pl.ds(place, rows), :]
    everything = normed[...]
    allowed = visible_keys(place, own_starts[...], starts[...])
    query = product(own, wq[0], 1, 0)
    keys = product(everything, wk[0], 1, 0)
    values = product(everything, wv[0], 1, 0).astype(BF16)
    v_out[...] = values
    own_cosine, own_sine = cosine[pl.ds(place, rows), :], sine[pl.ds(place, rows), :]
    for head in range(q_out.shape[1] // HEAD_DIM):
        lanes = slice(head * HEAD_DIM, (head + 1) * HEAD_DIM)
        turned_query = turn_head(query[:, lanes], own_cosine, own_sine).astype(BF16)
        turned_keys = turn_head(keys[:, lanes], cosine[...], sine[...]).astype(BF16)
        weights = head_weights(turned_query, turned_keys, allowed).astype(BF16)
        mixed = product(weights, values[:, lanes], 1, 0)
        q_out[:, lanes] = turned_query
        k_out[:, lanes] = turned_keys
        o_out[:, lanes] = mixed
        low_out[:, lanes] = mixed.astype(BF16)


def attention(place, normed, projections, cosine, sine, starts, rows):
    length, width = normed.shape
    span = 2 * HEAD_DIM
    own_starts = lax.dynamic_slice_in_dim(starts, place, rows)[:, None]
    starts = starts[None, :]
    column = lambda index: pl.BlockSpec((1, width, span), lambda p, _: (index, 0, p))
    blocks = lambda count: pl.BlockSpec((count, span), lambda p, _: (0, p))
    return pl.pallas_call(
        attention_kernel,
        grid_spec=pltpu.PrefetchScalarGridSpec(
            num_scalar_prefetch=1,
            grid=(width // span,),
            in_specs=[
                whole(normed),
                column(0),
                column(1),
                column(2),
                whole(cosine),
                whole(sine),
                whole(starts),
                whole(own_starts),
            ],
            out_specs=[blocks(rows), blocks(length), blocks(length), blocks(rows), blocks(rows)],
        ),
        out_shape=[
            jax.ShapeDtypeStruct((rows, width), BF16),
            jax.ShapeDtypeStruct((length, width), BF16),
            jax.ShapeDtypeStruct((length, width), BF16),
            jax.ShapeDtypeStruct((rows, width), F32),
            jax.ShapeDtypeStruct((rows, width), BF16),
        ],
        compiler_params=kernel_params(1),
        cost_estimate=pl.CostEstimate(
            flops=2 * width * width * (rows + 2 * length) + 4 * rows * length * width,
            bytes_accessed=6 * width * width + 10 * length * width,
            transcendentals=rows * length * width // HEAD_DIM,
        ),
        name="attention_forward",
    )(place[None], normed, projections, projections, projections, cosine, sine, starts, own_starts)


def attention_grad_kernel(
    place_ref, turned_normed, own_turned, wq, wk, wv, wo, q, k, v, o, arriving,
    cosine, sine, starts, own_starts, grads, normed_grad, own_grad, dq_s, dk_s, dv_s,
):
    rows = q.shape[0]
    place = pl.multiple_of(place_ref[0], rows)
    allowed = visible_keys(place, own_starts[...], starts[...])
    own_cosine, own_sine = cosine[pl.ds(place, rows), :], sine[pl.ds(place, rows), :]
    mixed_grad = product(arriving[...], wo[...], 1, 1).astype(BF16)
    for head in range(q.shape[1] // HEAD_DIM):
        lanes = slice(head * HEAD_DIM, (head + 1) * HEAD_DIM)
        query, keys, values = q[:, lanes], k[:, lanes], v[:, lanes]
        incoming = mixed_grad[:, lanes]
        weights = head_weights(query, keys, allowed)
        correction = jnp.sum(incoming.astype(F32) * o[:, lanes], axis=-1, keepdims=True)
        weights_grad = product(incoming, values, 1, 1)
        scores_grad = (weights * (weights_grad - correction)).astype(BF16)
        factor = HEAD_DIM ** (-0.5)
        query_grad = product(scores_grad, keys, 1, 0) * factor
        keys_grad = product(scores_grad, query, 0, 0) * factor
        values_grad = product(weights.astype(BF16), incoming, 0, 0)
        dq_s[:, lanes] = turn_head(query_grad, own_cosine, -own_sine).astype(BF16)
        dk_s[:, lanes] = turn_head(keys_grad, cosine[...], -sine[...]).astype(BF16)
        dv_s[:, lanes] = values_grad.astype(BF16)
    dq, dk, dv = dq_s[...], dk_s[...], dv_s[...]
    grads[0] = product(own_turned[...], dq, 1, 0).astype(BF16)
    grads[1] = product(turned_normed[...], dk, 1, 0).astype(BF16)
    grads[2] = product(turned_normed[...], dv, 1, 0).astype(BF16)
    part = product(dk, wk[0], 1, 1) + product(dv, wv[0], 1, 1)
    own_part = product(dq, wq[0], 1, 1)

    @pl.when(pl.program_id(0) == 0)
    def _():
        normed_grad[...] = part
        own_grad[...] = own_part

    @pl.when(pl.program_id(0) > 0)
    def _():
        normed_grad[...] += part
        own_grad[...] += own_part


def attention_grad(place, normed, own_normed, projections, wo, q, k, v, o, arriving, cosine, sine, starts):
    length, width = normed.shape
    rows = q.shape[0]
    span = 2 * HEAD_DIM
    own_starts = lax.dynamic_slice_in_dim(starts, place, rows)[:, None]
    starts = starts[None, :]
    turned, own_turned = normed.T, own_normed.T
    column = lambda index: pl.BlockSpec((1, width, span), lambda p, _: (index, 0, p))
    blocks = lambda count: pl.BlockSpec((count, span), lambda p, _: (0, p))
    return pl.pallas_call(
        attention_grad_kernel,
        grid_spec=pltpu.PrefetchScalarGridSpec(
            num_scalar_prefetch=1,
            grid=(width // span,),
            in_specs=[
                whole(turned),
                whole(own_turned),
                column(0),
                column(1),
                column(2),
                pl.BlockSpec((span, width), lambda p, _: (p, 0)),
                blocks(rows),
                blocks(length),
                blocks(length),
                blocks(rows),
                whole(arriving),
                whole(cosine),
                whole(sine),
                whole(starts),
                whole(own_starts),
            ],
            out_specs=[
                pl.BlockSpec((3, width, span), lambda p, _: (0, 0, p)),
                pl.BlockSpec((length, width), lambda p, _: (0, 0)),
                pl.BlockSpec((rows, width), lambda p, _: (0, 0)),
            ],
            scratch_shapes=[
                pltpu.VMEM((rows, span), BF16),
                pltpu.VMEM((length, span), BF16),
                pltpu.VMEM((length, span), BF16),
            ],
        ),
        out_shape=[
            jax.ShapeDtypeStruct((3, width, width), BF16),
            jax.ShapeDtypeStruct((length, width), F32),
            jax.ShapeDtypeStruct((rows, width), F32),
        ],
        compiler_params=kernel_params(1),
        cost_estimate=pl.CostEstimate(
            flops=4 * width * width * (rows + 2 * length) + 10 * rows * length * width,
            bytes_accessed=14 * width * width + 14 * length * width,
            transcendentals=rows * length * width // HEAD_DIM,
        ),
        name="attention_backward",
    )(
        place[None], turned, own_turned, projections, projections, projections, wo,
        q, k, v, o, arriving, cosine, sine, starts, own_starts,
    )


def expert_kernel(has_before, split, part_rows, *refs):
    odd_n, even_n, odd_c, even_c, gates, weights = refs[:6]
    refs = refs[6:]
    if has_before:
        routed_in, entry_in = refs[:2]
        refs = refs[2:]
    if split:
        routed_odd, routed_even, entry_odd, entry_even = refs[:4]
        refs = refs[4:]
    else:
        routed_out, entry_out = refs[:2]
        refs = refs[2:]
    gate_grad, hidden_out, pair_out, both, down, arrived = refs
    step = pl.program_id(0)
    half = pl.num_programs(0) // 2
    hidden_width = weights.shape[3]

    @pl.when(step == 0)
    def _():
        copies = []
        for level in range(weights.shape[0]):
            rows = pl.ds(level * part_rows, part_rows)
            for index in range(3):
                if index < 2:
                    target = both.at[rows, pl.ds(index * hidden_width, hidden_width)]
                else:
                    target = down.at[rows]
                copies.append(
                    pltpu.make_async_copy(
                        weights.at[level, index, pl.ds(0, part_rows)],
                        target,
                        arrived.at[level, index],
                    )
                )
        for copy in copies:
            copy.start()
        for copy in copies:
            copy.wait()

    first = step < half
    tokens = jnp.where(first, odd_n[0], even_n[0])
    incoming = jnp.where(first, odd_c[0], even_c[0]).astype(F32)
    gate = gates[...]
    parts = product(tokens, both[...], 1, 0)
    gate_part, up_part = parts[:, :hidden_width], parts[:, hidden_width:]
    sigma = 1.0 / (1.0 + jnp.exp(-gate_part))
    smooth = gate_part * sigma
    hidden = (smooth * up_part).astype(BF16)
    hidden_out[...] = hidden
    result = product(hidden, down[...], 1, 1).astype(BF16).astype(F32)
    gate_grad[...] = jnp.sum(incoming * result, axis=-1, keepdims=True)
    routed = gate * result
    grad_pair = (gate * incoming).astype(BF16)
    grad_hidden = product(grad_pair, down[...], 1, 0)
    grad_gate = (grad_hidden * up_part * sigma * (1.0 + gate_part * (1.0 - sigma))).astype(BF16)
    grad_up = (grad_hidden * smooth).astype(BF16)
    grad_parts = jnp.concatenate([grad_gate, grad_up], axis=1)
    pair_out[...] = grad_parts
    entry = product(grad_parts, both[...], 1, 1).astype(BF16).astype(F32)
    if has_before:
        routed = routed + routed_in[...]
        entry = entry + entry_in[...]
    if split:

        @pl.when(first)
        def _():
            routed_odd[0] = routed.astype(BF16)
            entry_odd[0] = entry.astype(BF16)

        @pl.when(jnp.logical_not(first))
        def _():
            routed_even[0] = routed.astype(BF16)
            entry_even[0] = entry.astype(BF16)
    else:
        routed_out[...] = routed
        entry_out[...] = entry


def expert_pass(tokens, grads, gates, weights, part_rows, before, split):
    even_n, odd_n = tokens
    even_c, odd_c = grads
    count, rows, width = even_n.shape
    hidden_width = weights.shape[3]
    tiles = 2 * count
    total = tiles * rows
    odd = pl.BlockSpec((1, rows, width), lambda t: (jnp.minimum(t, count - 1), 0, 0))
    even = pl.BlockSpec((1, rows, width), lambda t: (jnp.maximum(t - count, 0), 0, 0))
    tile = lambda size: pl.BlockSpec((rows, size), lambda t: (t, 0))
    in_specs = [odd, even, odd, even, tile(1), pl.BlockSpec(memory_space=pl.ANY)]
    operands = [odd_n, even_n, odd_c, even_c, gates, weights]
    if before is not None:
        in_specs += [tile(width), tile(width)]
        operands += list(before)
    if split:
        out_specs = [odd, even, odd, even]
        out_shape = [jax.ShapeDtypeStruct((count, rows, width), BF16)] * 4
    else:
        out_specs = [tile(width), tile(width)]
        out_shape = [jax.ShapeDtypeStruct((total, width), F32)] * 2
    out_specs += [tile(1), tile(hidden_width), tile(2 * hidden_width)]
    out_shape += [
        jax.ShapeDtypeStruct((total, 1), F32),
        jax.ShapeDtypeStruct((total, hidden_width), BF16),
        jax.ShapeDtypeStruct((total, 2 * hidden_width), BF16),
    ]
    return pl.pallas_call(
        functools.partial(expert_kernel, before is not None, split, part_rows),
        grid=(tiles,),
        in_specs=in_specs,
        out_specs=out_specs,
        out_shape=out_shape,
        scratch_shapes=[
            pltpu.VMEM((width, 2 * hidden_width), BF16),
            pltpu.VMEM((width, hidden_width), BF16),
            pltpu.SemaphoreType.DMA((weights.shape[0], 3)),
        ],
        compiler_params=kernel_params(1),
        cost_estimate=pl.CostEstimate(
            flops=12 * total * width * hidden_width,
            bytes_accessed=total * (8 * width + 6 * hidden_width) + 6 * width * hidden_width,
            transcendentals=total * hidden_width,
        ),
        name="expert_pass",
    )(*operands)


def expert_grad_kernel(odd_n, even_n, odd_c, even_c, gates, hidden, pair, out):
    count, rows, span = odd_n.shape
    half = count * rows
    hidden_width = hidden.shape[1]
    tokens = jnp.concatenate(
        [odd_n[...].reshape(half, span), even_n[...].reshape(half, span)], axis=0
    )
    incoming = jnp.concatenate(
        [odd_c[...].reshape(half, span), even_c[...].reshape(half, span)], axis=0
    )
    grad_pair = (gates[...] * incoming.astype(F32)).astype(BF16)
    both = product(tokens, pair[...], 0, 0)
    out[0] = both[:, :hidden_width].astype(BF16)
    out[1] = both[:, hidden_width:].astype(BF16)
    out[2] = product(grad_pair, hidden[...], 0, 0).astype(BF16)


def expert_grad(tokens, grads, gates, hidden, pair):
    even_n, odd_n = tokens
    even_c, odd_c = grads
    count, rows, width = even_n.shape
    hidden_width = hidden.shape[1]
    span = 256
    stack = pl.BlockSpec((count, rows, span), lambda t: (0, 0, t))
    return pl.pallas_call(
        expert_grad_kernel,
        grid=(width // span,),
        in_specs=[stack, stack, stack, stack, whole(gates), whole(hidden), whole(pair)],
        out_specs=pl.BlockSpec((3, span, hidden_width), lambda t: (0, t, 0)),
        out_shape=jax.ShapeDtypeStruct((3, width, hidden_width), BF16),
        compiler_params=kernel_params(1),
        cost_estimate=pl.CostEstimate(
            flops=12 * count * rows * width * hidden_width,
            bytes_accessed=8 * count * rows * (width + 2 * hidden_width) + 6 * width * hidden_width,
            transcendentals=0,
        ),
        name="expert_weight_grad",
    )(odd_n, even_n, odd_c, even_c, gates, hidden, pair)


def body(
    block_input_vectors,
    output_sensitivity,
    rotary_offsets,
    dispatched_specialist_ids,
    specialist_quotas,
    storage_holder,
    mixer_projection_matrices,
    mixer_mean_estimate,
    mixer_variance_estimate,
    common_projection_matrices,
    common_mean_estimate,
    common_variance_estimate,
    gating_projection_matrix,
    gating_mean_estimate,
    gating_variance_estimate,
    scaling_factors,
    scaling_mean_estimate,
    scaling_variance_estimate,
    dispatched_projection_matrices,
    dispatched_mean_estimate,
    dispatched_variance_estimate,
):
    token_rows = block_input_vectors.shape[1]
    width = block_input_vectors.shape[2]
    head_dim = HEAD_DIM
    heads = width // head_dim
    length = rotary_offsets.shape[1]
    specialist_total = specialist_quotas.shape[0]
    expert_local = dispatched_projection_matrices.shape[0]
    hidden_width = dispatched_projection_matrices.shape[3]
    part_rows = dispatched_projection_matrices.shape[2]
    dense_rows = mixer_projection_matrices.shape[1]
    groups = lax.axis_size("expert")
    deep = lax.axis_size("dp")
    here = lax.axis_index("expert")
    level = lax.axis_index("dp")
    scale_attn = head_dim ** (-0.5)
    straight = deep == 4

    attn_own = mixer_projection_matrices.astype(BF16)
    shared_own = common_projection_matrices.astype(BF16)
    router_own = gating_projection_matrix.astype(BF16)
    gain_own = scaling_factors.astype(BF16)
    expert_own = dispatched_projection_matrices.astype(BF16)

    everyone = deep * groups
    small = jnp.concatenate([router_own.reshape(-1), gain_own.reshape(-1)])
    small_size = small.shape[0]
    small_rows = -(-small_size // 1024) * 8
    small = jnp.pad(small, (0, small_rows * 128 - small_size)).reshape(small_rows, 128)
    small_all = lax.all_to_all(
        jnp.broadcast_to(small, (everyone, small_rows, 128)),
        ("dp", "expert"),
        0,
        0,
        tiled=True,
    ).reshape(everyone, small_rows * 128)
    router_size = dense_rows * specialist_total
    router_low = small_all[:, :router_size].reshape(width, specialist_total)
    gain_low = (
        small_all[:, router_size : router_size + 2 * dense_rows]
        .reshape(everyone, 2, dense_rows)
        .transpose(1, 0, 2)
        .reshape(2, width)
    )
    inputs_low = block_input_vectors[0]
    grad_low = output_sensitivity[0]
    grad_out = grad_low.astype(F32)
    attn_column = lax.all_gather(attn_own, "dp")
    projection_fan = fan(attn_column[:, :3])
    sequence = lax.all_gather(after(inputs_low, attn_column), "dp", axis=0, tiled=True)
    sequence, *projection_fan = lax.optimization_barrier((sequence, *projection_fan))
    expert_parts = [
        lax.all_gather(
            after(jnp.concatenate([expert_own[0], shared_own], 1), sequence), "dp"
        )
    ]
    projection_even = jnp.stack(projection_fan)
    projection_odd = swap(projection_even, 1)
    out_even, out_odd = gather_swaps(attn_column[:, 3:], sequence)
    for number in range(1, expert_local):
        expert_parts.append(
            lax.all_gather(after(expert_own[number], projection_odd), "dp")
        )
    projections = assemble(projection_even, projection_odd)
    out_low = assemble(out_even, out_odd)[0]
    grads_plane = gather_swaps(grad_low, out_even)
    shared_low = assemble(*gather_swaps(expert_parts[0][:, :, part_rows:]))
    gain_one = gain_low[0].astype(F32)
    gain_two = gain_low[1].astype(F32)

    sequence = sequence.astype(F32)

    normed_all, scaled_all, _ = norm_forward(sequence, gain_one)
    inputs = inputs_low.astype(F32)
    normed, scaled_one, inverse_one = norm_forward(inputs, gain_one)
    place = level * token_rows
    cosine_all, sine_all = rotary_tables(rotary_offsets[0], head_dim)
    starts = jnp.arange(length, dtype=jnp.int32) - rotary_offsets[0]
    query, keys, values, mixed, mixed_low = attention(
        place, normed_all, projections, cosine_all, sine_all, starts, token_rows
    )
    middle = inputs + contract(mixed_low, out_low, 1, 0)
    second, scaled_two, inverse_two = norm_forward(middle, gain_two)

    probs = jax.nn.softmax(contract(second, router_low, 1, 0), axis=-1)
    experts = jnp.arange(specialist_total, dtype=jnp.int32)
    named = jnp.any(dispatched_specialist_ids[0][:, :, None] == experts, axis=1)
    order = jnp.arange(token_rows)
    earlier = contract(
        (order[:, None] > order[None, :]).astype(BF16), named.astype(BF16), 1, 0
    )
    kept = named & (earlier < specialist_quotas.astype(F32)[None, :])
    gate = jnp.where(kept, probs, 0.0)
    to_storage = (storage_holder[:, None] == experts[None, :]).astype(F32)
    gate_stored = jnp.sum(gate[:, :, None] * to_storage[None], axis=1)
    gates_sent = gate_stored.reshape(token_rows, groups, expert_local).transpose(1, 0, 2)
    gates_received = lax.all_to_all(gates_sent, "expert", 0, 0, tiled=True)
    half = jnp.arange(groups // 2) * 2
    relative = here ^ jnp.concatenate([half + 1, half])
    gates_plane = gates_received[relative].reshape(groups * token_rows, expert_local)

    tokens = gather_swaps(second)

    gate_grads = []
    expert_sums = []
    before = None
    for number in range(expert_local):
        last = number == expert_local - 1
        gate_column = gates_plane[:, number : number + 1]
        parts = expert_pass(
            tokens, grads_plane, gate_column, expert_parts[number], part_rows, before, last
        )
        before, (gate_grad, hidden, pair) = parts[:-3], parts[-3:]
        gate_grads.append(gate_grad)
        if last:
            routed_odd, routed_even, entry_odd, entry_even = before
            entry_other = swap(entry_odd, 1)
            routed_other = swap(after(routed_odd, entry_other), 1)
            hidden = after(hidden, entry_other)
        expert_sums.append(
            lax.psum_scatter(
                expert_grad(tokens, grads_plane, gate_column, hidden, pair),
                "dp",
                scatter_dimension=1,
                tiled=True,
            ).astype(F32)
        )
    expert_sum = jnp.stack(expert_sums)

    grad_second = join_chips(join_cores(entry_even, entry_other))
    routed_even, routed_other = lax.optimization_barrier((routed_even, routed_other, grad_second))[:2]
    routed = join_chips(join_cores(routed_even, routed_other))
    mask = here ^ jnp.arange(groups)
    back = mask // 2 + jnp.where(mask % 2 == 1, 0, groups // 2)
    gate_grad_sent = jnp.concatenate(gate_grads, -1).reshape(groups, token_rows, expert_local)[back]
    gate_grad_back = lax.all_to_all(gate_grad_sent, "expert", 0, 0, tiled=True)
    gate_grad_stored = gate_grad_back.transpose(1, 0, 2).reshape(token_rows, specialist_total)
    grad_prob = jnp.sum(gate_grad_stored[:, None, :] * to_storage[None], axis=-1)
    grad_prob = jnp.where(kept, grad_prob, 0.0)

    gate_shared = contract(second, shared_low[0], 1, 0)
    up_shared = contract(second, shared_low[1], 1, 0)
    hidden_shared = (jax.nn.silu(gate_shared) * up_shared).astype(BF16)
    shared_out = contract(hidden_shared, shared_low[2], 1, 1)
    grad_hidden_shared = contract(grad_low, shared_low[2], 1, 0)
    sigma = jax.nn.sigmoid(gate_shared)
    grad_gate_shared = (
        grad_hidden_shared * up_shared * sigma * (1.0 + gate_shared * (1.0 - sigma))
    ).astype(BF16)
    grad_up_shared = (grad_hidden_shared * gate_shared * sigma).astype(BF16)
    shared_entry = contract(grad_gate_shared, shared_low[0], 1, 1) + contract(
        grad_up_shared, shared_low[1], 1, 1
    )
    block_out = (middle + shared_out + routed).astype(BF16)

    grad_logit = (probs * (grad_prob - jnp.sum(probs * grad_prob, axis=-1, keepdims=True))).astype(
        BF16
    )
    router_grad = contract(second, grad_logit, 0, 0)
    grad_second = grad_second + contract(grad_logit, router_low, 1, 1) + shared_entry
    shared_grad = jnp.stack(
        [
            contract(second, grad_gate_shared, 0, 0),
            contract(second, grad_up_shared, 0, 0),
            contract(grad_low, hidden_shared, 0, 0),
        ]
    )
    gain_two_grad = jnp.sum(grad_second * scaled_two, axis=0)
    grad_middle = norm_backward(grad_second, scaled_two, inverse_two, gain_two) + grad_out
    grad_attn_out = grad_middle.astype(BF16)
    out_grad = contract(mixed_low, grad_attn_out, 0, 0)
    projection_grad, grad_normed_all, grad_normed_own = attention_grad(
        place,
        normed_all,
        normed,
        projections,
        out_low,
        query,
        keys,
        values,
        mixed,
        after(grad_attn_out, routed_other),
        cosine_all,
        sine_all,
        starts,
    )
    gain_one_grad = jnp.sum(grad_normed_all * scaled_all, axis=0) + jnp.sum(
        grad_normed_own * scaled_one, axis=0
    )
    normed_low = grad_normed_all.astype(BF16).reshape(deep, token_rows, width)
    grad_normed = grad_normed_own + pick(
        grad_normed_all.reshape(deep, token_rows, width), level, 0
    )
    for step in range(1, deep):
        grad_normed = grad_normed + shift(pick(normed_low, (level - step) % deep, 0), -step).astype(
            F32
        )
    grad_inputs = norm_backward(grad_normed, scaled_one, inverse_one, gain_one) + grad_middle

    fill_rows = -(-(dense_rows * (specialist_total + 2)) // (8 * width)) * 8
    def by_owner(grad):
        return grad.reshape(grad.shape[0], deep, groups, dense_rows, grad.shape[-1]).transpose(
            1, 2, 0, 3, 4
        )

    small_grad = jnp.concatenate(
        [
            router_grad.reshape(deep, groups, dense_rows * specialist_total),
            jnp.stack([gain_one_grad, gain_two_grad])
            .reshape(2, deep, groups, dense_rows)
            .transpose(1, 2, 0, 3)
            .reshape(deep, groups, 2 * dense_rows),
        ],
        -1,
    )
    small_grad = jnp.pad(
        small_grad, ((0, 0), (0, 0), (0, fill_rows * width - small_grad.shape[-1]))
    ).reshape(deep, groups, fill_rows, width)
    projection_sums = scatter_dense(
        jnp.concatenate(
            [
                by_owner(projection_grad).reshape(deep, groups, 3 * dense_rows, width),
                small_grad,
            ],
            2,
        )
    )
    out_sum = scatter_dense(out_grad.reshape(deep, groups, dense_rows, width))
    shared_sum = scatter_dense(
        by_owner(shared_grad).reshape(deep, groups, 3 * dense_rows, hidden_width)
    ).reshape(3, dense_rows, hidden_width)
    attn_sum = jnp.concatenate(
        [projection_sums[: 3 * dense_rows].reshape(3, dense_rows, width), out_sum[None]], 0
    )
    small_sum = projection_sums[3 * dense_rows :].reshape(-1)
    router_sum = small_sum[: dense_rows * specialist_total].reshape(dense_rows, specialist_total)
    gain_sum = small_sum[
        dense_rows * specialist_total : dense_rows * (specialist_total + 2)
    ].reshape(2, dense_rows)

    local_squares = (
        jnp.sum(attn_sum * attn_sum)
        + jnp.sum(shared_sum * shared_sum)
        + jnp.sum(router_sum * router_sum)
        + jnp.sum(gain_sum * gain_sum)
        + jnp.sum(expert_sum * expert_sum)
    )
    spread = jnp.broadcast_to(local_squares, (everyone, 8, 128))
    squares = lax.all_to_all(spread, ("dp", "expert"), 0, 0, tiled=True)
    grad_norm = jnp.sqrt(jnp.sum(squares[:, 0, 0]))
    scale = jnp.minimum(1.0, CLIP_VALUE / (grad_norm + 1e-06))
    attn_new, attn_moment, attn_square = adam(
        mixer_projection_matrices,
        mixer_mean_estimate,
        mixer_variance_estimate,
        attn_sum,
        scale,
        RATE_MATRIX,
    )
    shared_new, shared_moment, shared_square = adam(
        common_projection_matrices,
        common_mean_estimate,
        common_variance_estimate,
        shared_sum,
        scale,
        RATE_MATRIX,
    )
    router_new, router_moment, router_square = adam(
        gating_projection_matrix,
        gating_mean_estimate,
        gating_variance_estimate,
        router_sum,
        scale,
        RATE_MATRIX,
    )
    gain_new, gain_moment, gain_square = adam(
        scaling_factors,
        scaling_mean_estimate,
        scaling_variance_estimate,
        gain_sum,
        scale,
        RATE_GAIN,
    )
    expert_new, expert_moment, expert_square = adam(
        dispatched_projection_matrices,
        dispatched_mean_estimate,
        dispatched_variance_estimate,
        expert_sum,
        scale,
        RATE_EXPERT,
    )
    return (
        block_out[None],
        grad_inputs[None],
        grad_norm,
        attn_new,
        attn_moment,
        attn_square,
        attn_new.astype(BF16),
        shared_new,
        shared_moment,
        shared_square,
        shared_new.astype(BF16),
        router_new,
        router_moment,
        router_square,
        router_new.astype(BF16),
        gain_new,
        gain_moment,
        gain_square,
        expert_new,
        expert_moment,
        expert_square,
        expert_new.astype(BF16),
    )


def solution(mesh):
    placed = (
        P("expert", "dp", None),
        P("expert", "dp", None),
        P("expert", None),
        P("expert", "dp", None),
        P(),
        P(),
        P(None, ("dp", "expert"), None),
        P(None, ("dp", "expert"), None),
        P(None, ("dp", "expert"), None),
        P(None, ("dp", "expert"), None),
        P(None, ("dp", "expert"), None),
        P(None, ("dp", "expert"), None),
        P(("dp", "expert"), None),
        P(("dp", "expert"), None),
        P(("dp", "expert"), None),
        P(None, ("dp", "expert")),
        P(None, ("dp", "expert")),
        P(None, ("dp", "expert")),
        P("expert", None, "dp", None),
        P("expert", None, "dp", None),
        P("expert", None, "dp", None),
    )
    return jax.shard_map(
        body,
        mesh=mesh,
        in_specs=placed,
        out_specs=(
            P("expert", "dp", None),
            P("expert", "dp", None),
            P(),
            P(None, ("dp", "expert"), None),
            P(None, ("dp", "expert"), None),
            P(None, ("dp", "expert"), None),
            P(None, ("dp", "expert"), None),
            P(None, ("dp", "expert"), None),
            P(None, ("dp", "expert"), None),
            P(None, ("dp", "expert"), None),
            P(None, ("dp", "expert"), None),
            P(("dp", "expert"), None),
            P(("dp", "expert"), None),
            P(("dp", "expert"), None),
            P(("dp", "expert"), None),
            P(None, ("dp", "expert")),
            P(None, ("dp", "expert")),
            P(None, ("dp", "expert")),
            P("expert", None, "dp", None),
            P("expert", None, "dp", None),
            P("expert", None, "dp", None),
            P("expert", None, "dp", None),
        ),
        check_vma=False,
    )
```

```python
import functools

import jax
import jax.numpy as jnp
from jax import lax
from jax.experimental import pallas as pl
from jax.experimental.pallas import tpu as pltpu
from jax.sharding import PartitionSpec as P

HEAD_DIM = 128
STEP = 10


NORM_EPS = 1e-06
THETA = 10000.0
CLIP_VALUE = 1.0
BETA_ONE = 0.9
BETA_TWO = 0.999
ADAM_EPS = 1e-08
DECAY = 0.1
RATE_MATRIX = 0.02
RATE_EXPERT = 0.1
RATE_GAIN = 0.3
MASKED = -1e30

F32 = jnp.float32
BF16 = jnp.bfloat16


def contract(left, right, left_dim, right_dim):
    return lax.dot_general(
        left, right, (((left_dim,), (right_dim,)), ((), ())), preferred_element_type=F32
    )


def rotary_tables(places, head_dim):
    half = head_dim // 2
    freq = THETA ** (-2.0 * jnp.arange(half, dtype=F32) / head_dim)
    angle = places.astype(F32)[:, None] * freq
    cosine, sine = jnp.cos(angle), jnp.sin(angle)
    return (jnp.concatenate([cosine, cosine], -1), jnp.concatenate([-sine, sine], -1))


def norm_forward(values, gain):
    inverse = lax.rsqrt(jnp.mean(values * values, axis=-1, keepdims=True) + NORM_EPS)
    scaled = values * inverse
    return ((scaled * gain).astype(BF16), scaled, inverse)


def norm_backward(grad, scaled, inverse, gain):
    local = grad * gain
    return inverse * (local - scaled * jnp.mean(local * scaled, axis=-1, keepdims=True))


def adam(master, first, second, grad, scale, rate):
    clipped = grad * scale
    first_new = BETA_ONE * first + (1.0 - BETA_ONE) * clipped
    second_new = BETA_TWO * second + (1.0 - BETA_TWO) * clipped * clipped
    first_hat = first_new / (1.0 - BETA_ONE**STEP)
    second_hat = second_new / (1.0 - BETA_TWO**STEP)
    master_new = master - rate * (first_hat / (jnp.sqrt(second_hat) + ADAM_EPS) + DECAY * master)
    return (master_new, first_new, second_new)


def after(value, *others):
    return lax.optimization_barrier((value,) + others)[0]


def hold_kernel(*_):
    pass


def hold(values, *others):
    anywhere = pl.BlockSpec(memory_space=pl.ANY)
    return pl.pallas_call(
        hold_kernel,
        in_specs=[anywhere] * (len(values) + len(others)),
        out_specs=[anywhere] * len(values),
        out_shape=[jax.ShapeDtypeStruct(value.shape, value.dtype) for value in values],
        input_output_aliases={index: index for index in range(len(values))},
        cost_estimate=LIGHT,
        name="hold",
    )(*values, *others)


def swap(value, mask):
    size = lax.axis_size("expert")
    return lax.ppermute(value, "expert", [(i, i ^ mask) for i in range(size)])


def rotate(value, step):
    size = lax.axis_size("dp")
    return lax.ppermute(value, "dp", [(i, (i + step) % size) for i in range(size)])


def shift(value, step):
    size = lax.axis_size("dp")
    return lax.ppermute(
        value, "dp", [(i, i + step) for i in range(size) if 0 <= i + step < size]
    )


def put(buffer, block, index, axis):
    return lax.dynamic_update_slice_in_dim(buffer, jnp.expand_dims(block, axis), index, axis)


def pick(buffer, index, axis):
    return lax.dynamic_index_in_dim(buffer, index, axis, keepdims=False)


def fan(block, *others):
    size = lax.axis_size("expert")
    block = after(block, *others) if others else block
    return [block] + [swap(block, mask) for mask in range(2, size, 2)]


def gather_swaps(block, *others):
    even = jnp.stack(fan(block, *others))
    return even, swap(even, 1)


def join_cores(even, other):
    return [even[k].astype(F32) + other[k].astype(F32) for k in range(even.shape[0])]


def spread_chips(summed):
    return [swap(summed[index].astype(BF16), 2 * index) for index in range(1, len(summed))]


def add_up(total, parts):
    for part in parts:
        total = total + part.astype(F32)
    return total


def join_chips(summed):
    return add_up(summed[0], spread_chips(summed))


def core_split(grad, rows):
    core = lax.axis_index("expert") % 2
    split = grad.reshape(grad.shape[0], -1, 2, rows, grad.shape[-1])
    return pick(split, core, 2), pick(split, 1 - core, 2)


def chip_sums(mine, received):
    chip = lax.axis_index("expert") // 2
    chips = lax.axis_size("expert") // 2
    shape = (mine.shape[0], -1, chips) + mine.shape[2:]
    mine, received = mine.reshape(shape), received.reshape(shape)
    return [
        pick(mine, chip ^ mask, 2).astype(F32) + pick(received, chip ^ mask, 2).astype(F32)
        for mask in range(chips)
    ]


def column_sum(total, axis):
    deep, level = lax.axis_size("dp"), lax.axis_index("dp")
    low = total.astype(BF16)
    result = pick(total, level, axis)
    arrived = low
    for step in range(1, deep):
        block = pick(low, (level + step) % deep, axis)
        if step == 2:
            block = hold([block], arrived)[0]
        arrived = rotate(block, step)
        result = result + arrived.astype(F32)
    return result


VMEM_LIMIT = 60 * 1024 * 1024
LIGHT = pl.CostEstimate(flops=1, bytes_accessed=1, transcendentals=0)


def product(left, right, left_dim, right_dim):
    return lax.dot_general(
        left, right, (((left_dim,), (right_dim,)), ((), ())), preferred_element_type=F32
    )


def kernel_params(steps):
    return pltpu.CompilerParams(
        dimension_semantics=("arbitrary",) * steps, vmem_limit_bytes=VMEM_LIMIT
    )


def whole(array):
    shape = array.shape
    return pl.BlockSpec(shape, lambda *_: (0,) * len(shape), pipeline_mode=pl.Buffered(1))


def assemble_kernel(place_ref, even, odd, out):
    core = place_ref[0] % 2
    out[:, :, pl.ds(core, 1)] = jnp.swapaxes(even[0], 0, 1)[:, :, None]
    out[:, :, pl.ds(1 - core, 1)] = jnp.swapaxes(odd[0], 0, 1)[:, :, None]


def assemble(even, odd):
    chips, deep, parts, rows, width = even.shape
    here = lax.axis_index("expert")
    chip = pl.BlockSpec(
        (1, deep, parts, rows, width), lambda c, p: (c ^ (p[0] // 2), 0, 0, 0, 0)
    )
    joined = pl.pallas_call(
        assemble_kernel,
        grid_spec=pltpu.PrefetchScalarGridSpec(
            num_scalar_prefetch=1,
            grid=(chips,),
            in_specs=[chip, chip],
            out_specs=pl.BlockSpec(
                (parts, deep, 2, rows, width), lambda c, p: (0, 0, c, 0, 0)
            ),
        ),
        out_shape=jax.ShapeDtypeStruct((parts, deep, 2 * chips, rows, width), even.dtype),
        compiler_params=kernel_params(1),
        cost_estimate=LIGHT,
        name="assemble",
    )(here[None], even, odd)
    return joined.reshape(parts, deep * 2 * chips * rows, width)


def turn_head(values, cosine, sine):
    return values * cosine + pltpu.roll(values, HEAD_DIM // 2, 1) * sine


def head_weights(query, keys, allowed):
    scores = product(query, keys, 1, 1) * HEAD_DIM ** (-0.5)
    scores = jnp.where(allowed, scores, MASKED)
    raised = jnp.exp(scores - jnp.max(scores, axis=-1, keepdims=True))
    return raised / jnp.sum(raised, axis=-1, keepdims=True)


def visible_keys(place, own_starts, starts):
    shape = (own_starts.shape[0], starts.shape[1])
    query_index = place + lax.broadcasted_iota(jnp.int32, shape, 0)
    key_index = lax.broadcasted_iota(jnp.int32, shape, 1)
    return (own_starts == starts) & (key_index <= query_index)


def attention_kernel(
    place_ref, normed, wq, wk, wv, cosine, sine, starts, own_starts, q_out, k_out, v_out, o_out, low_out
):
    rows = q_out.shape[0]
    place = pl.multiple_of(place_ref[0], rows)
    own = normed[pl.ds(place, rows), :]
    everything = normed[...]
    allowed = visible_keys(place, own_starts[...], starts[...])
    query = product(own, wq[0], 1, 0)
    keys = product(everything, wk[0], 1, 0)
    values = product(everything, wv[0], 1, 0).astype(BF16)
    v_out[...] = values
    own_cosine, own_sine = cosine[pl.ds(place, rows), :], sine[pl.ds(place, rows), :]
    for head in range(q_out.shape[1] // HEAD_DIM):
        lanes = slice(head * HEAD_DIM, (head + 1) * HEAD_DIM)
        turned_query = turn_head(query[:, lanes], own_cosine, own_sine).astype(BF16)
        turned_keys = turn_head(keys[:, lanes], cosine[...], sine[...]).astype(BF16)
        weights = head_weights(turned_query, turned_keys, allowed).astype(BF16)
        mixed = product(weights, values[:, lanes], 1, 0)
        q_out[:, lanes] = turned_query
        k_out[:, lanes] = turned_keys
        o_out[:, lanes] = mixed
        low_out[:, lanes] = mixed.astype(BF16)


def attention(place, normed, projections, cosine, sine, starts, rows):
    length, width = normed.shape
    span = 2 * HEAD_DIM
    own_starts = lax.dynamic_slice_in_dim(starts, place, rows)[:, None]
    starts = starts[None, :]
    column = lambda index: pl.BlockSpec((1, width, span), lambda p, _: (index, 0, p))
    blocks = lambda count: pl.BlockSpec((count, span), lambda p, _: (0, p))
    return pl.pallas_call(
        attention_kernel,
        grid_spec=pltpu.PrefetchScalarGridSpec(
            num_scalar_prefetch=1,
            grid=(width // span,),
            in_specs=[
                whole(normed),
                column(0),
                column(1),
                column(2),
                whole(cosine),
                whole(sine),
                whole(starts),
                whole(own_starts),
            ],
            out_specs=[blocks(rows), blocks(length), blocks(length), blocks(rows), blocks(rows)],
        ),
        out_shape=[
            jax.ShapeDtypeStruct((rows, width), BF16),
            jax.ShapeDtypeStruct((length, width), BF16),
            jax.ShapeDtypeStruct((length, width), BF16),
            jax.ShapeDtypeStruct((rows, width), F32),
            jax.ShapeDtypeStruct((rows, width), BF16),
        ],
        compiler_params=kernel_params(1),
        cost_estimate=LIGHT,
        name="attention_forward",
    )(place[None], normed, projections, projections, projections, cosine, sine, starts, own_starts)


def split_shapes(parts, rows_all, width, rows):
    if rows % 8 == 0:
        return [(parts, rows_all // (2 * rows), rows, width)] * 2
    return [(parts, rows_all, width)]


def store_split(grad, core, part, targets):
    if len(targets) == 1:
        targets[0][part] = grad.astype(BF16)
        return
    mine, other = targets
    count, rows = mine.shape[1], mine.shape[2]
    cut = grad.reshape(count, 2, rows, grad.shape[1])
    even, odd = cut[:, 0], cut[:, 1]
    mine[part] = jnp.where(core == 0, even, odd).astype(BF16)
    other[part] = jnp.where(core == 0, odd, even).astype(BF16)


def attention_grad_kernel(
    place_ref, turned_normed, own_turned, wo, q, k, v, o, arriving, cosine, sine, starts, own_starts, *refs
):
    *grads, dq_out, dk_out, dv_out = refs
    grads = grads[-2:] if len(grads[-1].shape) == 4 else grads[-1:]
    rows = q.shape[0]
    place = pl.multiple_of(place_ref[0], rows)
    allowed = visible_keys(place, own_starts[...], starts[...])
    own_cosine, own_sine = cosine[pl.ds(place, rows), :], sine[pl.ds(place, rows), :]
    mixed_grad = product(arriving[...], wo[...], 1, 1).astype(BF16)
    for head in range(q.shape[1] // HEAD_DIM):
        lanes = slice(head * HEAD_DIM, (head + 1) * HEAD_DIM)
        query, keys, values = q[:, lanes], k[:, lanes], v[:, lanes]
        incoming = mixed_grad[:, lanes]
        weights = head_weights(query, keys, allowed)
        correction = jnp.sum(incoming.astype(F32) * o[:, lanes], axis=-1, keepdims=True)
        weights_grad = product(incoming, values, 1, 1)
        scores_grad = (weights * (weights_grad - correction)).astype(BF16)
        factor = HEAD_DIM ** (-0.5)
        query_grad = product(scores_grad, keys, 1, 0) * factor
        keys_grad = product(scores_grad, query, 0, 0) * factor
        values_grad = product(weights.astype(BF16), incoming, 0, 0)
        dq_out[:, lanes] = turn_head(query_grad, own_cosine, -own_sine).astype(BF16)
        dk_out[:, lanes] = turn_head(keys_grad, cosine[...], -sine[...]).astype(BF16)
        dv_out[:, lanes] = values_grad.astype(BF16)
    core = place_ref[1]
    store_split(product(own_turned[...], dq_out[...], 1, 0), core, 0, grads)
    store_split(product(turned_normed[...], dk_out[...], 1, 0), core, 1, grads)
    store_split(product(turned_normed[...], dv_out[...], 1, 0), core, 2, grads)


def attention_grad(
    place, turned, own_turned, wo, q, k, v, o, arriving, cosine, sine, starts, dense_rows, first, count, waits=()
):
    width, length = turned.shape
    rows = q.shape[0]
    span = 2 * HEAD_DIM
    own_starts = lax.dynamic_slice_in_dim(starts, place, rows)[:, None]
    starts = starts[None, :]
    place = jnp.stack([place, lax.axis_index("expert") % 2])
    shapes = split_shapes(3, width, span * count, dense_rows)
    grad_specs = [
        pl.BlockSpec(shape[:-1] + (span,), lambda p, _, size=len(shape): (0,) * (size - 1) + (p,))
        for shape in shapes
    ]
    blocks = lambda size: pl.BlockSpec((size, span), lambda p, _: (0, p + first))
    column = lambda size: pl.BlockSpec((size, span), lambda p, _: (0, p))
    return pl.pallas_call(
        attention_grad_kernel,
        grid_spec=pltpu.PrefetchScalarGridSpec(
            num_scalar_prefetch=1,
            grid=(count,),
            in_specs=[
                whole(turned),
                whole(own_turned),
                pl.BlockSpec((span, width), lambda p, _: (p + first, 0)),
                blocks(rows),
                blocks(length),
                blocks(length),
                blocks(rows),
                whole(arriving),
                whole(cosine),
                whole(sine),
                whole(starts),
                whole(own_starts),
            ]
            + [pl.BlockSpec(memory_space=pl.ANY)] * len(waits),
            out_specs=[*grad_specs, column(rows), column(length), column(length)],
        ),
        out_shape=[
            *[jax.ShapeDtypeStruct(shape, BF16) for shape in shapes],
            jax.ShapeDtypeStruct((rows, span * count), BF16),
            jax.ShapeDtypeStruct((length, span * count), BF16),
            jax.ShapeDtypeStruct((length, span * count), BF16),
        ],
        compiler_params=kernel_params(1),
        cost_estimate=pl.CostEstimate(flops=32 * rows * length * width * count, bytes_accessed=1, transcendentals=0),
        name="attention_backward",
    )(
        place, turned, own_turned, wo, q, k, v, o, arriving, cosine, sine, starts, own_starts, *waits
    )


def normed_grad_kernel(parts, waits, *refs):
    level_ref, sequence, projections = refs[:3]
    grads = refs[3 : 3 + 3 * parts]
    low_out, own_out, gain_out = refs[3 + 3 * parts + waits :]
    step = pl.program_id(0)
    begin = 0
    total = None
    own = None
    for part in range(parts):
        dq, dk, dv = grads[3 * part : 3 * part + 3]
        lanes = slice(begin, begin + dk.shape[1])
        begin += dk.shape[1]
        term = product(dk[...], projections[1, :, lanes], 1, 1) + product(
            dv[...], projections[2, :, lanes], 1, 1
        )
        total = term if total is None else total + term
    low_out[0] = total.astype(BF16)
    values = sequence[...].astype(F32)
    scaled = values * lax.rsqrt(jnp.mean(values * values, axis=-1, keepdims=True) + NORM_EPS)

    @pl.when(step == 0)
    def _():
        gain_out[...] = jnp.zeros_like(gain_out)

    gain_out[...] += jnp.sum(total * scaled, axis=0, keepdims=True)

    @pl.when(step == level_ref[0])
    def _():
        begin = 0
        own = total
        for part in range(parts):
            dq = grads[3 * part]
            lanes = slice(begin, begin + dq.shape[1])
            begin += dq.shape[1]
            own = own + product(dq[...], projections[0, :, lanes], 1, 1)
        own_out[...] = own
        gain_out[...] += jnp.sum((own - total) * scaled, axis=0, keepdims=True)


def normed_grad(sequence, projections, grads, rows, waits):
    length, width = sequence.shape
    in_specs = [pl.BlockSpec((rows, width), lambda t, _: (t, 0)), whole(projections)]
    operands = [sequence, projections]
    for dq, dk, dv in grads:
        tile = pl.BlockSpec((rows, dk.shape[1]), lambda t, _: (t, 0))
        in_specs += [whole(dq), tile, tile]
        operands += [dq, dk, dv]
    return pl.pallas_call(
        functools.partial(normed_grad_kernel, len(grads), len(waits)),
        grid_spec=pltpu.PrefetchScalarGridSpec(
            num_scalar_prefetch=1,
            grid=(length // rows,),
            in_specs=in_specs + [pl.BlockSpec(memory_space=pl.ANY)] * len(waits),
            out_specs=[
                pl.BlockSpec((1, rows, width), lambda t, _: (t, 0, 0)),
                pl.BlockSpec((rows, width), lambda t, _: (0, 0)),
                pl.BlockSpec((1, width), lambda t, _: (0, 0)),
            ],
        ),
        out_shape=[
            jax.ShapeDtypeStruct((length // rows, rows, width), BF16),
            jax.ShapeDtypeStruct((rows, width), F32),
            jax.ShapeDtypeStruct((1, width), F32),
        ],
        compiler_params=kernel_params(1),
        cost_estimate=pl.CostEstimate(flops=24 * length * width * width, bytes_accessed=1, transcendentals=0),
        name="normed_grad",
    )(lax.axis_index("dp")[None], *operands, *waits)


def expert_kernel(has_before, split, part_rows, waits, *refs):
    odd_n, even_n, odd_c, even_c, gates, weights = refs[:6]
    refs = refs[6 + waits :]
    if has_before:
        routed_in, entry_in = refs[:2]
        refs = refs[2:]
    if split:
        routed_odd, routed_even, entry_odd, entry_even = refs[:4]
        refs = refs[4:]
    else:
        routed_out, entry_out = refs[:2]
        refs = refs[2:]
    gate_grad, hidden_out, pair_out, both, down, arrived = refs
    step = pl.program_id(0)
    half = pl.num_programs(0) // 2
    hidden_width = weights.shape[3]

    @pl.when(step == 0)
    def _():
        copies = []
        for level in range(weights.shape[0]):
            rows = pl.ds(level * part_rows, part_rows)
            for index in range(3):
                if index < 2:
                    target = both.at[rows, pl.ds(index * hidden_width, hidden_width)]
                else:
                    target = down.at[rows]
                copies.append(
                    pltpu.make_async_copy(
                        weights.at[level, index, pl.ds(0, part_rows)],
                        target,
                        arrived.at[level, index],
                    )
                )
        for copy in copies:
            copy.start()
        for copy in copies:
            copy.wait()

    first = step < half
    tokens = jnp.where(first, odd_n[0], even_n[0])
    incoming = jnp.where(first, odd_c[0], even_c[0]).astype(F32)
    gate = gates[...]
    parts = product(tokens, both[...], 1, 0)
    gate_part, up_part = parts[:, :hidden_width], parts[:, hidden_width:]
    sigma = 1.0 / (1.0 + jnp.exp(-gate_part))
    smooth = gate_part * sigma
    hidden = (smooth * up_part).astype(BF16)
    hidden_out[...] = hidden
    result = product(hidden, down[...], 1, 1).astype(BF16).astype(F32)
    gate_grad[...] = jnp.sum(incoming * result, axis=-1, keepdims=True)
    routed = gate * result
    grad_pair = (gate * incoming).astype(BF16)
    grad_hidden = product(grad_pair, down[...], 1, 0)
    grad_gate = (grad_hidden * up_part * sigma * (1.0 + gate_part * (1.0 - sigma))).astype(BF16)
    grad_up = (grad_hidden * smooth).astype(BF16)
    grad_parts = jnp.concatenate([grad_gate, grad_up], axis=1)
    pair_out[...] = grad_parts
    entry = product(grad_parts, both[...], 1, 1).astype(BF16).astype(F32)
    if has_before:
        routed = routed + routed_in[...]
        entry = entry + entry_in[...]
    if split:

        @pl.when(first)
        def _():
            routed_odd[0] = routed.astype(BF16)
            entry_odd[0] = entry.astype(BF16)

        @pl.when(jnp.logical_not(first))
        def _():
            routed_even[0] = routed.astype(BF16)
            entry_even[0] = entry.astype(BF16)
    else:
        routed_out[...] = routed
        entry_out[...] = entry


def expert_pass(tokens, grads, gates, weights, part_rows, before, split, waits=()):
    even_n, odd_n = tokens
    even_c, odd_c = grads
    count, rows, width = even_n.shape
    hidden_width = weights.shape[3]
    tiles = 2 * count
    total = tiles * rows
    odd = pl.BlockSpec((1, rows, width), lambda t: (jnp.minimum(t, count - 1), 0, 0))
    even = pl.BlockSpec((1, rows, width), lambda t: (jnp.maximum(t - count, 0), 0, 0))
    tile = lambda size: pl.BlockSpec((rows, size), lambda t: (t, 0))
    in_specs = [odd, even, odd, even, tile(1), pl.BlockSpec(memory_space=pl.ANY)]
    operands = [odd_n, even_n, odd_c, even_c, gates, weights, *waits]
    in_specs += [pl.BlockSpec(memory_space=pl.ANY)] * len(waits)
    if before is not None:
        in_specs += [tile(width), tile(width)]
        operands += list(before)
    if split:
        out_specs = [odd, even, odd, even]
        out_shape = [jax.ShapeDtypeStruct((count, rows, width), BF16)] * 4
    else:
        out_specs = [tile(width), tile(width)]
        out_shape = [jax.ShapeDtypeStruct((total, width), F32)] * 2
    out_specs += [tile(1), tile(hidden_width), tile(2 * hidden_width)]
    out_shape += [
        jax.ShapeDtypeStruct((total, 1), F32),
        jax.ShapeDtypeStruct((total, hidden_width), BF16),
        jax.ShapeDtypeStruct((total, 2 * hidden_width), BF16),
    ]
    return pl.pallas_call(
        functools.partial(expert_kernel, before is not None, split, part_rows, len(waits)),
        grid=(tiles,),
        in_specs=in_specs,
        out_specs=out_specs,
        out_shape=out_shape,
        scratch_shapes=[
            pltpu.VMEM((width, 2 * hidden_width), BF16),
            pltpu.VMEM((width, hidden_width), BF16),
            pltpu.SemaphoreType.DMA((weights.shape[0], 3)),
        ],
        compiler_params=kernel_params(1),
        cost_estimate=LIGHT,
        name="expert_pass",
    )(*operands)


def shared_kernel(place_ref, tokens_ref, incoming_ref, weights, result_out, entry_out, *targets):
    tokens, incoming = tokens_ref[...], incoming_ref[...]
    core = place_ref[0]
    gate_part = product(tokens, weights[0], 1, 0)
    up_part = product(tokens, weights[1], 1, 0)
    sigma = 1.0 / (1.0 + jnp.exp(-gate_part))
    smooth = gate_part * sigma
    hidden = (smooth * up_part).astype(BF16)
    result_out[...] = product(hidden, weights[2], 1, 1)
    grad_hidden = product(incoming, weights[2], 1, 0)
    grad_gate = (grad_hidden * up_part * sigma * (1.0 + gate_part * (1.0 - sigma))).astype(BF16)
    grad_up = (grad_hidden * smooth).astype(BF16)
    entry_out[...] = product(grad_gate, weights[0], 1, 1) + product(grad_up, weights[1], 1, 1)
    store_split(product(tokens, grad_gate, 0, 0), core, 0, targets)
    store_split(product(tokens, grad_up, 0, 0), core, 1, targets)
    store_split(product(incoming, hidden, 0, 0), core, 2, targets)


def shared_pass(tokens, incoming, weights, dense_rows):
    rows, width = tokens.shape
    hidden_width = weights.shape[2]
    shapes = split_shapes(3, width, hidden_width, dense_rows)
    out_shape = [jax.ShapeDtypeStruct((rows, width), F32)] * 2
    out_shape += [jax.ShapeDtypeStruct(shape, BF16) for shape in shapes]
    return pl.pallas_call(
        shared_kernel,
        grid_spec=pltpu.PrefetchScalarGridSpec(
            num_scalar_prefetch=1,
            grid=(1,),
            in_specs=[whole(tokens), whole(incoming), whole(weights)],
            out_specs=[whole(shape) for shape in out_shape],
        ),
        out_shape=out_shape,
        compiler_params=kernel_params(1),
        cost_estimate=LIGHT,
        name="shared_pass",
    )(lax.axis_index("expert")[None] % 2, tokens, incoming, weights)


def expert_grad_kernel(odd_n, even_n, odd_c, even_c, gates, hidden, pair, *refs):
    out = refs[-1]
    count, rows, span = odd_n.shape
    half = count * rows
    hidden_width = hidden.shape[1]
    tokens = jnp.concatenate(
        [odd_n[...].reshape(half, span), even_n[...].reshape(half, span)], axis=0
    )
    incoming = jnp.concatenate(
        [odd_c[...].reshape(half, span), even_c[...].reshape(half, span)], axis=0
    )
    grad_pair = (gates[...] * incoming.astype(F32)).astype(BF16)
    both = product(tokens, pair[...], 0, 0)
    out[0] = both[:, :hidden_width].astype(BF16)
    out[1] = both[:, hidden_width:].astype(BF16)
    out[2] = product(grad_pair, hidden[...], 0, 0).astype(BF16)


def expert_grad(tokens, grads, gates, hidden, pair, waits=()):
    even_n, odd_n = tokens
    even_c, odd_c = grads
    count, rows, width = even_n.shape
    hidden_width = hidden.shape[1]
    span = 256
    stack = pl.BlockSpec((count, rows, span), lambda t: (0, 0, t))
    return pl.pallas_call(
        expert_grad_kernel,
        grid=(width // span,),
        in_specs=[stack, stack, stack, stack, whole(gates), whole(hidden), whole(pair)]
        + [pl.BlockSpec(memory_space=pl.ANY)] * len(waits),
        out_specs=pl.BlockSpec((3, span, hidden_width), lambda t: (0, t, 0)),
        out_shape=jax.ShapeDtypeStruct((3, width, hidden_width), BF16),
        compiler_params=kernel_params(1),
        cost_estimate=LIGHT,
        name="expert_weight_grad",
    )(odd_n, even_n, odd_c, even_c, gates, hidden, pair, *waits)


def body(
    block_input_vectors,
    output_sensitivity,
    rotary_offsets,
    dispatched_specialist_ids,
    specialist_quotas,
    storage_holder,
    mixer_projection_matrices,
    mixer_mean_estimate,
    mixer_variance_estimate,
    common_projection_matrices,
    common_mean_estimate,
    common_variance_estimate,
    gating_projection_matrix,
    gating_mean_estimate,
    gating_variance_estimate,
    scaling_factors,
    scaling_mean_estimate,
    scaling_variance_estimate,
    dispatched_projection_matrices,
    dispatched_mean_estimate,
    dispatched_variance_estimate,
):
    token_rows = block_input_vectors.shape[1]
    width = block_input_vectors.shape[2]
    head_dim = HEAD_DIM
    heads = width // head_dim
    length = rotary_offsets.shape[1]
    specialist_total = specialist_quotas.shape[0]
    expert_local = dispatched_projection_matrices.shape[0]
    hidden_width = dispatched_projection_matrices.shape[3]
    part_rows = dispatched_projection_matrices.shape[2]
    dense_rows = mixer_projection_matrices.shape[1]
    groups = lax.axis_size("expert")
    deep = lax.axis_size("dp")
    here = lax.axis_index("expert")
    level = lax.axis_index("dp")
    scale_attn = head_dim ** (-0.5)
    straight = deep == 4

    attn_own = mixer_projection_matrices.astype(BF16)
    shared_own = common_projection_matrices.astype(BF16)
    router_own = gating_projection_matrix.astype(BF16)
    gain_own = scaling_factors.astype(BF16)
    expert_own = dispatched_projection_matrices.astype(BF16)

    everyone = deep * groups
    small = jnp.concatenate([router_own.reshape(-1), gain_own.reshape(-1)])
    small_size = small.shape[0]
    small_rows = -(-small_size // 1024) * 8
    small = jnp.pad(small, (0, small_rows * 128 - small_size)).reshape(small_rows, 128)
    small_all = lax.all_to_all(
        jnp.broadcast_to(small, (everyone, small_rows, 128)),
        ("dp", "expert"),
        0,
        0,
        tiled=True,
    ).reshape(everyone, small_rows * 128)
    router_size = dense_rows * specialist_total
    router_low = small_all[:, :router_size].reshape(width, specialist_total)
    gain_low = (
        small_all[:, router_size : router_size + 2 * dense_rows]
        .reshape(everyone, 2, dense_rows)
        .transpose(1, 0, 2)
        .reshape(2, width)
    )
    inputs_low = block_input_vectors[0]
    grad_low = output_sensitivity[0]
    grad_out = grad_low.astype(F32)
    attn_column = lax.all_gather(attn_own, "dp")
    projection_fan = fan(attn_column[:, :3])
    shared_size = shared_own.size
    shared_rows = -(-shared_size // (8 * width)) * 8
    shared_flat = jnp.pad(shared_own.reshape(-1), (0, shared_rows * width - shared_size))
    column = lax.all_gather(
        after(
            jnp.concatenate([inputs_low, shared_flat.reshape(shared_rows, width)], 0), attn_column
        ),
        "dp",
    )
    column, *projection_fan = lax.optimization_barrier((column, *projection_fan))
    sequence = column[:, :token_rows].reshape(length, width)
    shared_column = column[:, token_rows:].reshape(deep, -1)[:, :shared_size].reshape(
        deep, 3, dense_rows, hidden_width
    )
    expert_parts = [lax.all_gather(after(expert_own[0], sequence), "dp")]
    projection_even = jnp.stack(projection_fan)
    projection_odd = swap(projection_even, 1)
    out_even, out_odd = gather_swaps(attn_column[:, 3:], sequence)
    for number in range(1, expert_local):
        expert_parts.append(
            lax.all_gather(after(expert_own[number], projection_odd), "dp")
        )
    projections = assemble(projection_even, projection_odd)
    out_low = assemble(out_even, out_odd)[0]
    grads_fan = fan(hold([grad_low], projections)[0])
    gain_one = gain_low[0].astype(F32)
    gain_two = gain_low[1].astype(F32)

    sequence_low, sequence = sequence, sequence.astype(F32)

    normed_all, _, _ = norm_forward(sequence, gain_one)
    inputs = inputs_low.astype(F32)
    normed, scaled_one, inverse_one = norm_forward(inputs, gain_one)
    place = level * token_rows
    cosine_all, sine_all = rotary_tables(rotary_offsets[0], head_dim)
    starts = jnp.arange(length, dtype=jnp.int32) - rotary_offsets[0]
    query, keys, values, mixed, mixed_low = attention(
        place, normed_all, projections, cosine_all, sine_all, starts, token_rows
    )
    mixed_low = hold([mixed_low], *grads_fan[1:])[0]
    grads_even = jnp.stack(grads_fan)
    grads_plane = (grads_even, swap(grads_even, 1))
    middle = inputs + contract(mixed_low, out_low, 1, 0)
    second, scaled_two, inverse_two = norm_forward(middle, gain_two)

    probs = jax.nn.softmax(contract(second, router_low, 1, 0), axis=-1)
    experts = jnp.arange(specialist_total, dtype=jnp.int32)
    named = jnp.any(dispatched_specialist_ids[0][:, :, None] == experts, axis=1)
    order = jnp.arange(token_rows)
    earlier = contract(
        (order[:, None] > order[None, :]).astype(BF16), named.astype(BF16), 1, 0
    )
    kept = named & (earlier < specialist_quotas.astype(F32)[None, :])
    gate = jnp.where(kept, probs, 0.0)
    to_storage = (storage_holder[:, None] == experts[None, :]).astype(F32)
    gate_stored = jnp.sum(gate[:, :, None] * to_storage[None], axis=1)
    gates_sent = gate_stored.reshape(token_rows, groups, expert_local).transpose(1, 0, 2)
    gates_received = lax.all_to_all(gates_sent, "expert", 0, 0, tiled=True)
    half = jnp.arange(groups // 2) * 2
    relative = here ^ jnp.concatenate([half + 1, half])
    gates_plane = gates_received[relative].reshape(groups * token_rows, expert_local)

    tokens = gather_swaps(second)
    expert_parts[0] = after(expert_parts[0], tokens[1], grads_plane[1], gates_plane)

    shared_fan = fan(hold([shared_column], tokens[1], expert_parts[0])[0])

    def shared_step(shared_even, shared_odd):
        shared_low = assemble(shared_even, shared_odd)
        out, entry, *grad = shared_pass(second, grad_low, shared_low, dense_rows)
        if len(grad) == 1:
            grad = core_split(grad[0], dense_rows)
        return out, entry, chip_sums(grad[0], swap(grad[1], 1))

    def spread_after(sums, *others):
        lows = hold([part.astype(BF16) for part in sums[1:]], *others)
        return [swap(part, 2 * index + 2) for index, part in enumerate(lows)]

    mask = here ^ jnp.arange(groups)
    back = mask // 2 + jnp.where(mask % 2 == 1, 0, groups // 2)

    def return_gates(gate_grads):
        sent = jnp.concatenate(gate_grads, -1).reshape(groups, token_rows, expert_local)[back]
        return lax.all_to_all(sent, "expert", 0, 0, tiled=True)

    gate_grads = []
    expert_sums = []
    part_sums = []
    before = None
    turned, own_turned = normed_all.T, normed.T
    for number in range(expert_local):
        last = number == expert_local - 1
        gate_column = gates_plane[:, number : number + 1]
        parts = expert_pass(
            tokens, grads_plane, gate_column, expert_parts[number], part_rows, before, last,
            (turned, own_turned) if number == 1 else (),
        )
        before, (gate_grad, hidden, pair) = parts[:-3], parts[-3:]
        gate_grads.append(gate_grad)
        if number == 0:
            shared_even = hold([jnp.stack(shared_fan)], hidden)[0]
            shared_odd = swap(shared_even, 1)
        if last:
            routed_odd, routed_even, entry_odd, entry_even = before
            entry_odd = hold([entry_odd], *shared_parts)[0]
            entry_other = swap(entry_odd, 1)
            gate_grad_back = return_gates(gate_grads)
            entry_sums = join_cores(entry_even, entry_other)
            entry_parts = spread_chips(entry_sums)
            routed_other = swap(hold([routed_odd], entry_sums[1].astype(BF16))[0], 1)
        expert_part = expert_grad(
            tokens,
            grads_plane,
            gate_column,
            hidden,
            pair,
            [routed_other, gate_grad_back] if last else shared_fan[1:],
        )
        if number == 0:
            shared_odd = hold([shared_odd], expert_part)[0]
            shared_out, shared_entry, shared_sums = shared_step(shared_even, shared_odd)
            shared_parts = spread_after(shared_sums, *expert_parts[1:2])
        expert_part = expert_part.reshape(3, deep, part_rows, hidden_width)
        if last:
            shared_total = add_up(shared_sums[0], shared_parts)
            extra = -(part_rows + dense_rows) % 16
            shared_total = jnp.pad(shared_total.astype(BF16), ((0, 0), (0, 0), (0, extra), (0, 0)))
            expert_part = jnp.concatenate([expert_part, shared_total], 2)
        part_sum = lax.psum_scatter(
            expert_part.reshape(3, -1, hidden_width), "dp", scatter_dimension=1, tiled=True
        )
        part_sums.append(part_sum)
        expert_sums.append(part_sum[:, :part_rows].astype(F32))
    shared_sum = part_sum[:, part_rows : part_rows + dense_rows].astype(F32)
    expert_sum = jnp.stack(expert_sums)

    entry_parts = hold(entry_parts, expert_part)
    grad_second = add_up(entry_sums[0], entry_parts)
    routed_sums = join_cores(routed_even, routed_other)
    gate_grad_stored = gate_grad_back.transpose(1, 0, 2).reshape(token_rows, specialist_total)
    grad_prob = jnp.sum(gate_grad_stored[:, None, :] * to_storage[None], axis=-1)
    grad_prob = jnp.where(kept, grad_prob, 0.0)


    grad_logit = (probs * (grad_prob - jnp.sum(probs * grad_prob, axis=-1, keepdims=True))).astype(
        BF16
    )
    router_grad = contract(second, grad_logit, 0, 0)
    grad_second = grad_second + contract(grad_logit, router_low, 1, 1) + shared_entry
    gain_two_grad = jnp.sum(grad_second * scaled_two, axis=0)
    grad_middle = norm_backward(grad_second, scaled_two, inverse_two, gain_two) + grad_out
    grad_attn_out = grad_middle.astype(BF16)
    out_grad = contract(mixed_low, grad_attn_out, 0, 0).astype(BF16)
    out_mine, out_other = core_split(out_grad[None], dense_rows)
    out_received = swap(out_other, 1)

    def grad_part(first, count, waits=()):
        *grads, dq, dk, dv = attention_grad(
            place,
            turned,
            own_turned,
            out_low,
            query,
            keys,
            values,
            mixed,
            grad_attn_out,
            cosine_all,
            sine_all,
            starts,
            dense_rows,
            first,
            count,
            waits,
        )
        if len(grads) == 1:
            grads = core_split(grads[0], dense_rows)
        return grads[0], grads[1], (dq, dk, dv)

    pairs = width // (2 * head_dim)
    early = (pairs + 1) // 2
    first_mine, first_other, first_terms = grad_part(0, early)
    last_mine, last_other, last_terms = grad_part(
        early, pairs - early, [first_other, part_sums[0]]
    )
    cut = first_mine.shape[-1]
    first_sums = chip_sums(
        jnp.concatenate([first_mine, out_mine[..., :cut]], 0),
        jnp.concatenate([swap(first_other, 1), out_received[..., :cut]], 0),
    )
    first_parts = spread_chips(first_sums)
    last_sums = chip_sums(
        jnp.concatenate([last_mine, out_mine[..., cut:]], 0),
        jnp.concatenate([swap(last_other, 1), out_received[..., cut:]], 0),
    )
    last_parts = spread_after(last_sums, *first_parts)
    routed_parts = spread_after(routed_sums, *last_parts)
    normed_low, grad_normed, gain_one_grad = normed_grad(
        sequence_low,
        projections,
        (first_terms, last_terms),
        token_rows,
        [first_sums[1].astype(BF16)],
    )
    gain_one_grad = gain_one_grad[0]
    small_grad = jnp.concatenate(
        [
            router_grad.reshape(everyone, router_size),
            jnp.stack([gain_one_grad, gain_two_grad])
            .reshape(2, everyone, dense_rows)
            .transpose(1, 0, 2)
            .reshape(everyone, 2 * dense_rows),
        ],
        -1,
    )
    small_grad = jnp.pad(small_grad, ((0, 0), (0, small_rows * 128 - small_size)))
    small_received = lax.all_to_all(
        small_grad.reshape(everyone, small_rows, 128), ("dp", "expert"), 0, 0, tiled=True
    )
    small_sum = jnp.sum(hold([small_received], *last_parts)[0], axis=0).reshape(-1)
    first_total = add_up(first_sums[0], hold(first_parts, grad_normed))
    last_total = add_up(last_sums[0], last_parts)
    first_sum = column_sum(first_total, 1)
    last_sum = column_sum(last_total, 1)
    grad_normed = grad_normed - pick(normed_low, level, 0).astype(F32)
    arrived = lax.psum_scatter(
        hold([normed_low.reshape(length, width)], part_sums[-1])[0],
        "dp",
        scatter_dimension=0,
        tiled=True,
    )
    grad_normed = grad_normed + arrived.astype(F32)
    grad_inputs = norm_backward(grad_normed, scaled_one, inverse_one, gain_one) + grad_middle
    attn_sum = jnp.concatenate([first_sum, last_sum], -1)
    router_sum = small_sum[:router_size].reshape(dense_rows, specialist_total)
    gain_sum = small_sum[router_size:small_size].reshape(2, dense_rows)

    local_squares = (
        jnp.sum(attn_sum * attn_sum)
        + jnp.sum(shared_sum * shared_sum)
        + jnp.sum(router_sum * router_sum)
        + jnp.sum(gain_sum * gain_sum)
        + jnp.sum(expert_sum * expert_sum)
    )
    spread = jnp.broadcast_to(local_squares, (everyone, 8, 128))
    squares = lax.all_to_all(spread, ("dp", "expert"), 0, 0, tiled=True)
    grad_norm = jnp.sqrt(jnp.sum(squares[:, 0, 0]))
    routed = add_up(routed_sums[0], hold(routed_parts, squares))
    block_out = (middle + shared_out + routed).astype(BF16)
    scale = jnp.minimum(1.0, CLIP_VALUE / (grad_norm + 1e-06))
    attn_new, attn_moment, attn_square = adam(
        mixer_projection_matrices,
        mixer_mean_estimate,
        mixer_variance_estimate,
        attn_sum,
        scale,
        RATE_MATRIX,
    )
    shared_new, shared_moment, shared_square = adam(
        common_projection_matrices,
        common_mean_estimate,
        common_variance_estimate,
        shared_sum,
        scale,
        RATE_MATRIX,
    )
    router_new, router_moment, router_square = adam(
        gating_projection_matrix,
        gating_mean_estimate,
        gating_variance_estimate,
        router_sum,
        scale,
        RATE_MATRIX,
    )
    gain_new, gain_moment, gain_square = adam(
        scaling_factors,
        scaling_mean_estimate,
        scaling_variance_estimate,
        gain_sum,
        scale,
        RATE_GAIN,
    )
    expert_new, expert_moment, expert_square = adam(
        dispatched_projection_matrices,
        dispatched_mean_estimate,
        dispatched_variance_estimate,
        expert_sum,
        scale,
        RATE_EXPERT,
    )
    return (
        block_out[None],
        grad_inputs[None],
        grad_norm,
        attn_new,
        attn_moment,
        attn_square,
        attn_new.astype(BF16),
        shared_new,
        shared_moment,
        shared_square,
        shared_new.astype(BF16),
        router_new,
        router_moment,
        router_square,
        router_new.astype(BF16),
        gain_new,
        gain_moment,
        gain_square,
        expert_new,
        expert_moment,
        expert_square,
        expert_new.astype(BF16),
    )


def solution(mesh):
    placed = (
        P("expert", "dp", None),
        P("expert", "dp", None),
        P("expert", None),
        P("expert", "dp", None),
        P(),
        P(),
        P(None, ("dp", "expert"), None),
        P(None, ("dp", "expert"), None),
        P(None, ("dp", "expert"), None),
        P(None, ("dp", "expert"), None),
        P(None, ("dp", "expert"), None),
        P(None, ("dp", "expert"), None),
        P(("dp", "expert"), None),
        P(("dp", "expert"), None),
        P(("dp", "expert"), None),
        P(None, ("dp", "expert")),
        P(None, ("dp", "expert")),
        P(None, ("dp", "expert")),
        P("expert", None, "dp", None),
        P("expert", None, "dp", None),
        P("expert", None, "dp", None),
    )
    return jax.shard_map(
        body,
        mesh=mesh,
        in_specs=placed,
        out_specs=(
            P("expert", "dp", None),
            P("expert", "dp", None),
            P(),
            P(None, ("dp", "expert"), None),
            P(None, ("dp", "expert"), None),
            P(None, ("dp", "expert"), None),
            P(None, ("dp", "expert"), None),
            P(None, ("dp", "expert"), None),
            P(None, ("dp", "expert"), None),
            P(None, ("dp", "expert"), None),
            P(None, ("dp", "expert"), None),
            P(("dp", "expert"), None),
            P(("dp", "expert"), None),
            P(("dp", "expert"), None),
            P(("dp", "expert"), None),
            P(None, ("dp", "expert")),
            P(None, ("dp", "expert")),
            P(None, ("dp", "expert")),
            P("expert", None, "dp", None),
            P("expert", None, "dp", None),
            P("expert", None, "dp", None),
            P("expert", None, "dp", None),
        ),
        check_vma=False,
    )
```

```python
import functools

import jax
import jax.numpy as jnp
from jax import lax
from jax.experimental import pallas as pl
from jax.experimental.pallas import tpu as pltpu
from jax.sharding import PartitionSpec as P

HEAD_DIM = 128
STEP = 10


NORM_EPS = 1e-06
THETA = 10000.0
CLIP_VALUE = 1.0
BETA_ONE = 0.9
BETA_TWO = 0.999
ADAM_EPS = 1e-08
DECAY = 0.1
RATE_MATRIX = 0.02
RATE_EXPERT = 0.1
RATE_GAIN = 0.3
MASKED = -1e30

F32 = jnp.float32
BF16 = jnp.bfloat16


def contract(left, right, left_dim, right_dim):
    return lax.dot_general(
        left, right, (((left_dim,), (right_dim,)), ((), ())), preferred_element_type=F32
    )


def rotary_tables(places, head_dim):
    half = head_dim // 2
    freq = THETA ** (-2.0 * jnp.arange(half, dtype=F32) / head_dim)
    angle = places.astype(F32)[:, None] * freq
    cosine, sine = jnp.cos(angle), jnp.sin(angle)
    return (jnp.concatenate([cosine, cosine], -1), jnp.concatenate([-sine, sine], -1))


def norm_forward(values, gain):
    inverse = lax.rsqrt(jnp.mean(values * values, axis=-1, keepdims=True) + NORM_EPS)
    scaled = values * inverse
    return ((scaled * gain).astype(BF16), scaled, inverse)


def norm_backward(grad, scaled, inverse, gain):
    local = grad * gain
    return inverse * (local - scaled * jnp.mean(local * scaled, axis=-1, keepdims=True))


def adam(master, first, second, grad, scale, rate):
    clipped = grad * scale
    first_new = BETA_ONE * first + (1.0 - BETA_ONE) * clipped
    second_new = BETA_TWO * second + (1.0 - BETA_TWO) * clipped * clipped
    first_hat = first_new / (1.0 - BETA_ONE**STEP)
    second_hat = second_new / (1.0 - BETA_TWO**STEP)
    master_new = master - rate * (first_hat / (jnp.sqrt(second_hat) + ADAM_EPS) + DECAY * master)
    return (master_new, first_new, second_new)


def after(value, *others):
    return lax.optimization_barrier((value,) + others)[0]


def hold_kernel(*_):
    pass


def hold(values, *others):
    anywhere = pl.BlockSpec(memory_space=pl.ANY)
    return pl.pallas_call(
        hold_kernel,
        in_specs=[anywhere] * (len(values) + len(others)),
        out_specs=[anywhere] * len(values),
        out_shape=[jax.ShapeDtypeStruct(value.shape, value.dtype) for value in values],
        input_output_aliases={index: index for index in range(len(values))},
        cost_estimate=LIGHT,
        name="hold",
    )(*values, *others)


def swap(value, mask):
    size = lax.axis_size("expert")
    return lax.ppermute(value, "expert", [(i, i ^ mask) for i in range(size)])


def rotate(value, step):
    size = lax.axis_size("dp")
    return lax.ppermute(value, "dp", [(i, (i + step) % size) for i in range(size)])


def shift(value, step):
    size = lax.axis_size("dp")
    return lax.ppermute(
        value, "dp", [(i, i + step) for i in range(size) if 0 <= i + step < size]
    )


def put(buffer, block, index, axis):
    return lax.dynamic_update_slice_in_dim(buffer, jnp.expand_dims(block, axis), index, axis)


def pick(buffer, index, axis):
    return lax.dynamic_index_in_dim(buffer, index, axis, keepdims=False)


def fan(block, *others):
    size = lax.axis_size("expert")
    block = after(block, *others) if others else block
    return [block] + [swap(block, mask) for mask in range(2, size, 2)]


def gather_swaps(block, *others):
    even = jnp.stack(fan(block, *others))
    return even, swap(even, 1)


def join_cores(even, other):
    return [even[k].astype(F32) + other[k].astype(F32) for k in range(even.shape[0])]


def spread_chips(summed):
    return [swap(summed[index].astype(BF16), 2 * index) for index in range(1, len(summed))]


def add_up(total, parts):
    for part in parts:
        total = total + part.astype(F32)
    return total


def join_chips(summed):
    return add_up(summed[0], spread_chips(summed))


def core_split(grad, rows):
    core = lax.axis_index("expert") % 2
    split = grad.reshape(grad.shape[0], -1, 2, rows, grad.shape[-1])
    return pick(split, core, 2), pick(split, 1 - core, 2)


def chip_sums(mine, received):
    chip = lax.axis_index("expert") // 2
    chips = lax.axis_size("expert") // 2
    shape = (mine.shape[0], -1, chips) + mine.shape[2:]
    mine, received = mine.reshape(shape), received.reshape(shape)
    return [
        pick(mine, chip ^ mask, 2).astype(F32) + pick(received, chip ^ mask, 2).astype(F32)
        for mask in range(chips)
    ]


def column_sum(total, axis, later, *others):
    deep, level = lax.axis_size("dp"), lax.axis_index("dp")
    low = total.astype(BF16)
    result = pick(total, level, axis)
    parts = []
    for step in range(1, deep):
        block = pick(low, (level + step) % deep, axis)
        if later is not None and step == 2:
            block = hold([block], later)[0]
        parts.append(rotate(block, step))
    if others:
        parts = hold(parts, *others)
    return add_up(result, parts), parts


VMEM_LIMIT = 60 * 1024 * 1024
LIGHT = pl.CostEstimate(flops=1, bytes_accessed=1, transcendentals=0)


def product(left, right, left_dim, right_dim):
    return lax.dot_general(
        left, right, (((left_dim,), (right_dim,)), ((), ())), preferred_element_type=F32
    )


def kernel_params(steps):
    return pltpu.CompilerParams(
        dimension_semantics=("arbitrary",) * steps, vmem_limit_bytes=VMEM_LIMIT
    )


def whole(array):
    shape = array.shape
    return pl.BlockSpec(shape, lambda *_: (0,) * len(shape), pipeline_mode=pl.Buffered(1))


def assemble_kernel(place_ref, even, odd, out):
    core = place_ref[0] % 2
    out[:, :, pl.ds(core, 1)] = jnp.swapaxes(even[0], 0, 1)[:, :, None]
    out[:, :, pl.ds(1 - core, 1)] = jnp.swapaxes(odd[0], 0, 1)[:, :, None]


def assemble(even, odd):
    chips, deep, parts, rows, width = even.shape
    here = lax.axis_index("expert")
    chip = pl.BlockSpec(
        (1, deep, parts, rows, width), lambda c, p: (c ^ (p[0] // 2), 0, 0, 0, 0)
    )
    joined = pl.pallas_call(
        assemble_kernel,
        grid_spec=pltpu.PrefetchScalarGridSpec(
            num_scalar_prefetch=1,
            grid=(chips,),
            in_specs=[chip, chip],
            out_specs=pl.BlockSpec(
                (parts, deep, 2, rows, width), lambda c, p: (0, 0, c, 0, 0)
            ),
        ),
        out_shape=jax.ShapeDtypeStruct((parts, deep, 2 * chips, rows, width), even.dtype),
        compiler_params=kernel_params(1),
        cost_estimate=LIGHT,
        name="assemble",
    )(here[None], even, odd)
    return joined.reshape(parts, deep * 2 * chips * rows, width)


def turn_head(values, cosine, sine):
    return values * cosine + pltpu.roll(values, HEAD_DIM // 2, 1) * sine


def head_weights(query, keys, allowed):
    scores = product(query, keys, 1, 1) * HEAD_DIM ** (-0.5)
    scores = jnp.where(allowed, scores, MASKED)
    raised = jnp.exp(scores - jnp.max(scores, axis=-1, keepdims=True))
    return raised / jnp.sum(raised, axis=-1, keepdims=True)


def visible_keys(place, own_starts, starts):
    shape = (own_starts.shape[0], starts.shape[1])
    query_index = place + lax.broadcasted_iota(jnp.int32, shape, 0)
    key_index = lax.broadcasted_iota(jnp.int32, shape, 1)
    return (own_starts == starts) & (key_index <= query_index)


def attention_kernel(
    place_ref, normed, wq, wk, wv, cosine, sine, starts, own_starts, q_out, k_out, v_out, o_out, low_out
):
    rows = q_out.shape[0]
    place = pl.multiple_of(place_ref[0], rows)
    own = normed[pl.ds(place, rows), :]
    everything = normed[...]
    allowed = visible_keys(place, own_starts[...], starts[...])
    query = product(own, wq[0], 1, 0)
    keys = product(everything, wk[0], 1, 0)
    values = product(everything, wv[0], 1, 0).astype(BF16)
    v_out[...] = values
    own_cosine, own_sine = cosine[pl.ds(place, rows), :], sine[pl.ds(place, rows), :]
    for head in range(q_out.shape[1] // HEAD_DIM):
        lanes = slice(head * HEAD_DIM, (head + 1) * HEAD_DIM)
        turned_query = turn_head(query[:, lanes], own_cosine, own_sine).astype(BF16)
        turned_keys = turn_head(keys[:, lanes], cosine[...], sine[...]).astype(BF16)
        weights = head_weights(turned_query, turned_keys, allowed).astype(BF16)
        mixed = product(weights, values[:, lanes], 1, 0)
        q_out[:, lanes] = turned_query
        k_out[:, lanes] = turned_keys
        o_out[:, lanes] = mixed
        low_out[:, lanes] = mixed.astype(BF16)


def attention(place, normed, projections, cosine, sine, starts, rows):
    length, width = normed.shape
    span = 2 * HEAD_DIM
    own_starts = lax.dynamic_slice_in_dim(starts, place, rows)[:, None]
    starts = starts[None, :]
    column = lambda index: pl.BlockSpec((1, width, span), lambda p, _: (index, 0, p))
    blocks = lambda count: pl.BlockSpec((count, span), lambda p, _: (0, p))
    return pl.pallas_call(
        attention_kernel,
        grid_spec=pltpu.PrefetchScalarGridSpec(
            num_scalar_prefetch=1,
            grid=(width // span,),
            in_specs=[
                whole(normed),
                column(0),
                column(1),
                column(2),
                whole(cosine),
                whole(sine),
                whole(starts),
                whole(own_starts),
            ],
            out_specs=[blocks(rows), blocks(length), blocks(length), blocks(rows), blocks(rows)],
        ),
        out_shape=[
            jax.ShapeDtypeStruct((rows, width), BF16),
            jax.ShapeDtypeStruct((length, width), BF16),
            jax.ShapeDtypeStruct((length, width), BF16),
            jax.ShapeDtypeStruct((rows, width), F32),
            jax.ShapeDtypeStruct((rows, width), BF16),
        ],
        compiler_params=kernel_params(1),
        cost_estimate=LIGHT,
        name="attention_forward",
    )(place[None], normed, projections, projections, projections, cosine, sine, starts, own_starts)


def split_shapes(parts, rows_all, width, rows):
    if rows % 8 == 0:
        return [(parts, rows_all // (2 * rows), rows, width)] * 2
    return [(parts, rows_all, width)]


def store_split(grad, core, part, targets):
    if len(targets) == 1:
        targets[0][part] = grad.astype(BF16)
        return
    mine, other = targets
    count, rows = mine.shape[1], mine.shape[2]
    cut = grad.reshape(count, 2, rows, grad.shape[1])
    even, odd = cut[:, 0], cut[:, 1]
    mine[part] = jnp.where(core == 0, even, odd).astype(BF16)
    other[part] = jnp.where(core == 0, odd, even).astype(BF16)


def attention_grad_kernel(
    place_ref, turned_normed, own_turned, mixed_turned, wo, q, k, v, o, arriving, arriving_columns,
    cosine, sine, starts, own_starts, *refs
):
    *grads, dq_out, dk_out, dv_out = refs
    grads = grads[-2:] if len(grads[-1].shape) == 4 else grads[-1:]
    rows = q.shape[0]
    place = pl.multiple_of(place_ref[0], rows)
    allowed = visible_keys(place, own_starts[...], starts[...])
    own_cosine, own_sine = cosine[pl.ds(place, rows), :], sine[pl.ds(place, rows), :]
    mixed_grad = product(arriving[...], wo[...], 1, 1).astype(BF16)
    for head in range(q.shape[1] // HEAD_DIM):
        lanes = slice(head * HEAD_DIM, (head + 1) * HEAD_DIM)
        query, keys, values = q[:, lanes], k[:, lanes], v[:, lanes]
        incoming = mixed_grad[:, lanes]
        weights = head_weights(query, keys, allowed)
        correction = jnp.sum(incoming.astype(F32) * o[:, lanes], axis=-1, keepdims=True)
        weights_grad = product(incoming, values, 1, 1)
        scores_grad = (weights * (weights_grad - correction)).astype(BF16)
        factor = HEAD_DIM ** (-0.5)
        query_grad = product(scores_grad, keys, 1, 0) * factor
        keys_grad = product(scores_grad, query, 0, 0) * factor
        values_grad = product(weights.astype(BF16), incoming, 0, 0)
        dq_out[:, lanes] = turn_head(query_grad, own_cosine, -own_sine).astype(BF16)
        dk_out[:, lanes] = turn_head(keys_grad, cosine[...], -sine[...]).astype(BF16)
        dv_out[:, lanes] = values_grad.astype(BF16)
    core = place_ref[1]
    store_split(product(own_turned[...], dq_out[...], 1, 0), core, 0, grads)
    store_split(product(turned_normed[...], dk_out[...], 1, 0), core, 1, grads)
    store_split(product(turned_normed[...], dv_out[...], 1, 0), core, 2, grads)
    store_split(product(mixed_turned[...], arriving_columns[...], 1, 0), core, 3, grads)


def attention_grad(
    place, turned, own_turned, mixed_turned, wo, q, k, v, o, arriving, cosine, sine, starts, dense_rows,
    first, count, waits=(),
):
    width, length = turned.shape
    rows = q.shape[0]
    span = 2 * HEAD_DIM
    own_starts = lax.dynamic_slice_in_dim(starts, place, rows)[:, None]
    starts = starts[None, :]
    place = jnp.stack([place, lax.axis_index("expert") % 2])
    shapes = split_shapes(4, width, span * count, dense_rows)
    grad_specs = [
        pl.BlockSpec(shape[:-1] + (span,), lambda p, _, size=len(shape): (0,) * (size - 1) + (p,))
        for shape in shapes
    ]
    blocks = lambda size: pl.BlockSpec((size, span), lambda p, _: (0, p + first))
    column = lambda size: pl.BlockSpec((size, span), lambda p, _: (0, p))
    return pl.pallas_call(
        attention_grad_kernel,
        grid_spec=pltpu.PrefetchScalarGridSpec(
            num_scalar_prefetch=1,
            grid=(count,),
            in_specs=[
                whole(turned),
                whole(own_turned),
                whole(mixed_turned),
                pl.BlockSpec((span, width), lambda p, _: (p + first, 0)),
                blocks(rows),
                blocks(length),
                blocks(length),
                blocks(rows),
                whole(arriving),
                blocks(rows),
                whole(cosine),
                whole(sine),
                whole(starts),
                whole(own_starts),
            ]
            + [pl.BlockSpec(memory_space=pl.ANY)] * len(waits),
            out_specs=[*grad_specs, column(rows), column(length), column(length)],
        ),
        out_shape=[
            *[jax.ShapeDtypeStruct(shape, BF16) for shape in shapes],
            jax.ShapeDtypeStruct((rows, span * count), BF16),
            jax.ShapeDtypeStruct((length, span * count), BF16),
            jax.ShapeDtypeStruct((length, span * count), BF16),
        ],
        compiler_params=kernel_params(1),
        cost_estimate=pl.CostEstimate(flops=64 * rows * length * width * count, bytes_accessed=1, transcendentals=0),
        name="attention_backward",
    )(
        place, turned, own_turned, mixed_turned, wo, q, k, v, o, arriving, arriving, cosine, sine, starts,
        own_starts, *waits
    )


def normed_grad_kernel(parts, waits, *refs):
    level_ref, sequence, projections = refs[:3]
    grads = refs[3 : 3 + 3 * parts]
    low_out, own_out, gain_out = refs[3 + 3 * parts + waits :]
    step = pl.program_id(0)
    begin = 0
    total = None
    own = None
    for part in range(parts):
        dq, dk, dv = grads[3 * part : 3 * part + 3]
        lanes = slice(begin, begin + dk.shape[1])
        begin += dk.shape[1]
        term = product(dk[...], projections[1, :, lanes], 1, 1) + product(
            dv[...], projections[2, :, lanes], 1, 1
        )
        total = term if total is None else total + term
    low_out[0] = total.astype(BF16)
    values = sequence[...].astype(F32)
    scaled = values * lax.rsqrt(jnp.mean(values * values, axis=-1, keepdims=True) + NORM_EPS)

    @pl.when(step == 0)
    def _():
        gain_out[...] = jnp.zeros_like(gain_out)

    gain_out[...] += jnp.sum(total * scaled, axis=0, keepdims=True)

    @pl.when(step == level_ref[0])
    def _():
        begin = 0
        own = total
        for part in range(parts):
            dq = grads[3 * part]
            lanes = slice(begin, begin + dq.shape[1])
            begin += dq.shape[1]
            own = own + product(dq[...], projections[0, :, lanes], 1, 1)
        own_out[...] = own
        gain_out[...] += jnp.sum((own - total) * scaled, axis=0, keepdims=True)


def normed_grad(sequence, projections, grads, rows, waits):
    length, width = sequence.shape
    in_specs = [pl.BlockSpec((rows, width), lambda t, _: (t, 0)), whole(projections)]
    operands = [sequence, projections]
    for dq, dk, dv in grads:
        tile = pl.BlockSpec((rows, dk.shape[1]), lambda t, _: (t, 0))
        in_specs += [whole(dq), tile, tile]
        operands += [dq, dk, dv]
    return pl.pallas_call(
        functools.partial(normed_grad_kernel, len(grads), len(waits)),
        grid_spec=pltpu.PrefetchScalarGridSpec(
            num_scalar_prefetch=1,
            grid=(length // rows,),
            in_specs=in_specs + [pl.BlockSpec(memory_space=pl.ANY)] * len(waits),
            out_specs=[
                pl.BlockSpec((1, rows, width), lambda t, _: (t, 0, 0)),
                pl.BlockSpec((rows, width), lambda t, _: (0, 0)),
                pl.BlockSpec((1, width), lambda t, _: (0, 0)),
            ],
        ),
        out_shape=[
            jax.ShapeDtypeStruct((length // rows, rows, width), BF16),
            jax.ShapeDtypeStruct((rows, width), F32),
            jax.ShapeDtypeStruct((1, width), F32),
        ],
        compiler_params=kernel_params(1),
        cost_estimate=pl.CostEstimate(flops=48 * length * width * width, bytes_accessed=1, transcendentals=0),
        name="normed_grad",
    )(lax.axis_index("dp")[None], *operands, *waits)


def expert_kernel(has_before, split, part_rows, waits, *refs):
    odd_n, even_n, odd_c, even_c, gates, weights = refs[:6]
    refs = refs[6 + waits :]
    if has_before:
        routed_in, entry_in = refs[:2]
        refs = refs[2:]
    if split:
        routed_odd, routed_even, entry_odd, entry_even = refs[:4]
        refs = refs[4:]
    else:
        routed_out, entry_out = refs[:2]
        refs = refs[2:]
    gate_grad, hidden_out, pair_out, both, down, arrived = refs
    step = pl.program_id(0)
    half = pl.num_programs(0) // 2
    hidden_width = weights.shape[3]

    @pl.when(step == 0)
    def _():
        copies = []
        for level in range(weights.shape[0]):
            rows = pl.ds(level * part_rows, part_rows)
            for index in range(3):
                if index < 2:
                    target = both.at[rows, pl.ds(index * hidden_width, hidden_width)]
                else:
                    target = down.at[rows]
                copies.append(
                    pltpu.make_async_copy(
                        weights.at[level, index, pl.ds(0, part_rows)],
                        target,
                        arrived.at[level, index],
                    )
                )
        for copy in copies:
            copy.start()
        for copy in copies:
            copy.wait()

    first = step < half
    tokens = jnp.where(first, odd_n[0], even_n[0])
    incoming = jnp.where(first, odd_c[0], even_c[0]).astype(F32)
    gate = gates[...]
    parts = product(tokens, both[...], 1, 0)
    gate_part, up_part = parts[:, :hidden_width], parts[:, hidden_width:]
    sigma = 1.0 / (1.0 + jnp.exp(-gate_part))
    smooth = gate_part * sigma
    hidden = (smooth * up_part).astype(BF16)
    hidden_out[...] = hidden
    result = product(hidden, down[...], 1, 1).astype(BF16).astype(F32)
    gate_grad[...] = jnp.sum(incoming * result, axis=-1, keepdims=True)
    routed = gate * result
    grad_pair = (gate * incoming).astype(BF16)
    grad_hidden = product(grad_pair, down[...], 1, 0)
    grad_gate = (grad_hidden * up_part * sigma * (1.0 + gate_part * (1.0 - sigma))).astype(BF16)
    grad_up = (grad_hidden * smooth).astype(BF16)
    grad_parts = jnp.concatenate([grad_gate, grad_up], axis=1)
    pair_out[...] = grad_parts
    entry = product(grad_parts, both[...], 1, 1).astype(BF16).astype(F32)
    if has_before:
        routed = routed + routed_in[...]
        entry = entry + entry_in[...]
    if split:

        @pl.when(first)
        def _():
            routed_odd[0] = routed.astype(BF16)
            entry_odd[0] = entry.astype(BF16)

        @pl.when(jnp.logical_not(first))
        def _():
            routed_even[0] = routed.astype(BF16)
            entry_even[0] = entry.astype(BF16)
    else:
        routed_out[...] = routed
        entry_out[...] = entry


def expert_pass(tokens, grads, gates, weights, part_rows, before, split, waits=()):
    even_n, odd_n = tokens
    even_c, odd_c = grads
    count, rows, width = even_n.shape
    hidden_width = weights.shape[3]
    tiles = 2 * count
    total = tiles * rows
    odd = pl.BlockSpec((1, rows, width), lambda t: (jnp.minimum(t, count - 1), 0, 0))
    even = pl.BlockSpec((1, rows, width), lambda t: (jnp.maximum(t - count, 0), 0, 0))
    tile = lambda size: pl.BlockSpec((rows, size), lambda t: (t, 0))
    in_specs = [odd, even, odd, even, tile(1), pl.BlockSpec(memory_space=pl.ANY)]
    operands = [odd_n, even_n, odd_c, even_c, gates, weights, *waits]
    in_specs += [pl.BlockSpec(memory_space=pl.ANY)] * len(waits)
    if before is not None:
        in_specs += [tile(width), tile(width)]
        operands += list(before)
    if split:
        out_specs = [odd, even, odd, even]
        out_shape = [jax.ShapeDtypeStruct((count, rows, width), BF16)] * 4
    else:
        out_specs = [tile(width), tile(width)]
        out_shape = [jax.ShapeDtypeStruct((total, width), F32)] * 2
    out_specs += [tile(1), tile(hidden_width), tile(2 * hidden_width)]
    out_shape += [
        jax.ShapeDtypeStruct((total, 1), F32),
        jax.ShapeDtypeStruct((total, hidden_width), BF16),
        jax.ShapeDtypeStruct((total, 2 * hidden_width), BF16),
    ]
    return pl.pallas_call(
        functools.partial(expert_kernel, before is not None, split, part_rows, len(waits)),
        grid=(tiles,),
        in_specs=in_specs,
        out_specs=out_specs,
        out_shape=out_shape,
        scratch_shapes=[
            pltpu.VMEM((width, 2 * hidden_width), BF16),
            pltpu.VMEM((width, hidden_width), BF16),
            pltpu.SemaphoreType.DMA((weights.shape[0], 3)),
        ],
        compiler_params=kernel_params(1),
        cost_estimate=LIGHT,
        name="expert_pass",
    )(*operands)


def shared_kernel(place_ref, tokens_ref, incoming_ref, weights, result_out, entry_out, *targets):
    tokens, incoming = tokens_ref[...], incoming_ref[...]
    core = place_ref[0]
    gate_part = product(tokens, weights[0], 1, 0)
    up_part = product(tokens, weights[1], 1, 0)
    sigma = 1.0 / (1.0 + jnp.exp(-gate_part))
    smooth = gate_part * sigma
    hidden = (smooth * up_part).astype(BF16)
    result_out[...] = product(hidden, weights[2], 1, 1)
    grad_hidden = product(incoming, weights[2], 1, 0)
    grad_gate = (grad_hidden * up_part * sigma * (1.0 + gate_part * (1.0 - sigma))).astype(BF16)
    grad_up = (grad_hidden * smooth).astype(BF16)
    entry_out[...] = product(grad_gate, weights[0], 1, 1) + product(grad_up, weights[1], 1, 1)
    store_split(product(tokens, grad_gate, 0, 0), core, 0, targets)
    store_split(product(tokens, grad_up, 0, 0), core, 1, targets)
    store_split(product(incoming, hidden, 0, 0), core, 2, targets)


def shared_pass(tokens, incoming, weights, dense_rows):
    rows, width = tokens.shape
    hidden_width = weights.shape[2]
    shapes = split_shapes(3, width, hidden_width, dense_rows)
    out_shape = [jax.ShapeDtypeStruct((rows, width), F32)] * 2
    out_shape += [jax.ShapeDtypeStruct(shape, BF16) for shape in shapes]
    return pl.pallas_call(
        shared_kernel,
        grid_spec=pltpu.PrefetchScalarGridSpec(
            num_scalar_prefetch=1,
            grid=(1,),
            in_specs=[whole(tokens), whole(incoming), whole(weights)],
            out_specs=[whole(shape) for shape in out_shape],
        ),
        out_shape=out_shape,
        compiler_params=kernel_params(1),
        cost_estimate=LIGHT,
        name="shared_pass",
    )(lax.axis_index("expert")[None] % 2, tokens, incoming, weights)


def expert_grad_kernel(odd_n, even_n, odd_c, even_c, gates, hidden, pair, *refs):
    out = refs[-1]
    count, rows, span = odd_n.shape
    half = count * rows
    hidden_width = hidden.shape[1]
    tokens = jnp.concatenate(
        [odd_n[...].reshape(half, span), even_n[...].reshape(half, span)], axis=0
    )
    incoming = jnp.concatenate(
        [odd_c[...].reshape(half, span), even_c[...].reshape(half, span)], axis=0
    )
    grad_pair = (gates[...] * incoming.astype(F32)).astype(BF16)
    both = product(tokens, pair[...], 0, 0)
    out[0] = both[:, :hidden_width].astype(BF16)
    out[1] = both[:, hidden_width:].astype(BF16)
    out[2] = product(grad_pair, hidden[...], 0, 0).astype(BF16)


def expert_grad(tokens, grads, gates, hidden, pair, waits=()):
    even_n, odd_n = tokens
    even_c, odd_c = grads
    count, rows, width = even_n.shape
    hidden_width = hidden.shape[1]
    span = 256
    stack = pl.BlockSpec((count, rows, span), lambda t: (0, 0, t))
    return pl.pallas_call(
        expert_grad_kernel,
        grid=(width // span,),
        in_specs=[stack, stack, stack, stack, whole(gates), whole(hidden), whole(pair)]
        + [pl.BlockSpec(memory_space=pl.ANY)] * len(waits),
        out_specs=pl.BlockSpec((3, span, hidden_width), lambda t: (0, t, 0)),
        out_shape=jax.ShapeDtypeStruct((3, width, hidden_width), BF16),
        compiler_params=kernel_params(1),
        cost_estimate=LIGHT,
        name="expert_weight_grad",
    )(odd_n, even_n, odd_c, even_c, gates, hidden, pair, *waits)


def body(
    block_input_vectors,
    output_sensitivity,
    rotary_offsets,
    dispatched_specialist_ids,
    specialist_quotas,
    storage_holder,
    mixer_projection_matrices,
    mixer_mean_estimate,
    mixer_variance_estimate,
    common_projection_matrices,
    common_mean_estimate,
    common_variance_estimate,
    gating_projection_matrix,
    gating_mean_estimate,
    gating_variance_estimate,
    scaling_factors,
    scaling_mean_estimate,
    scaling_variance_estimate,
    dispatched_projection_matrices,
    dispatched_mean_estimate,
    dispatched_variance_estimate,
):
    token_rows = block_input_vectors.shape[1]
    width = block_input_vectors.shape[2]
    head_dim = HEAD_DIM
    heads = width // head_dim
    length = rotary_offsets.shape[1]
    specialist_total = specialist_quotas.shape[0]
    expert_local = dispatched_projection_matrices.shape[0]
    hidden_width = dispatched_projection_matrices.shape[3]
    part_rows = dispatched_projection_matrices.shape[2]
    dense_rows = mixer_projection_matrices.shape[1]
    groups = lax.axis_size("expert")
    deep = lax.axis_size("dp")
    here = lax.axis_index("expert")
    level = lax.axis_index("dp")
    scale_attn = head_dim ** (-0.5)
    straight = deep == 4

    attn_own = mixer_projection_matrices.astype(BF16)
    shared_own = common_projection_matrices.astype(BF16)
    router_own = gating_projection_matrix.astype(BF16)
    gain_own = scaling_factors.astype(BF16)
    expert_own = dispatched_projection_matrices.astype(BF16)

    everyone = deep * groups
    small = jnp.concatenate([router_own.reshape(-1), gain_own.reshape(-1)])
    small_size = small.shape[0]
    small_rows = -(-small_size // 1024) * 8
    small = jnp.pad(small, (0, small_rows * 128 - small_size)).reshape(small_rows, 128)
    small_all = lax.all_to_all(
        jnp.broadcast_to(small, (everyone, small_rows, 128)),
        ("dp", "expert"),
        0,
        0,
        tiled=True,
    ).reshape(everyone, small_rows * 128)
    router_size = dense_rows * specialist_total
    router_low = small_all[:, :router_size].reshape(width, specialist_total)
    gain_low = (
        small_all[:, router_size : router_size + 2 * dense_rows]
        .reshape(everyone, 2, dense_rows)
        .transpose(1, 0, 2)
        .reshape(2, width)
    )
    inputs_low = block_input_vectors[0]
    grad_low = output_sensitivity[0]
    grad_out = grad_low.astype(F32)
    attn_column = lax.all_gather(attn_own, "dp")
    projection_fan = fan(attn_column[:, :3])
    shared_size = shared_own.size
    shared_rows = -(-shared_size // (8 * width)) * 8
    shared_flat = jnp.pad(shared_own.reshape(-1), (0, shared_rows * width - shared_size))
    column = lax.all_gather(
        after(
            jnp.concatenate([inputs_low, shared_flat.reshape(shared_rows, width)], 0), attn_column
        ),
        "dp",
    )
    column, *projection_fan = lax.optimization_barrier((column, *projection_fan))
    sequence = column[:, :token_rows].reshape(length, width)
    shared_column = column[:, token_rows:].reshape(deep, -1)[:, :shared_size].reshape(
        deep, 3, dense_rows, hidden_width
    )
    expert_parts = [lax.all_gather(after(expert_own[0], sequence), "dp")]
    projection_even = jnp.stack(projection_fan)
    projection_odd = swap(projection_even, 1)
    out_even, out_odd = gather_swaps(attn_column[:, 3:], sequence)
    for number in range(1, expert_local):
        expert_parts.append(
            lax.all_gather(after(expert_own[number], projection_odd), "dp")
        )
    projections = assemble(projection_even, projection_odd)
    out_low = assemble(out_even, out_odd)[0]
    grads_fan = fan(hold([grad_low], projections)[0])
    gain_one = gain_low[0].astype(F32)
    gain_two = gain_low[1].astype(F32)

    sequence_low, sequence = sequence, sequence.astype(F32)

    normed_all, _, _ = norm_forward(sequence, gain_one)
    inputs = inputs_low.astype(F32)
    normed, scaled_one, inverse_one = norm_forward(inputs, gain_one)
    place = level * token_rows
    cosine_all, sine_all = rotary_tables(rotary_offsets[0], head_dim)
    starts = jnp.arange(length, dtype=jnp.int32) - rotary_offsets[0]
    query, keys, values, mixed, mixed_low = attention(
        place, normed_all, projections, cosine_all, sine_all, starts, token_rows
    )
    mixed_low = hold([mixed_low], *grads_fan[1:])[0]
    grads_even = jnp.stack(grads_fan)
    grads_plane = (grads_even, swap(grads_even, 1))
    middle = inputs + contract(mixed_low, out_low, 1, 0)
    second, scaled_two, inverse_two = norm_forward(middle, gain_two)

    probs = jax.nn.softmax(contract(second, router_low, 1, 0), axis=-1)
    experts = jnp.arange(specialist_total, dtype=jnp.int32)
    named = jnp.any(dispatched_specialist_ids[0][:, :, None] == experts, axis=1)
    order = jnp.arange(token_rows)
    earlier = contract(
        (order[:, None] > order[None, :]).astype(BF16), named.astype(BF16), 1, 0
    )
    kept = named & (earlier < specialist_quotas.astype(F32)[None, :])
    gate = jnp.where(kept, probs, 0.0)
    to_storage = (storage_holder[:, None] == experts[None, :]).astype(F32)
    gate_stored = jnp.sum(gate[:, :, None] * to_storage[None], axis=1)
    gates_sent = gate_stored.reshape(token_rows, groups, expert_local).transpose(1, 0, 2)
    gates_received = lax.all_to_all(gates_sent, "expert", 0, 0, tiled=True)
    half = jnp.arange(groups // 2) * 2
    relative = here ^ jnp.concatenate([half + 1, half])
    gates_plane = gates_received[relative].reshape(groups * token_rows, expert_local)

    turned, own_turned, mixed_turned = normed_all.T, normed.T, mixed_low.T
    second_fan = fan(second)
    second_even = jnp.stack(
        list(second_fan[:1])
        + list(hold(
            second_fan[1:], shared_column, turned, own_turned, mixed_turned
        ))
    )
    tokens = (second_even, swap(second_even, 1))
    expert_parts[0] = after(expert_parts[0], tokens[1], grads_plane[1], gates_plane)

    shared_fan = fan(hold([shared_column], tokens[1], expert_parts[0])[0])

    def shared_step(shared_even, shared_odd):
        shared_low = assemble(shared_even, shared_odd)
        out, entry, *grad = shared_pass(second, grad_low, shared_low, dense_rows)
        if len(grad) == 1:
            grad = core_split(grad[0], dense_rows)
        return out, entry, chip_sums(grad[0], swap(grad[1], 1))

    def spread_after(sums, *others):
        lows = hold([part.astype(BF16) for part in sums[1:]], *others)
        return [swap(part, 2 * index + 2) for index, part in enumerate(lows)]

    mask = here ^ jnp.arange(groups)
    back = mask // 2 + jnp.where(mask % 2 == 1, 0, groups // 2)

    def return_gates(gate_grads, *others):
        sent = jnp.concatenate(gate_grads, -1).reshape(groups, token_rows, expert_local)[back]
        return lax.all_to_all(hold([sent], *others)[0], "expert", 0, 0, tiled=True)

    gate_grads = []
    expert_sums = []
    part_sums = []
    before = None
    for number in range(expert_local):
        last = number == expert_local - 1
        gate_column = gates_plane[:, number : number + 1]
        parts = expert_pass(
            tokens, grads_plane, gate_column, expert_parts[number], part_rows, before, last,
            (),
        )
        before, (gate_grad, hidden, pair) = parts[:-3], parts[-3:]
        gate_grads.append(gate_grad)
        if number == 0:
            shared_even = hold([jnp.stack(shared_fan)], hidden)[0]
            shared_odd = swap(shared_even, 1)
        if last:
            routed_odd, routed_even, entry_odd, entry_even = before
            entry_odd = hold([entry_odd], *shared_parts)[0]
            entry_other = swap(entry_odd, 1)
            entry_sums = join_cores(entry_even, entry_other)
            entry_parts = spread_chips(entry_sums)
            routed_other = swap(
                hold([routed_odd], *[part.astype(BF16) for part in entry_sums[1:]])[0], 1
            )
        expert_part = expert_grad(
            tokens,
            grads_plane,
            gate_column,
            hidden,
            pair,
            [routed_other] if last else shared_fan[1:],
        )
        if number == 0:
            shared_odd = hold([shared_odd], expert_part)[0]
            shared_out, shared_entry, shared_sums = shared_step(shared_even, shared_odd)
            shared_parts = spread_after(shared_sums, *expert_parts[1:2])
        expert_whole = expert_part
        expert_part = expert_part.reshape(3, deep, part_rows, hidden_width)
        if last:
            gate_grad_back = return_gates(gate_grads, expert_whole)
            shared_total = add_up(shared_sums[0], hold(shared_parts, expert_whole))
            extra = -(part_rows + dense_rows) % 16
            shared_total = jnp.pad(shared_total.astype(BF16), ((0, 0), (0, 0), (0, extra), (0, 0)))
            expert_part = jnp.concatenate([expert_part, shared_total], 2)
        part_sum = lax.psum_scatter(
            expert_part.reshape(3, -1, hidden_width), "dp", scatter_dimension=1, tiled=True
        )
        part_sums.append(part_sum)
        expert_sums.append(part_sum[:, :part_rows].astype(F32))
    shared_sum = part_sum[:, part_rows : part_rows + dense_rows].astype(F32)
    expert_sum = jnp.stack(expert_sums)

    entry_parts = hold(entry_parts, expert_whole)
    grad_second = add_up(entry_sums[0], entry_parts)
    routed_sums = join_cores(routed_even, routed_other)
    gate_grad_stored = gate_grad_back.transpose(1, 0, 2).reshape(token_rows, specialist_total)
    grad_prob = jnp.sum(gate_grad_stored[:, None, :] * to_storage[None], axis=-1)
    grad_prob = jnp.where(kept, grad_prob, 0.0)


    grad_logit = (probs * (grad_prob - jnp.sum(probs * grad_prob, axis=-1, keepdims=True))).astype(
        BF16
    )
    router_grad = contract(second, grad_logit, 0, 0)
    grad_second = grad_second + contract(grad_logit, router_low, 1, 1) + shared_entry
    gain_two_grad = jnp.sum(grad_second * scaled_two, axis=0)
    grad_middle = norm_backward(grad_second, scaled_two, inverse_two, gain_two) + grad_out
    grad_attn_out = grad_middle.astype(BF16)

    def grad_part(first, count, waits=()):
        *grads, dq, dk, dv = attention_grad(
            place,
            turned,
            own_turned,
            mixed_turned,
            out_low,
            query,
            keys,
            values,
            mixed,
            grad_attn_out,
            cosine_all,
            sine_all,
            starts,
            dense_rows,
            first,
            count,
            waits,
        )
        if len(grads) == 1:
            grads = core_split(grads[0], dense_rows)
        return grads[0], grads[1], (dq, dk, dv)

    pairs = width // (2 * head_dim)
    early = (pairs + 1) // 2
    first_mine, first_other, first_terms = grad_part(0, early)
    last_mine, last_other, last_terms = grad_part(
        early, pairs - early, [first_other, part_sums[0]]
    )
    first_sums = chip_sums(first_mine, swap(first_other, 1))
    first_parts = spread_chips(first_sums)
    last_received = hold([swap(last_other, 1)], first_sums[1].astype(BF16))[0]
    last_sums = chip_sums(last_mine, last_received)
    last_parts = spread_after(last_sums, *first_parts)
    normed_low, grad_normed, gain_one_grad = normed_grad(
        sequence_low,
        projections,
        (first_terms, last_terms),
        token_rows,
        [first_sums[1].astype(BF16)],
    )
    gain_one_grad = gain_one_grad[0]
    small_grad = jnp.concatenate(
        [
            router_grad.reshape(everyone, router_size),
            jnp.stack([gain_one_grad, gain_two_grad])
            .reshape(2, everyone, dense_rows)
            .transpose(1, 0, 2)
            .reshape(everyone, 2 * dense_rows),
        ],
        -1,
    )
    small_grad = jnp.pad(small_grad, ((0, 0), (0, small_rows * 128 - small_size)))
    small_received = lax.all_to_all(
        small_grad.reshape(everyone, small_rows, 128), ("dp", "expert"), 0, 0, tiled=True
    )
    small_sum = jnp.sum(hold([small_received], *last_parts)[0], axis=0).reshape(-1)
    first_total = add_up(first_sums[0], hold(first_parts, grad_normed))
    last_total = add_up(last_sums[0], last_parts)
    first_sum, first_column = column_sum(
        first_total, 1, last_parts[0], last_total.astype(BF16)
    )
    expert_squares = sum(jnp.sum(part * part) for part in expert_sums)
    last_sum, _ = column_sum(last_total, 1, None, jnp.broadcast_to(expert_squares, (8, 128)))
    routed_parts = spread_after(routed_sums, *first_column)
    grad_normed = grad_normed - pick(normed_low, level, 0).astype(F32)
    arrived = lax.psum_scatter(
        hold([normed_low.reshape(length, width)], part_sums[-1])[0],
        "dp",
        scatter_dimension=0,
        tiled=True,
    )
    grad_normed = grad_normed + arrived.astype(F32)
    grad_inputs = norm_backward(grad_normed, scaled_one, inverse_one, gain_one) + grad_middle
    attn_sum = jnp.concatenate([first_sum, last_sum], -1)
    router_sum = small_sum[:router_size].reshape(dense_rows, specialist_total)
    gain_sum = small_sum[router_size:small_size].reshape(2, dense_rows)

    local_squares = (
        jnp.sum(attn_sum * attn_sum)
        + jnp.sum(shared_sum * shared_sum)
        + jnp.sum(router_sum * router_sum)
        + jnp.sum(gain_sum * gain_sum)
        + expert_squares
    )
    spread = jnp.broadcast_to(local_squares, (everyone, 8, 128))
    squares = lax.all_to_all(spread, ("dp", "expert"), 0, 0, tiled=True)
    grad_norm = jnp.sqrt(jnp.sum(squares[:, 0, 0]))
    routed = add_up(routed_sums[0], hold(routed_parts, squares))
    block_out = (middle + shared_out + routed).astype(BF16)
    scale = jnp.minimum(1.0, CLIP_VALUE / (grad_norm + 1e-06))
    attn_new, attn_moment, attn_square = adam(
        mixer_projection_matrices,
        mixer_mean_estimate,
        mixer_variance_estimate,
        attn_sum,
        scale,
        RATE_MATRIX,
    )
    shared_new, shared_moment, shared_square = adam(
        common_projection_matrices,
        common_mean_estimate,
        common_variance_estimate,
        shared_sum,
        scale,
        RATE_MATRIX,
    )
    router_new, router_moment, router_square = adam(
        gating_projection_matrix,
        gating_mean_estimate,
        gating_variance_estimate,
        router_sum,
        scale,
        RATE_MATRIX,
    )
    gain_new, gain_moment, gain_square = adam(
        scaling_factors,
        scaling_mean_estimate,
        scaling_variance_estimate,
        gain_sum,
        scale,
        RATE_GAIN,
    )
    expert_new, expert_moment, expert_square = adam(
        dispatched_projection_matrices,
        dispatched_mean_estimate,
        dispatched_variance_estimate,
        expert_sum,
        scale,
        RATE_EXPERT,
    )
    return (
        block_out[None],
        grad_inputs[None],
        grad_norm,
        attn_new,
        attn_moment,
        attn_square,
        attn_new.astype(BF16),
        shared_new,
        shared_moment,
        shared_square,
        shared_new.astype(BF16),
        router_new,
        router_moment,
        router_square,
        router_new.astype(BF16),
        gain_new,
        gain_moment,
        gain_square,
        expert_new,
        expert_moment,
        expert_square,
        expert_new.astype(BF16),
    )


def solution(mesh):
    placed = (
        P("expert", "dp", None),
        P("expert", "dp", None),
        P("expert", None),
        P("expert", "dp", None),
        P(),
        P(),
        P(None, ("dp", "expert"), None),
        P(None, ("dp", "expert"), None),
        P(None, ("dp", "expert"), None),
        P(None, ("dp", "expert"), None),
        P(None, ("dp", "expert"), None),
        P(None, ("dp", "expert"), None),
        P(("dp", "expert"), None),
        P(("dp", "expert"), None),
        P(("dp", "expert"), None),
        P(None, ("dp", "expert")),
        P(None, ("dp", "expert")),
        P(None, ("dp", "expert")),
        P("expert", None, "dp", None),
        P("expert", None, "dp", None),
        P("expert", None, "dp", None),
    )
    return jax.shard_map(
        body,
        mesh=mesh,
        in_specs=placed,
        out_specs=(
            P("expert", "dp", None),
            P("expert", "dp", None),
            P(),
            P(None, ("dp", "expert"), None),
            P(None, ("dp", "expert"), None),
            P(None, ("dp", "expert"), None),
            P(None, ("dp", "expert"), None),
            P(None, ("dp", "expert"), None),
            P(None, ("dp", "expert"), None),
            P(None, ("dp", "expert"), None),
            P(None, ("dp", "expert"), None),
            P(("dp", "expert"), None),
            P(("dp", "expert"), None),
            P(("dp", "expert"), None),
            P(("dp", "expert"), None),
            P(None, ("dp", "expert")),
            P(None, ("dp", "expert")),
            P(None, ("dp", "expert")),
            P("expert", None, "dp", None),
            P("expert", None, "dp", None),
            P("expert", None, "dp", None),
            P("expert", None, "dp", None),
        ),
        check_vma=False,
    )
```

```python
import functools

import jax
import jax.numpy as jnp
from jax import lax
from jax.experimental import pallas as pl
from jax.experimental.pallas import tpu as pltpu
from jax.sharding import PartitionSpec as P

HEAD_DIM = 128
STEP = 10


NORM_EPS = 1e-06
THETA = 10000.0
CLIP_VALUE = 1.0
BETA_ONE = 0.9
BETA_TWO = 0.999
ADAM_EPS = 1e-08
DECAY = 0.1
RATE_MATRIX = 0.02
RATE_EXPERT = 0.1
RATE_GAIN = 0.3
MASKED = -1e30

F32 = jnp.float32
BF16 = jnp.bfloat16


def contract(left, right, left_dim, right_dim):
    return lax.dot_general(
        left, right, (((left_dim,), (right_dim,)), ((), ())), preferred_element_type=F32
    )


def rotary_tables(places, head_dim):
    half = head_dim // 2
    freq = THETA ** (-2.0 * jnp.arange(half, dtype=F32) / head_dim)
    angle = places.astype(F32)[:, None] * freq
    cosine, sine = jnp.cos(angle), jnp.sin(angle)
    return (jnp.concatenate([cosine, cosine], -1), jnp.concatenate([-sine, sine], -1))


def norm_forward(values, gain):
    inverse = lax.rsqrt(jnp.mean(values * values, axis=-1, keepdims=True) + NORM_EPS)
    scaled = values * inverse
    return ((scaled * gain).astype(BF16), scaled, inverse)


def norm_backward(grad, scaled, inverse, gain):
    local = grad * gain
    return inverse * (local - scaled * jnp.mean(local * scaled, axis=-1, keepdims=True))


def adam(master, first, second, grad, scale, rate):
    clipped = grad * scale
    first_new = BETA_ONE * first + (1.0 - BETA_ONE) * clipped
    second_new = BETA_TWO * second + (1.0 - BETA_TWO) * clipped * clipped
    first_hat = first_new / (1.0 - BETA_ONE**STEP)
    second_hat = second_new / (1.0 - BETA_TWO**STEP)
    master_new = master - rate * (first_hat / (jnp.sqrt(second_hat) + ADAM_EPS) + DECAY * master)
    return (master_new, first_new, second_new)


def after(value, *others):
    return lax.optimization_barrier((value,) + others)[0]


def hold_kernel(*_):
    pass


def hold(values, *others):
    anywhere = pl.BlockSpec(memory_space=pl.ANY)
    return pl.pallas_call(
        hold_kernel,
        in_specs=[anywhere] * (len(values) + len(others)),
        out_specs=[anywhere] * len(values),
        out_shape=[jax.ShapeDtypeStruct(value.shape, value.dtype) for value in values],
        input_output_aliases={index: index for index in range(len(values))},
        cost_estimate=LIGHT,
        name="hold",
    )(*values, *others)


def swap(value, mask):
    size = lax.axis_size("expert")
    return lax.ppermute(value, "expert", [(i, i ^ mask) for i in range(size)])


def rotate(value, step):
    size = lax.axis_size("dp")
    return lax.ppermute(value, "dp", [(i, (i + step) % size) for i in range(size)])


def shift(value, step):
    size = lax.axis_size("dp")
    return lax.ppermute(
        value, "dp", [(i, i + step) for i in range(size) if 0 <= i + step < size]
    )


def put(buffer, block, index, axis):
    return lax.dynamic_update_slice_in_dim(buffer, jnp.expand_dims(block, axis), index, axis)


def pick(buffer, index, axis):
    return lax.dynamic_index_in_dim(buffer, index, axis, keepdims=False)


def fan(block, *others):
    size = lax.axis_size("expert")
    block = after(block, *others) if others else block
    return [block] + [swap(block, mask) for mask in range(2, size, 2)]


def gather_swaps(block, *others):
    even = jnp.stack(fan(block, *others))
    return even, swap(even, 1)


def join_cores(even, other):
    return [even[k].astype(F32) + other[k].astype(F32) for k in range(even.shape[0])]


def spread_chips(summed):
    return [swap(summed[index].astype(BF16), 2 * index) for index in range(1, len(summed))]


def add_up(total, parts):
    for part in parts:
        total = total + part.astype(F32)
    return total


def join_chips(summed):
    return add_up(summed[0], spread_chips(summed))


def core_split(grad, rows):
    core = lax.axis_index("expert") % 2
    split = grad.reshape(grad.shape[0], -1, 2, rows, grad.shape[-1])
    return pick(split, core, 2), pick(split, 1 - core, 2)


def chip_sums(mine, received):
    chip = lax.axis_index("expert") // 2
    chips = lax.axis_size("expert") // 2
    shape = (mine.shape[0], -1, chips) + mine.shape[2:]
    mine, received = mine.reshape(shape), received.reshape(shape)
    return [
        pick(mine, chip ^ mask, 2).astype(F32) + pick(received, chip ^ mask, 2).astype(F32)
        for mask in range(chips)
    ]


def column_sum(total, axis, later, *others):
    deep, level = lax.axis_size("dp"), lax.axis_index("dp")
    low = total.astype(BF16)
    result = pick(total, level, axis)
    parts = []
    for step in range(1, deep):
        block = pick(low, (level + step) % deep, axis)
        if later is not None and step == 2:
            block = hold([block], later)[0]
        parts.append(rotate(block, step))
    if others:
        parts = hold(parts, *others)
    return add_up(result, parts), parts


VMEM_LIMIT = 60 * 1024 * 1024
LIGHT = pl.CostEstimate(flops=1, bytes_accessed=1, transcendentals=0)


def product(left, right, left_dim, right_dim):
    return lax.dot_general(
        left, right, (((left_dim,), (right_dim,)), ((), ())), preferred_element_type=F32
    )


def kernel_params(steps):
    return pltpu.CompilerParams(
        dimension_semantics=("arbitrary",) * steps, vmem_limit_bytes=VMEM_LIMIT
    )


def whole(array):
    shape = array.shape
    return pl.BlockSpec(shape, lambda *_: (0,) * len(shape), pipeline_mode=pl.Buffered(1))


def assemble_kernel(place_ref, even, odd, out):
    core = place_ref[0] % 2
    out[:, :, pl.ds(core, 1)] = jnp.swapaxes(even[0], 0, 1)[:, :, None]
    out[:, :, pl.ds(1 - core, 1)] = jnp.swapaxes(odd[0], 0, 1)[:, :, None]


def assemble(even, odd):
    chips, deep, parts, rows, width = even.shape
    here = lax.axis_index("expert")
    chip = pl.BlockSpec(
        (1, deep, parts, rows, width), lambda c, p: (c ^ (p[0] // 2), 0, 0, 0, 0)
    )
    joined = pl.pallas_call(
        assemble_kernel,
        grid_spec=pltpu.PrefetchScalarGridSpec(
            num_scalar_prefetch=1,
            grid=(chips,),
            in_specs=[chip, chip],
            out_specs=pl.BlockSpec(
                (parts, deep, 2, rows, width), lambda c, p: (0, 0, c, 0, 0)
            ),
        ),
        out_shape=jax.ShapeDtypeStruct((parts, deep, 2 * chips, rows, width), even.dtype),
        compiler_params=kernel_params(1),
        cost_estimate=LIGHT,
        name="assemble",
    )(here[None], even, odd)
    return joined.reshape(parts, deep * 2 * chips * rows, width)


def turn_head(values, cosine, sine):
    return values * cosine + pltpu.roll(values, HEAD_DIM // 2, 1) * sine


def head_weights(query, keys, allowed):
    scores = product(query, keys, 1, 1) * HEAD_DIM ** (-0.5)
    scores = jnp.where(allowed, scores, MASKED)
    raised = jnp.exp(scores - jnp.max(scores, axis=-1, keepdims=True))
    return raised / jnp.sum(raised, axis=-1, keepdims=True)


def visible_keys(place, own_starts, starts):
    shape = (own_starts.shape[0], starts.shape[1])
    query_index = place + lax.broadcasted_iota(jnp.int32, shape, 0)
    key_index = lax.broadcasted_iota(jnp.int32, shape, 1)
    return (own_starts == starts) & (key_index <= query_index)


def attention_kernel(
    place_ref, normed, wq, wk, wv, cosine, sine, starts, own_starts, q_out, k_out, v_out, o_out, low_out
):
    rows = q_out.shape[0]
    place = pl.multiple_of(place_ref[0], rows)
    own = normed[pl.ds(place, rows), :]
    everything = normed[...]
    allowed = visible_keys(place, own_starts[...], starts[...])
    query = product(own, wq[0], 1, 0)
    keys = product(everything, wk[0], 1, 0)
    values = product(everything, wv[0], 1, 0).astype(BF16)
    v_out[...] = values
    own_cosine, own_sine = cosine[pl.ds(place, rows), :], sine[pl.ds(place, rows), :]
    for head in range(q_out.shape[1] // HEAD_DIM):
        lanes = slice(head * HEAD_DIM, (head + 1) * HEAD_DIM)
        turned_query = turn_head(query[:, lanes], own_cosine, own_sine).astype(BF16)
        turned_keys = turn_head(keys[:, lanes], cosine[...], sine[...]).astype(BF16)
        weights = head_weights(turned_query, turned_keys, allowed).astype(BF16)
        mixed = product(weights, values[:, lanes], 1, 0)
        q_out[:, lanes] = turned_query
        k_out[:, lanes] = turned_keys
        o_out[:, lanes] = mixed
        low_out[:, lanes] = mixed.astype(BF16)


def attention(place, normed, projections, cosine, sine, starts, rows):
    length, width = normed.shape
    span = 2 * HEAD_DIM
    own_starts = lax.dynamic_slice_in_dim(starts, place, rows)[:, None]
    starts = starts[None, :]
    column = lambda index: pl.BlockSpec((1, width, span), lambda p, _: (index, 0, p))
    blocks = lambda count: pl.BlockSpec((count, span), lambda p, _: (0, p))
    return pl.pallas_call(
        attention_kernel,
        grid_spec=pltpu.PrefetchScalarGridSpec(
            num_scalar_prefetch=1,
            grid=(width // span,),
            in_specs=[
                whole(normed),
                column(0),
                column(1),
                column(2),
                whole(cosine),
                whole(sine),
                whole(starts),
                whole(own_starts),
            ],
            out_specs=[blocks(rows), blocks(length), blocks(length), blocks(rows), blocks(rows)],
        ),
        out_shape=[
            jax.ShapeDtypeStruct((rows, width), BF16),
            jax.ShapeDtypeStruct((length, width), BF16),
            jax.ShapeDtypeStruct((length, width), BF16),
            jax.ShapeDtypeStruct((rows, width), F32),
            jax.ShapeDtypeStruct((rows, width), BF16),
        ],
        compiler_params=kernel_params(1),
        cost_estimate=LIGHT,
        name="attention_forward",
    )(place[None], normed, projections, projections, projections, cosine, sine, starts, own_starts)


def split_shapes(parts, rows_all, width, rows):
    if rows % 8 == 0:
        return [(parts, rows_all // (2 * rows), rows, width)] * 2
    return [(parts, rows_all, width)]


def store_split(grad, core, part, targets):
    if len(targets) == 1:
        targets[0][part] = grad.astype(BF16)
        return
    mine, other = targets
    count, rows = mine.shape[1], mine.shape[2]
    cut = grad.reshape(count, 2, rows, grad.shape[1])
    even, odd = cut[:, 0], cut[:, 1]
    mine[part] = jnp.where(core == 0, even, odd).astype(BF16)
    other[part] = jnp.where(core == 0, odd, even).astype(BF16)


def attention_grad_kernel(
    place_ref, turned_normed, own_turned, mixed_turned, wo, q, k, v, o, arriving, arriving_columns,
    cosine, sine, starts, own_starts, *refs
):
    *grads, dq_out, dk_out, dv_out = refs
    grads = grads[-2:] if len(grads[-1].shape) == 4 else grads[-1:]
    rows = q.shape[0]
    place = pl.multiple_of(place_ref[0], rows)
    allowed = visible_keys(place, own_starts[...], starts[...])
    own_cosine, own_sine = cosine[pl.ds(place, rows), :], sine[pl.ds(place, rows), :]
    mixed_grad = product(arriving[...], wo[...], 1, 1).astype(BF16)
    for head in range(q.shape[1] // HEAD_DIM):
        lanes = slice(head * HEAD_DIM, (head + 1) * HEAD_DIM)
        query, keys, values = q[:, lanes], k[:, lanes], v[:, lanes]
        incoming = mixed_grad[:, lanes]
        weights = head_weights(query, keys, allowed)
        correction = jnp.sum(incoming.astype(F32) * o[:, lanes], axis=-1, keepdims=True)
        weights_grad = product(incoming, values, 1, 1)
        scores_grad = (weights * (weights_grad - correction)).astype(BF16)
        factor = HEAD_DIM ** (-0.5)
        query_grad = product(scores_grad, keys, 1, 0) * factor
        keys_grad = product(scores_grad, query, 0, 0) * factor
        values_grad = product(weights.astype(BF16), incoming, 0, 0)
        dq_out[:, lanes] = turn_head(query_grad, own_cosine, -own_sine).astype(BF16)
        dk_out[:, lanes] = turn_head(keys_grad, cosine[...], -sine[...]).astype(BF16)
        dv_out[:, lanes] = values_grad.astype(BF16)
    core = place_ref[1]
    store_split(product(own_turned[...], dq_out[...], 1, 0), core, 0, grads)
    store_split(product(turned_normed[...], dk_out[...], 1, 0), core, 1, grads)
    store_split(product(turned_normed[...], dv_out[...], 1, 0), core, 2, grads)
    store_split(product(mixed_turned[...], arriving_columns[...], 1, 0), core, 3, grads)


def attention_grad(
    place, turned, own_turned, mixed_turned, wo, q, k, v, o, arriving, cosine, sine, starts, dense_rows,
    first, count, waits=(),
):
    width, length = turned.shape
    rows = q.shape[0]
    span = 2 * HEAD_DIM
    own_starts = lax.dynamic_slice_in_dim(starts, place, rows)[:, None]
    starts = starts[None, :]
    place = jnp.stack([place, lax.axis_index("expert") % 2])
    shapes = split_shapes(4, width, span * count, dense_rows)
    grad_specs = [
        pl.BlockSpec(shape[:-1] + (span,), lambda p, _, size=len(shape): (0,) * (size - 1) + (p,))
        for shape in shapes
    ]
    blocks = lambda size: pl.BlockSpec((size, span), lambda p, _: (0, p + first))
    column = lambda size: pl.BlockSpec((size, span), lambda p, _: (0, p))
    return pl.pallas_call(
        attention_grad_kernel,
        grid_spec=pltpu.PrefetchScalarGridSpec(
            num_scalar_prefetch=1,
            grid=(count,),
            in_specs=[
                whole(turned),
                whole(own_turned),
                whole(mixed_turned),
                pl.BlockSpec((span, width), lambda p, _: (p + first, 0)),
                blocks(rows),
                blocks(length),
                blocks(length),
                blocks(rows),
                whole(arriving),
                blocks(rows),
                whole(cosine),
                whole(sine),
                whole(starts),
                whole(own_starts),
            ]
            + [pl.BlockSpec(memory_space=pl.ANY)] * len(waits),
            out_specs=[*grad_specs, column(rows), column(length), column(length)],
        ),
        out_shape=[
            *[jax.ShapeDtypeStruct(shape, BF16) for shape in shapes],
            jax.ShapeDtypeStruct((rows, span * count), BF16),
            jax.ShapeDtypeStruct((length, span * count), BF16),
            jax.ShapeDtypeStruct((length, span * count), BF16),
        ],
        compiler_params=kernel_params(1),
        cost_estimate=pl.CostEstimate(flops=64 * rows * length * width * count, bytes_accessed=1, transcendentals=0),
        name="attention_backward",
    )(
        place, turned, own_turned, mixed_turned, wo, q, k, v, o, arriving, arriving, cosine, sine, starts,
        own_starts, *waits
    )


def normed_grad_kernel(parts, waits, *refs):
    level_ref, sequence, projections = refs[:3]
    grads = refs[3 : 3 + 3 * parts]
    low_out, own_out, gain_out = refs[3 + 3 * parts + waits :]
    step = pl.program_id(0)
    begin = 0
    total = None
    own = None
    for part in range(parts):
        dq, dk, dv = grads[3 * part : 3 * part + 3]
        lanes = slice(begin, begin + dk.shape[1])
        begin += dk.shape[1]
        term = product(dk[...], projections[1, :, lanes], 1, 1) + product(
            dv[...], projections[2, :, lanes], 1, 1
        )
        total = term if total is None else total + term
    low_out[0] = total.astype(BF16)
    values = sequence[...].astype(F32)
    scaled = values * lax.rsqrt(jnp.mean(values * values, axis=-1, keepdims=True) + NORM_EPS)

    @pl.when(step == 0)
    def _():
        gain_out[...] = jnp.zeros_like(gain_out)

    gain_out[...] += jnp.sum(total * scaled, axis=0, keepdims=True)

    @pl.when(step == level_ref[0])
    def _():
        begin = 0
        own = total
        for part in range(parts):
            dq = grads[3 * part]
            lanes = slice(begin, begin + dq.shape[1])
            begin += dq.shape[1]
            own = own + product(dq[...], projections[0, :, lanes], 1, 1)
        own_out[...] = own
        gain_out[...] += jnp.sum((own - total) * scaled, axis=0, keepdims=True)


def normed_grad(sequence, projections, grads, rows, waits):
    length, width = sequence.shape
    in_specs = [pl.BlockSpec((rows, width), lambda t, _: (t, 0)), whole(projections)]
    operands = [sequence, projections]
    for dq, dk, dv in grads:
        tile = pl.BlockSpec((rows, dk.shape[1]), lambda t, _: (t, 0))
        in_specs += [whole(dq), tile, tile]
        operands += [dq, dk, dv]
    return pl.pallas_call(
        functools.partial(normed_grad_kernel, len(grads), len(waits)),
        grid_spec=pltpu.PrefetchScalarGridSpec(
            num_scalar_prefetch=1,
            grid=(length // rows,),
            in_specs=in_specs + [pl.BlockSpec(memory_space=pl.ANY)] * len(waits),
            out_specs=[
                pl.BlockSpec((1, rows, width), lambda t, _: (t, 0, 0)),
                pl.BlockSpec((rows, width), lambda t, _: (0, 0)),
                pl.BlockSpec((1, width), lambda t, _: (0, 0)),
            ],
        ),
        out_shape=[
            jax.ShapeDtypeStruct((length // rows, rows, width), BF16),
            jax.ShapeDtypeStruct((rows, width), F32),
            jax.ShapeDtypeStruct((1, width), F32),
        ],
        compiler_params=kernel_params(1),
        cost_estimate=pl.CostEstimate(flops=48 * length * width * width, bytes_accessed=1, transcendentals=0),
        name="normed_grad",
    )(lax.axis_index("dp")[None], *operands, *waits)


def expert_kernel(has_before, split, part_rows, waits, *refs):
    odd_n, even_n, odd_c, even_c, gates, weights = refs[:6]
    refs = refs[6 + waits :]
    if has_before:
        routed_in, entry_in = refs[:2]
        refs = refs[2:]
    if split:
        routed_odd, routed_even, entry_odd, entry_even = refs[:4]
        refs = refs[4:]
    else:
        routed_out, entry_out = refs[:2]
        refs = refs[2:]
    gate_grad, hidden_out, pair_out, both, down, arrived = refs
    step = pl.program_id(0)
    half = pl.num_programs(0) // 2
    hidden_width = weights.shape[3]

    @pl.when(step == 0)
    def _():
        copies = []
        for level in range(weights.shape[0]):
            rows = pl.ds(level * part_rows, part_rows)
            for index in range(3):
                if index < 2:
                    target = both.at[rows, pl.ds(index * hidden_width, hidden_width)]
                else:
                    target = down.at[rows]
                copies.append(
                    pltpu.make_async_copy(
                        weights.at[level, index, pl.ds(0, part_rows)],
                        target,
                        arrived.at[level, index],
                    )
                )
        for copy in copies:
            copy.start()
        for copy in copies:
            copy.wait()

    first = step < half
    tokens = jnp.where(first, odd_n[0], even_n[0])
    incoming = jnp.where(first, odd_c[0], even_c[0]).astype(F32)
    gate = gates[...]
    parts = product(tokens, both[...], 1, 0)
    gate_part, up_part = parts[:, :hidden_width], parts[:, hidden_width:]
    sigma = 1.0 / (1.0 + jnp.exp(-gate_part))
    smooth = gate_part * sigma
    hidden = (smooth * up_part).astype(BF16)
    hidden_out[...] = hidden
    result = product(hidden, down[...], 1, 1).astype(BF16).astype(F32)
    gate_grad[...] = jnp.sum(incoming * result, axis=-1, keepdims=True)
    routed = gate * result
    grad_pair = (gate * incoming).astype(BF16)
    grad_hidden = product(grad_pair, down[...], 1, 0)
    grad_gate = (grad_hidden * up_part * sigma * (1.0 + gate_part * (1.0 - sigma))).astype(BF16)
    grad_up = (grad_hidden * smooth).astype(BF16)
    grad_parts = jnp.concatenate([grad_gate, grad_up], axis=1)
    pair_out[...] = grad_parts
    entry = product(grad_parts, both[...], 1, 1).astype(BF16).astype(F32)
    if has_before:
        routed = routed + routed_in[...]
        entry = entry + entry_in[...]
    if split:

        @pl.when(first)
        def _():
            routed_odd[0] = routed.astype(BF16)
            entry_odd[0] = entry.astype(BF16)

        @pl.when(jnp.logical_not(first))
        def _():
            routed_even[0] = routed.astype(BF16)
            entry_even[0] = entry.astype(BF16)
    else:
        routed_out[...] = routed
        entry_out[...] = entry


def expert_pass(tokens, grads, gates, weights, part_rows, before, split, waits=()):
    even_n, odd_n = tokens
    even_c, odd_c = grads
    count, rows, width = even_n.shape
    hidden_width = weights.shape[3]
    tiles = 2 * count
    total = tiles * rows
    odd = pl.BlockSpec((1, rows, width), lambda t: (jnp.minimum(t, count - 1), 0, 0))
    even = pl.BlockSpec((1, rows, width), lambda t: (jnp.maximum(t - count, 0), 0, 0))
    tile = lambda size: pl.BlockSpec((rows, size), lambda t: (t, 0))
    in_specs = [odd, even, odd, even, tile(1), pl.BlockSpec(memory_space=pl.ANY)]
    operands = [odd_n, even_n, odd_c, even_c, gates, weights, *waits]
    in_specs += [pl.BlockSpec(memory_space=pl.ANY)] * len(waits)
    if before is not None:
        in_specs += [tile(width), tile(width)]
        operands += list(before)
    if split:
        out_specs = [odd, even, odd, even]
        out_shape = [jax.ShapeDtypeStruct((count, rows, width), BF16)] * 4
    else:
        out_specs = [tile(width), tile(width)]
        out_shape = [jax.ShapeDtypeStruct((total, width), F32)] * 2
    out_specs += [tile(1), tile(hidden_width), tile(2 * hidden_width)]
    out_shape += [
        jax.ShapeDtypeStruct((total, 1), F32),
        jax.ShapeDtypeStruct((total, hidden_width), BF16),
        jax.ShapeDtypeStruct((total, 2 * hidden_width), BF16),
    ]
    return pl.pallas_call(
        functools.partial(expert_kernel, before is not None, split, part_rows, len(waits)),
        grid=(tiles,),
        in_specs=in_specs,
        out_specs=out_specs,
        out_shape=out_shape,
        scratch_shapes=[
            pltpu.VMEM((width, 2 * hidden_width), BF16),
            pltpu.VMEM((width, hidden_width), BF16),
            pltpu.SemaphoreType.DMA((weights.shape[0], 3)),
        ],
        compiler_params=kernel_params(1),
        cost_estimate=LIGHT,
        name="expert_pass",
    )(*operands)


def shared_kernel(place_ref, tokens_ref, incoming_ref, weights, result_out, entry_out, *targets):
    tokens, incoming = tokens_ref[...], incoming_ref[...]
    core = place_ref[0]
    gate_part = product(tokens, weights[0], 1, 0)
    up_part = product(tokens, weights[1], 1, 0)
    sigma = 1.0 / (1.0 + jnp.exp(-gate_part))
    smooth = gate_part * sigma
    hidden = (smooth * up_part).astype(BF16)
    result_out[...] = product(hidden, weights[2], 1, 1)
    grad_hidden = product(incoming, weights[2], 1, 0)
    grad_gate = (grad_hidden * up_part * sigma * (1.0 + gate_part * (1.0 - sigma))).astype(BF16)
    grad_up = (grad_hidden * smooth).astype(BF16)
    entry_out[...] = product(grad_gate, weights[0], 1, 1) + product(grad_up, weights[1], 1, 1)
    store_split(product(tokens, grad_gate, 0, 0), core, 0, targets)
    store_split(product(tokens, grad_up, 0, 0), core, 1, targets)
    store_split(product(incoming, hidden, 0, 0), core, 2, targets)


def shared_pass(tokens, incoming, weights, dense_rows):
    rows, width = tokens.shape
    hidden_width = weights.shape[2]
    shapes = split_shapes(3, width, hidden_width, dense_rows)
    out_shape = [jax.ShapeDtypeStruct((rows, width), F32)] * 2
    out_shape += [jax.ShapeDtypeStruct(shape, BF16) for shape in shapes]
    return pl.pallas_call(
        shared_kernel,
        grid_spec=pltpu.PrefetchScalarGridSpec(
            num_scalar_prefetch=1,
            grid=(1,),
            in_specs=[whole(tokens), whole(incoming), whole(weights)],
            out_specs=[whole(shape) for shape in out_shape],
        ),
        out_shape=out_shape,
        compiler_params=kernel_params(1),
        cost_estimate=LIGHT,
        name="shared_pass",
    )(lax.axis_index("expert")[None] % 2, tokens, incoming, weights)


def expert_grad_kernel(odd_n, even_n, odd_c, even_c, gates, hidden, pair, *refs):
    out = refs[-1]
    count, rows, span = odd_n.shape
    half = count * rows
    hidden_width = hidden.shape[1]
    tokens = jnp.concatenate(
        [odd_n[...].reshape(half, span), even_n[...].reshape(half, span)], axis=0
    )
    incoming = jnp.concatenate(
        [odd_c[...].reshape(half, span), even_c[...].reshape(half, span)], axis=0
    )
    grad_pair = (gates[...] * incoming.astype(F32)).astype(BF16)
    both = product(tokens, pair[...], 0, 0)
    out[0] = both[:, :hidden_width].astype(BF16)
    out[1] = both[:, hidden_width:].astype(BF16)
    out[2] = product(grad_pair, hidden[...], 0, 0).astype(BF16)


def expert_grad(tokens, grads, gates, hidden, pair, waits=()):
    even_n, odd_n = tokens
    even_c, odd_c = grads
    count, rows, width = even_n.shape
    hidden_width = hidden.shape[1]
    span = 256
    stack = pl.BlockSpec((count, rows, span), lambda t: (0, 0, t))
    return pl.pallas_call(
        expert_grad_kernel,
        grid=(width // span,),
        in_specs=[stack, stack, stack, stack, whole(gates), whole(hidden), whole(pair)]
        + [pl.BlockSpec(memory_space=pl.ANY)] * len(waits),
        out_specs=pl.BlockSpec((3, span, hidden_width), lambda t: (0, t, 0)),
        out_shape=jax.ShapeDtypeStruct((3, width, hidden_width), BF16),
        compiler_params=kernel_params(1),
        cost_estimate=LIGHT,
        name="expert_weight_grad",
    )(odd_n, even_n, odd_c, even_c, gates, hidden, pair, *waits)


def body(
    block_input_vectors,
    output_sensitivity,
    rotary_offsets,
    dispatched_specialist_ids,
    specialist_quotas,
    storage_holder,
    mixer_projection_matrices,
    mixer_mean_estimate,
    mixer_variance_estimate,
    common_projection_matrices,
    common_mean_estimate,
    common_variance_estimate,
    gating_projection_matrix,
    gating_mean_estimate,
    gating_variance_estimate,
    scaling_factors,
    scaling_mean_estimate,
    scaling_variance_estimate,
    dispatched_projection_matrices,
    dispatched_mean_estimate,
    dispatched_variance_estimate,
):
    token_rows = block_input_vectors.shape[1]
    width = block_input_vectors.shape[2]
    head_dim = HEAD_DIM
    heads = width // head_dim
    length = rotary_offsets.shape[1]
    specialist_total = specialist_quotas.shape[0]
    expert_local = dispatched_projection_matrices.shape[0]
    hidden_width = dispatched_projection_matrices.shape[3]
    part_rows = dispatched_projection_matrices.shape[2]
    dense_rows = mixer_projection_matrices.shape[1]
    groups = lax.axis_size("expert")
    deep = lax.axis_size("dp")
    here = lax.axis_index("expert")
    level = lax.axis_index("dp")
    scale_attn = head_dim ** (-0.5)
    straight = deep == 4

    attn_own = mixer_projection_matrices.astype(BF16)
    shared_own = common_projection_matrices.astype(BF16)
    router_own = gating_projection_matrix.astype(BF16)
    gain_own = scaling_factors.astype(BF16)
    expert_own = dispatched_projection_matrices.astype(BF16)

    everyone = deep * groups
    small = jnp.concatenate([router_own.reshape(-1), gain_own.reshape(-1)])
    small_size = small.shape[0]
    small_rows = -(-small_size // 1024) * 8
    small = jnp.pad(small, (0, small_rows * 128 - small_size)).reshape(small_rows, 128)
    small_all = lax.all_to_all(
        jnp.broadcast_to(small, (everyone, small_rows, 128)),
        ("dp", "expert"),
        0,
        0,
        tiled=True,
    ).reshape(everyone, small_rows * 128)
    router_size = dense_rows * specialist_total
    router_low = small_all[:, :router_size].reshape(width, specialist_total)
    gain_low = (
        small_all[:, router_size : router_size + 2 * dense_rows]
        .reshape(everyone, 2, dense_rows)
        .transpose(1, 0, 2)
        .reshape(2, width)
    )
    inputs_low = block_input_vectors[0]
    grad_low = output_sensitivity[0]
    grad_out = grad_low.astype(F32)
    attn_column = lax.all_gather(attn_own, "dp")
    projection_fan = fan(attn_column[:, :3])
    shared_size = shared_own.size
    shared_rows = -(-shared_size // (8 * width)) * 8
    shared_flat = jnp.pad(shared_own.reshape(-1), (0, shared_rows * width - shared_size))
    column = lax.all_gather(
        after(
            jnp.concatenate([inputs_low, shared_flat.reshape(shared_rows, width)], 0), attn_column
        ),
        "dp",
    )
    column, *projection_fan = lax.optimization_barrier((column, *projection_fan))
    sequence = column[:, :token_rows].reshape(length, width)
    shared_column = column[:, token_rows:].reshape(deep, -1)[:, :shared_size].reshape(
        deep, 3, dense_rows, hidden_width
    )
    expert_parts = [lax.all_gather(after(expert_own[0], sequence), "dp")]
    projection_even = jnp.stack(projection_fan)
    projection_odd = swap(projection_even, 1)
    out_even, out_odd = gather_swaps(attn_column[:, 3:], sequence)
    for number in range(1, expert_local):
        expert_parts.append(
            lax.all_gather(after(expert_own[number], projection_odd), "dp")
        )
    projections = assemble(projection_even, projection_odd)
    out_low = assemble(out_even, out_odd)[0]
    grads_fan = fan(hold([grad_low], projections)[0])
    gain_one = gain_low[0].astype(F32)
    gain_two = gain_low[1].astype(F32)

    sequence_low, sequence = sequence, sequence.astype(F32)

    normed_all, _, _ = norm_forward(sequence, gain_one)
    inputs = inputs_low.astype(F32)
    normed, scaled_one, inverse_one = norm_forward(inputs, gain_one)
    place = level * token_rows
    cosine_all, sine_all = rotary_tables(rotary_offsets[0], head_dim)
    starts = jnp.arange(length, dtype=jnp.int32) - rotary_offsets[0]
    query, keys, values, mixed, mixed_low = attention(
        place, normed_all, projections, cosine_all, sine_all, starts, token_rows
    )
    mixed_low = hold([mixed_low], *grads_fan[1:])[0]
    grads_even = jnp.stack(grads_fan)
    grads_plane = (grads_even, swap(grads_even, 1))
    middle = inputs + contract(mixed_low, out_low, 1, 0)
    second, scaled_two, inverse_two = norm_forward(middle, gain_two)

    probs = jax.nn.softmax(contract(second, router_low, 1, 0), axis=-1)
    experts = jnp.arange(specialist_total, dtype=jnp.int32)
    named = jnp.any(dispatched_specialist_ids[0][:, :, None] == experts, axis=1)
    order = jnp.arange(token_rows)
    earlier = contract(
        (order[:, None] > order[None, :]).astype(BF16), named.astype(BF16), 1, 0
    )
    kept = named & (earlier < specialist_quotas.astype(F32)[None, :])
    gate = jnp.where(kept, probs, 0.0)
    to_storage = (storage_holder[:, None] == experts[None, :]).astype(F32)
    gate_stored = jnp.sum(gate[:, :, None] * to_storage[None], axis=1)
    gates_sent = gate_stored.reshape(token_rows, groups, expert_local).transpose(1, 0, 2)
    gates_received = lax.all_to_all(gates_sent, "expert", 0, 0, tiled=True)
    half = jnp.arange(groups // 2) * 2
    relative = here ^ jnp.concatenate([half + 1, half])
    gates_plane = gates_received[relative].reshape(groups * token_rows, expert_local)

    turned, own_turned, mixed_turned = normed_all.T, normed.T, mixed_low.T
    second_fan = fan(second)
    second_even = jnp.stack(
        list(second_fan[:1])
        + list(hold(
            second_fan[1:], shared_column, turned, own_turned, mixed_turned
        ))
    )
    tokens = (second_even, swap(second_even, 1))
    expert_parts[0] = after(expert_parts[0], tokens[1], grads_plane[1], gates_plane)

    shared_fan = fan(hold([shared_column], tokens[1], expert_parts[0])[0])

    def shared_step(shared_even, shared_odd):
        shared_low = assemble(shared_even, shared_odd)
        out, entry, *grad = shared_pass(second, grad_low, shared_low, dense_rows)
        if len(grad) == 1:
            grad = core_split(grad[0], dense_rows)
        return out, entry, chip_sums(grad[0], swap(grad[1], 1))

    def spread_after(sums, *others):
        lows = hold([part.astype(BF16) for part in sums[1:]], *others)
        return [swap(part, 2 * index + 2) for index, part in enumerate(lows)]

    mask = here ^ jnp.arange(groups)
    back = mask // 2 + jnp.where(mask % 2 == 1, 0, groups // 2)

    def return_gates(gate_grads, *others):
        sent = jnp.concatenate(gate_grads, -1).reshape(groups, token_rows, expert_local)[back]
        return lax.all_to_all(hold([sent], *others)[0], "expert", 0, 0, tiled=True)

    gate_grads = []
    expert_sums = []
    part_sums = []
    before = None
    for number in range(expert_local):
        last = number == expert_local - 1
        gate_column = gates_plane[:, number : number + 1]
        parts = expert_pass(
            tokens, grads_plane, gate_column, expert_parts[number], part_rows, before, last,
            (),
        )
        before, (gate_grad, hidden, pair) = parts[:-3], parts[-3:]
        gate_grads.append(gate_grad)
        if number == 0:
            shared_even = hold([jnp.stack(shared_fan)], hidden)[0]
            shared_odd = swap(shared_even, 1)
        if last:
            routed_odd, routed_even, entry_odd, entry_even = before
            entry_odd = hold([entry_odd], *shared_parts)[0]
            entry_other = swap(entry_odd, 1)
            entry_sums = join_cores(entry_even, entry_other)
            entry_parts = spread_chips(entry_sums)
            routed_other = swap(
                hold([routed_odd], *[part.astype(BF16) for part in entry_sums[1:]])[0], 1
            )
        expert_part = expert_grad(
            tokens,
            grads_plane,
            gate_column,
            hidden,
            pair,
            [routed_other] if last else shared_fan[1:],
        )
        if number == 0:
            shared_odd = hold([shared_odd], expert_part)[0]
            shared_out, shared_entry, shared_sums = shared_step(shared_even, shared_odd)
            shared_parts = spread_after(shared_sums, *expert_parts[1:2])
        expert_whole = expert_part
        expert_part = expert_part.reshape(3, deep, part_rows, hidden_width)
        if last:
            gate_grad_back = return_gates(gate_grads, expert_whole)
            shared_total = add_up(shared_sums[0], hold(shared_parts, expert_whole))
            extra = -(part_rows + dense_rows) % 16
            shared_total = jnp.pad(shared_total.astype(BF16), ((0, 0), (0, 0), (0, extra), (0, 0)))
            expert_part = jnp.concatenate([expert_part, shared_total], 2)
        part_sum = lax.psum_scatter(
            expert_part.reshape(3, -1, hidden_width), "dp", scatter_dimension=1, tiled=True
        )
        part_sums.append(part_sum)
        expert_sums.append(part_sum[:, :part_rows].astype(F32))
    shared_sum = part_sum[:, part_rows : part_rows + dense_rows].astype(F32)
    expert_sum = jnp.stack(expert_sums)

    entry_parts = hold(entry_parts, expert_whole)
    grad_second = add_up(entry_sums[0], entry_parts)
    routed_sums = join_cores(routed_even, routed_other)
    gate_grad_stored = gate_grad_back.transpose(1, 0, 2).reshape(token_rows, specialist_total)
    grad_prob = jnp.sum(gate_grad_stored[:, None, :] * to_storage[None], axis=-1)
    grad_prob = jnp.where(kept, grad_prob, 0.0)


    grad_logit = (probs * (grad_prob - jnp.sum(probs * grad_prob, axis=-1, keepdims=True))).astype(
        BF16
    )
    router_grad = contract(second, grad_logit, 0, 0)
    grad_second = grad_second + contract(grad_logit, router_low, 1, 1) + shared_entry
    gain_two_grad = jnp.sum(grad_second * scaled_two, axis=0)
    grad_middle = norm_backward(grad_second, scaled_two, inverse_two, gain_two) + grad_out
    grad_attn_out = grad_middle.astype(BF16)

    def grad_part(first, count, waits=()):
        *grads, dq, dk, dv = attention_grad(
            place,
            turned,
            own_turned,
            mixed_turned,
            out_low,
            query,
            keys,
            values,
            mixed,
            grad_attn_out,
            cosine_all,
            sine_all,
            starts,
            dense_rows,
            first,
            count,
            waits,
        )
        if len(grads) == 1:
            grads = core_split(grads[0], dense_rows)
        return grads[0], grads[1], (dq, dk, dv)

    pairs = width // (2 * head_dim)
    early = (pairs + 1) // 2
    first_mine, first_other, first_terms = grad_part(0, early)
    last_mine, last_other, last_terms = grad_part(
        early, pairs - early, [first_other, part_sums[0]]
    )
    first_sums = chip_sums(first_mine, swap(first_other, 1))
    first_parts = spread_chips(first_sums)
    last_received = hold([swap(last_other, 1)], first_sums[1].astype(BF16))[0]
    last_sums = chip_sums(last_mine, last_received)
    last_parts = spread_after(last_sums, *first_parts)
    normed_low, grad_normed, gain_one_grad = normed_grad(
        sequence_low,
        projections,
        (first_terms, last_terms),
        token_rows,
        [first_sums[1].astype(BF16)],
    )
    gain_one_grad = gain_one_grad[0]
    small_grad = jnp.concatenate(
        [
            router_grad.reshape(everyone, router_size),
            jnp.stack([gain_one_grad, gain_two_grad])
            .reshape(2, everyone, dense_rows)
            .transpose(1, 0, 2)
            .reshape(everyone, 2 * dense_rows),
        ],
        -1,
    )
    small_grad = jnp.pad(small_grad, ((0, 0), (0, small_rows * 128 - small_size)))
    small_received = lax.all_to_all(
        small_grad.reshape(everyone, small_rows, 128), ("dp", "expert"), 0, 0, tiled=True
    )
    small_sum = jnp.sum(hold([small_received], *last_parts)[0], axis=0).reshape(-1)
    first_total = add_up(first_sums[0], hold(first_parts, grad_normed))
    last_total = add_up(last_sums[0], last_parts)
    first_sum, first_column = column_sum(
        first_total, 1, None, last_total.astype(BF16)
    )
    expert_squares = sum(jnp.sum(part * part) for part in expert_sums)
    last_sum, _ = column_sum(last_total, 1, None, jnp.broadcast_to(expert_squares, (8, 128)))
    routed_parts = spread_after(routed_sums, *first_column)
    grad_normed = grad_normed - pick(normed_low, level, 0).astype(F32)
    arrived = lax.psum_scatter(
        hold([normed_low.reshape(length, width)], part_sums[-1])[0],
        "dp",
        scatter_dimension=0,
        tiled=True,
    )
    grad_normed = grad_normed + arrived.astype(F32)
    grad_inputs = norm_backward(grad_normed, scaled_one, inverse_one, gain_one) + grad_middle
    attn_sum = jnp.concatenate([first_sum, last_sum], -1)
    router_sum = small_sum[:router_size].reshape(dense_rows, specialist_total)
    gain_sum = small_sum[router_size:small_size].reshape(2, dense_rows)

    local_squares = (
        jnp.sum(attn_sum * attn_sum)
        + jnp.sum(shared_sum * shared_sum)
        + jnp.sum(router_sum * router_sum)
        + jnp.sum(gain_sum * gain_sum)
        + expert_squares
    )
    spread = jnp.broadcast_to(local_squares, (everyone, 8, 128))
    squares = lax.all_to_all(spread, ("dp", "expert"), 0, 0, tiled=True)
    grad_norm = jnp.sqrt(jnp.sum(squares[:, 0, 0]))
    routed = add_up(routed_sums[0], hold(routed_parts, squares))
    block_out = (middle + shared_out + routed).astype(BF16)
    scale = jnp.minimum(1.0, CLIP_VALUE / (grad_norm + 1e-06))
    attn_new, attn_moment, attn_square = adam(
        mixer_projection_matrices,
        mixer_mean_estimate,
        mixer_variance_estimate,
        attn_sum,
        scale,
        RATE_MATRIX,
    )
    shared_new, shared_moment, shared_square = adam(
        common_projection_matrices,
        common_mean_estimate,
        common_variance_estimate,
        shared_sum,
        scale,
        RATE_MATRIX,
    )
    router_new, router_moment, router_square = adam(
        gating_projection_matrix,
        gating_mean_estimate,
        gating_variance_estimate,
        router_sum,
        scale,
        RATE_MATRIX,
    )
    gain_new, gain_moment, gain_square = adam(
        scaling_factors,
        scaling_mean_estimate,
        scaling_variance_estimate,
        gain_sum,
        scale,
        RATE_GAIN,
    )
    expert_new, expert_moment, expert_square = adam(
        dispatched_projection_matrices,
        dispatched_mean_estimate,
        dispatched_variance_estimate,
        expert_sum,
        scale,
        RATE_EXPERT,
    )
    return (
        block_out[None],
        grad_inputs[None],
        grad_norm,
        attn_new,
        attn_moment,
        attn_square,
        attn_new.astype(BF16),
        shared_new,
        shared_moment,
        shared_square,
        shared_new.astype(BF16),
        router_new,
        router_moment,
        router_square,
        router_new.astype(BF16),
        gain_new,
        gain_moment,
        gain_square,
        expert_new,
        expert_moment,
        expert_square,
        expert_new.astype(BF16),
    )


def solution(mesh):
    placed = (
        P("expert", "dp", None),
        P("expert", "dp", None),
        P("expert", None),
        P("expert", "dp", None),
        P(),
        P(),
        P(None, ("dp", "expert"), None),
        P(None, ("dp", "expert"), None),
        P(None, ("dp", "expert"), None),
        P(None, ("dp", "expert"), None),
        P(None, ("dp", "expert"), None),
        P(None, ("dp", "expert"), None),
        P(("dp", "expert"), None),
        P(("dp", "expert"), None),
        P(("dp", "expert"), None),
        P(None, ("dp", "expert")),
        P(None, ("dp", "expert")),
        P(None, ("dp", "expert")),
        P("expert", None, "dp", None),
        P("expert", None, "dp", None),
        P("expert", None, "dp", None),
    )
    return jax.shard_map(
        body,
        mesh=mesh,
        in_specs=placed,
        out_specs=(
            P("expert", "dp", None),
            P("expert", "dp", None),
            P(),
            P(None, ("dp", "expert"), None),
            P(None, ("dp", "expert"), None),
            P(None, ("dp", "expert"), None),
            P(None, ("dp", "expert"), None),
            P(None, ("dp", "expert"), None),
            P(None, ("dp", "expert"), None),
            P(None, ("dp", "expert"), None),
            P(None, ("dp", "expert"), None),
            P(("dp", "expert"), None),
            P(("dp", "expert"), None),
            P(("dp", "expert"), None),
            P(("dp", "expert"), None),
            P(None, ("dp", "expert")),
            P(None, ("dp", "expert")),
            P(None, ("dp", "expert")),
            P("expert", None, "dp", None),
            P("expert", None, "dp", None),
            P("expert", None, "dp", None),
            P("expert", None, "dp", None),
        ),
        check_vma=False,
    )
```
